32 devices in a mesh: dp: 2 (over core), wide: 16 (over z, y, x).
Axes of the slice: x: 2, y: 2, z: 4, core: 2. Of those that a mesh axis runs over, the one named last changes fastest.
Arguments:
- tower_states: bfloat16 [2, 6304, 768], P('dp', 'wide'), may hold values from -6 to 6
- caption_lengths: int32 [2, 8, 2], P('dp'), may hold values from 1 to 314, 394 in all within a row
- assignment: int32 [2, 8, 2], P('dp'), may hold values from 0 to 1, each once within a row
- cls_token: bfloat16 [768], replicated, may hold values from -6 to 6
- w_img: bfloat16 [768, 768], replicated, may hold values from -0.21875 to 0.21875
- b_img: bfloat16 [768], replicated, may hold values from -2 to 2
- w_txt: bfloat16 [768, 768], replicated, may hold values from -0.21875 to 0.21875
- b_txt: bfloat16 [768], replicated, may hold values from -2 to 2
- gain_one: bfloat16 [768], replicated, may hold values from 0.5 to 1.5
- bias_one: bfloat16 [768], replicated, may hold values from -2 to 2
- w_qkv: bfloat16 [768, 2304], replicated, may hold values from -0.21875 to 0.21875
- b_query: bfloat16 [768], replicated, may hold values from -2 to 2
- b_value: bfloat16 [768], replicated, may hold values from -2 to 2
- w_out: bfloat16 [768, 768], replicated, may hold values from -1.75 to 1.75
- b_out: bfloat16 [768], replicated, may hold values from -2 to 2
- gain_two: bfloat16 [768], replicated, may hold values from 0.5 to 1.5
- bias_two: bfloat16 [768], replicated, may hold values from -2 to 2
- w_up: bfloat16 [768, 3072], replicated, may hold values from -0.21875 to 0.21875
- b_up: bfloat16 [3072], replicated, may hold values from -2 to 2
- w_down: bfloat16 [3072, 768], replicated, may hold values from -0.109375 to 0.109375
- b_down: bfloat16 [768], replicated, may hold values from -2 to 2
- cotangent: bfloat16 [2, 8192, 768], P('dp', 'wide'), may hold values from -6 to 6
Outputs:
- layer_out: bfloat16 [2, 8192, 768], P('dp', 'wide')
- d_tower: bfloat16 [2, 6304, 768], P('dp', 'wide')
- d_cls: float32 [768], P('wide')
- d_w_img: float32 [768, 768], P('wide')
- d_b_img: float32 [768], P('wide')
- d_w_txt: float32 [768, 768], P('wide')
- d_b_txt: float32 [768], P('wide')
- d_gain_one: float32 [768], P('wide')
- d_bias_one: float32 [768], P('wide')
- d_w_qkv: float32 [768, 2304], P('wide')
- d_b_query: float32 [768], P('wide')
- d_b_value: float32 [768], P('wide')
- d_w_out: float32 [768, 768], P('wide')
- d_b_out: float32 [768], P('wide')
- d_gain_two: float32 [768], P('wide')
- d_bias_two: float32 [768], P('wide')
- d_w_up: float32 [768, 3072], P('wide')
- d_b_up: float32 [3072], P('wide')
- d_w_down: float32 [3072, 768], P('wide')
- d_b_down: float32 [768], P('wide')
The draws below stay inside these ranges and needn't reach their ends.
Inputs may be any that keep to these rules, and one draw needn't show every extreme that they name: `caption_lengths`: the two captions of a pair fill the 394 caption rows of that pair exactly: their lengths sum to 394, and each has at most 314 rows. `assignment`: each row is 0 and 1 in some order.
All inputs are finite; a program needn't handle non-finite values.
Results may differ from the reference program's by a relative error of at most 0.015.
Values may be sent and summed in bfloat16 or wider, within the bound.
No kernel may reach another device: no remote copies, remote signals or barrier semaphores. Data moves between devices by JAX's collectives and lax.ppermute only.
A program may use at most 192 MiB of HBM per device.

```python
import math
import jax
import jax.numpy as jnp
import numpy as np
from jax import lax

D = 768
HEAD = 64
FF = 3072
PATCHES = 197
BLOCK = 512
PAIRS_DEV = 1
MAXCAP = 314
HALF = 8
TOWER_ROWS = 6304
BLOCK_ROWS = 8192
N_DP = 2
N_WIDE = 16


def shard_levels(own_key, dims, pieces, least, top_value):
    factor_of, own = 1.0, jax.random.fold_in(own_key, 6)
    for position, shards_of in pieces:
        steps = jnp.exp(jax.random.uniform(jax.random.fold_in(own, position), (shards_of,), jnp.float32, least / len(pieces), top_value / len(pieces)))
        factor_of = factor_of * jnp.repeat(steps, dims[position] // shards_of).reshape([-1 if axis == position else 1 for axis in range(len(dims))])
    return factor_of


def split_up(count, total, bound, slope):
    portions = [(1 << 20) // math.isqrt(grade ** slope) + 1 for grade in range(2, count + 1)]
    surplus, holding = total - bound - (count - 1), [1] * (count - 1)
    while surplus > 0:
        free = [i for i in range(count - 1) if holding[i] < bound]
        whole, remaining = sum([portions[i] for i in free]), surplus
        for i in free:
            extra = min(bound - holding[i], max(1, remaining * portions[i] // whole), surplus)
            holding[i] = holding[i] + extra
            surplus = surplus - extra
    return np.array([bound] + holding)


def ragged(key, count, total, most, slope):
    if count == 2:
        one = jax.random.randint(key, (), max(1, total - most), min(most, total - 1) + 1)
        return jnp.stack([one, total - one])
    lengths = jnp.asarray(split_up(count, total, most, slope), jnp.int32)
    pairs = (count - 1) // 2
    giver, receiver = lengths[1:1 + 2 * pairs:2], lengths[2:2 + 2 * pairs:2]
    room = jnp.minimum(giver - 1, most - receiver)
    passed = jax.random.randint(jax.random.fold_in(key, 1), (pairs,), 0, 1 << 20) % (room + 1)
    lengths = lengths.at[1:1 + 2 * pairs:2].set(giver - passed).at[2:2 + 2 * pairs:2].set(receiver + passed)
    return lengths[jax.random.permutation(jax.random.fold_in(key, 2), count)]


def bell_draw(own_key, extent, deviation, most, split=(), held_as=jnp.bfloat16):
    level = shard_levels(own_key, extent, split, -0.22, 0.18) if split else 1.0
    drawn = jax.random.normal(own_key, extent, jnp.float32) * deviation * level
    return jnp.minimum(jnp.maximum(drawn, -most), most).astype(held_as)


def setup_inputs(seed: int = 0) -> dict:
    key_of = jax.random.split(jax.random.key(seed), 23)
    return {
        "tower_states": bell_draw(key_of[0], (N_DP, TOWER_ROWS, D), 1.0, 6.0, ((0, 2), (1, 16))),
        "caption_lengths": jax.vmap(lambda own: ragged(own, 2, 2 * PATCHES, MAXCAP, 0))(jax.random.split(key_of[1], N_DP * HALF)).reshape((N_DP, HALF, 2)).astype(jnp.int32),
        "assignment": jax.vmap(lambda own: jax.random.permutation(own, 2))(jax.random.split(key_of[2], N_DP * HALF)).reshape((N_DP, HALF, 2)).astype(jnp.int32),
        "cls_token": bell_draw(key_of[3], (D,), 1.0, 6.0),
        "w_img": bell_draw(key_of[4], (D, D), D ** -0.5, 0.21875),
        "b_img": bell_draw(key_of[5], (D,), 0.3, 2.0),
        "w_txt": bell_draw(key_of[6], (D, D), D ** -0.5, 0.21875),
        "b_txt": bell_draw(key_of[7], (D,), 0.3, 2.0),
        "gain_one": jnp.clip(1.0 + 0.1 * jax.random.normal(key_of[8], (D,), jnp.float32), 0.5, 1.5).astype(jnp.bfloat16),
        "bias_one": bell_draw(key_of[9], (D,), 0.3, 2.0),
        "w_qkv": bell_draw(key_of[10], (D, 3 * D), D ** -0.5, 0.21875),
        "b_query": bell_draw(key_of[11], (D,), 0.3, 2.0),
        "b_value": bell_draw(key_of[12], (D,), 0.3, 2.0),
        "w_out": bell_draw(key_of[13], (D, D), (D // 64) ** -0.5, 1.75),
        "b_out": bell_draw(key_of[14], (D,), 0.3, 2.0),
        "gain_two": jnp.clip(1.0 + 0.1 * jax.random.normal(key_of[15], (D,), jnp.float32), 0.5, 1.5).astype(jnp.bfloat16),
        "bias_two": bell_draw(key_of[16], (D,), 0.3, 2.0),
        "w_up": bell_draw(key_of[17], (D, FF), D ** -0.5, 0.21875),
        "b_up": bell_draw(key_of[18], (FF,), 0.3, 2.0),
        "w_down": bell_draw(key_of[19], (FF, D), FF ** -0.5, 0.109375),
        "b_down": bell_draw(key_of[20], (D,), 0.3, 2.0),
        "cotangent": bell_draw(key_of[21], (N_DP, BLOCK_ROWS, D), 1.0, 6.0, ((0, 2), (1, 16))),
    }


@jax.custom_vjp
def low(v):
    return lax.optimization_barrier(v.astype(jnp.bfloat16)).astype(jnp.float32)

@jax.custom_vjp
def low_back(v):
    return v

def low_keep(v):
    return (low(v), None)

def low_pass(kept, grad):
    return (grad,)

def back_keep(v):
    return (v, None)

def back_low(kept, grad):
    return (low(grad),)
low.defvjp(low_keep, low_pass)
low_back.defvjp(back_keep, back_low)

def matmul(left, right):
    return jnp.einsum('...i,ij->...j', left, right, precision=lax.Precision.HIGHEST)

def layer_norm(rows, gain, shift):
    mean = lax.optimization_barrier(jnp.mean(rows, axis=-1, keepdims=True))
    centred = rows - mean
    factor = lax.rsqrt(lax.optimization_barrier(jnp.mean(centred * centred, axis=-1, keepdims=True)) + 1e-05)
    return centred * factor * gain + shift

def layer(params, block, count):
    gain_one, bias_one, w_qkv, b_query, b_value, w_out, b_out, gain_two, bias_two, w_up, b_up, w_down, b_down = params
    rows, width = block.shape
    heads = width // HEAD
    live = jnp.arange(rows) < count
    first = low(layer_norm(block, gain_one, bias_one))
    packed = matmul(first, w_qkv)
    query = low(low_back(packed[:, :width] + b_query)).reshape(rows, heads, HEAD)
    keys = low(low_back(packed[:, width:2 * width])).reshape(rows, heads, HEAD)
    values = low(low_back(packed[:, 2 * width:] + b_value)).reshape(rows, heads, HEAD)
    scores = low_back(jnp.einsum('qhd,khd->hqk', query, keys, precision=lax.Precision.HIGHEST) * 0.125)
    scores = jnp.where(live[None, None, :], scores, -1000000000.0)
    probs = low(jax.nn.softmax(scores, axis=-1))
    joined = jnp.einsum('hqk,khd->qhd', probs, values, precision=lax.Precision.HIGHEST).reshape(rows, width)
    joined = low_back(low(joined))
    middle = block + low_back(matmul(joined, w_out) + b_out)
    second = low(layer_norm(middle, gain_two, bias_two))
    inner = low_back(matmul(second, w_up) + b_up)
    active = low(jax.nn.gelu(inner, approximate=False))
    result = middle + matmul(active, w_down) + b_down
    return jnp.where(live[:, None], result, 0.0)

def assemble(image_rows, text_rows, lens, order, cls_row):
    extended = jnp.concatenate([text_rows, jnp.zeros((MAXCAP, text_rows.shape[1]), jnp.float32)], 0)

    def one(item):
        image = lax.dynamic_slice_in_dim(image_rows, (item * PATCHES).astype(jnp.int32), PATCHES, 0)
        start = jnp.where(item == 0, 0, lens[0]).astype(jnp.int32)
        text = lax.dynamic_slice_in_dim(extended, start, MAXCAP, 0)
        length = jnp.where(item == 0, lens[0], lens[1])
        keep = jnp.arange(MAXCAP) < length
        text = jnp.where(keep[:, None], text, 0.0)
        return (jnp.concatenate([cls_row[None, :], image, text], 0), 1 + PATCHES + length)
    first, first_count = one(order[0])
    second, second_count = one(order[1])
    return (jnp.stack([first, second]), jnp.stack([first_count, second_count]))

def reference(tower_states, caption_lengths, assignment, cls_token, w_img, b_img, w_txt, b_txt, gain_one, bias_one, w_qkv, b_query, b_value, w_out, b_out, gain_two, bias_two, w_up, b_up, w_down, b_down, cotangent):
    params = tuple((v.astype(jnp.float32) for v in (cls_token, w_img, b_img, w_txt, b_txt, gain_one, bias_one, w_qkv, b_query, b_value, w_out, b_out, gain_two, bias_two, w_up, b_up, w_down, b_down)))
    states = tower_states.astype(jnp.float32)
    half = N_WIDE // 2
    lens_all = caption_lengths.reshape(N_DP, half, PAIRS_DEV, 2)
    order_all = assignment.reshape(N_DP, half, PAIRS_DEV, 2)

    def forward(states, params):
        cls_row, wi, bi, wt, bt = params[:5]
        layer_params = params[5:]
        shaped = states.reshape(N_DP, N_WIDE, PAIRS_DEV, 2 * PATCHES, D)
        image = low(low_back(matmul(shaped[:, :half], wi) + bi))
        text = low(low_back(matmul(shaped[:, half:], wt) + bt))
        inner_build = jax.vmap(assemble, in_axes=(0, 0, 0, 0, None))
        middle_build = jax.vmap(inner_build, in_axes=(0, 0, 0, 0, None))
        build = jax.vmap(middle_build, in_axes=(0, 0, 0, 0, None))
        blocks, counts = build(image, text, lens_all, order_all, cls_row)
        blocks = jnp.moveaxis(blocks, 3, 1).reshape(N_DP * N_WIDE * PAIRS_DEV, BLOCK, D)
        counts = jnp.moveaxis(counts, 3, 1).reshape(N_DP * N_WIDE * PAIRS_DEV)
        step = jax.checkpoint(layer)
        outs = lax.map(lambda pair: step(layer_params, pair[0], pair[1]), (blocks, counts))
        return outs.reshape(N_DP, N_WIDE * PAIRS_DEV * BLOCK, D)
    result, pull = jax.vjp(forward, states, params)
    d_states, d_params = pull(cotangent.astype(jnp.float32))
    return (result.astype(jnp.bfloat16), d_states.astype(jnp.bfloat16)) + tuple(d_params)
```

```python
from functools import partial

import jax
import jax.numpy as jnp
from jax import lax
from jax.sharding import PartitionSpec as P

HEAD = 64
PATCHES = 197
BLOCK = 512


def inner_rows(left, right):
    return lax.dot_general(
        left, right, (((0,), (0,)), ((), ())), preferred_element_type=jnp.float32
    )


def by_rows(left, weight):
    return lax.dot_general(
        left, weight, (((1,), (1,)), ((), ())), preferred_element_type=jnp.float32
    )


def layer_norm(rows, gain, shift):
    mean = jnp.mean(rows, axis=-1, keepdims=True)
    centred = rows - mean
    factor = lax.rsqrt(jnp.mean(centred * centred, axis=-1, keepdims=True) + 1e-05)
    normed = centred * factor
    return (normed * gain + shift, normed, factor)


def norm_back(upstream, gain, normed, factor):
    scaled = upstream * gain
    return factor * (
        scaled
        - jnp.mean(scaled, axis=-1, keepdims=True)
        - normed * jnp.mean(scaled * normed, axis=-1, keepdims=True)
    )


def block_pass(block, live, upstream, weights):
    (
        gain_one,
        bias_one,
        w_qkv,
        b_query,
        b_value,
        w_out,
        b_out,
        gain_two,
        bias_two,
        w_up,
        b_up,
        w_down,
        b_down,
    ) = weights
    bf16 = jnp.bfloat16
    f32 = jnp.float32
    rows, width = block.shape
    heads = width // HEAD
    first, normed_one, factor_one = layer_norm(block, gain_one, bias_one)
    first_low = first.astype(bf16)
    packed = jnp.dot(first_low, w_qkv, preferred_element_type=f32)
    query = (packed[:, :width] + b_query).astype(bf16).reshape(rows, heads, HEAD)
    keys = packed[:, width : 2 * width].astype(bf16).reshape(rows, heads, HEAD)
    values = (packed[:, 2 * width :] + b_value).astype(bf16).reshape(rows, heads, HEAD)
    scores = jnp.einsum("qhd,khd->hqk", query, keys, preferred_element_type=f32) * 0.125
    scores = jnp.where(live[None, None, :], scores, -1000000000.0)
    top = jnp.max(scores, axis=-1, keepdims=True)
    expo = jnp.exp(scores - top)
    probs = expo / jnp.sum(expo, axis=-1, keepdims=True)
    probs_low = probs.astype(bf16)
    joined = jnp.einsum("hqk,khd->qhd", probs_low, values, preferred_element_type=f32)
    joined_low = joined.reshape(rows, width).astype(bf16)
    middle = block + jnp.dot(joined_low, w_out, preferred_element_type=f32) + b_out
    second, normed_two, factor_two = layer_norm(middle, gain_two, bias_two)
    second_low = second.astype(bf16)
    inner = jnp.dot(second_low, w_up, preferred_element_type=f32) + b_up
    active, active_back = jax.vjp(partial(jax.nn.gelu, approximate=False), inner)
    active_low = active.astype(bf16)
    result = middle + jnp.dot(active_low, w_down, preferred_element_type=f32) + b_down
    result = jnp.where(live[:, None], result, 0.0)
    grad_out = jnp.where(live[:, None], upstream, 0.0)
    grad_low = grad_out.astype(bf16)
    d_w_down = inner_rows(active_low, grad_low)
    d_b_down = jnp.sum(grad_out, axis=0)
    d_active = by_rows(grad_low, w_down)
    d_inner = active_back(d_active)[0].astype(bf16)
    d_w_up = inner_rows(second_low, d_inner)
    d_b_up = jnp.sum(d_inner.astype(f32), axis=0)
    d_second = by_rows(d_inner, w_up)
    d_gain_two = jnp.sum(d_second * normed_two, axis=0)
    d_bias_two = jnp.sum(d_second, axis=0)
    d_middle = grad_out + norm_back(d_second, gain_two, normed_two, factor_two)
    d_attn = d_middle.astype(bf16)
    d_w_out = inner_rows(joined_low, d_attn)
    d_b_out = jnp.sum(d_attn.astype(f32), axis=0)
    d_joined = by_rows(d_attn, w_out).astype(bf16).reshape(rows, heads, HEAD)
    d_probs = jnp.einsum("qhd,khd->hqk", d_joined, values, preferred_element_type=f32)
    d_values = jnp.einsum("hqk,qhd->khd", probs_low, d_joined, preferred_element_type=f32)
    d_scores = probs * (d_probs - jnp.sum(d_probs * probs, axis=-1, keepdims=True))
    d_scores_low = d_scores.astype(bf16)
    d_query = jnp.einsum("hqk,khd->qhd", d_scores_low, keys, preferred_element_type=f32) * 0.125
    d_keys = jnp.einsum("hqk,qhd->khd", d_scores_low, query, preferred_element_type=f32) * 0.125
    d_packed = jnp.concatenate(
        [d_query.reshape(rows, width), d_keys.reshape(rows, width), d_values.reshape(rows, width)],
        axis=1,
    ).astype(bf16)
    d_w_qkv = inner_rows(first_low, d_packed)
    d_b_query = jnp.sum(d_packed[:, :width].astype(f32), axis=0)
    d_b_value = jnp.sum(d_packed[:, 2 * width :].astype(f32), axis=0)
    d_first = by_rows(d_packed, w_qkv)
    d_gain_one = jnp.sum(d_first * normed_one, axis=0)
    d_bias_one = jnp.sum(d_first, axis=0)
    d_block = d_middle + norm_back(d_first, gain_one, normed_one, factor_one)
    grads = (
        d_gain_one,
        d_bias_one,
        d_w_qkv,
        d_b_query,
        d_b_value,
        d_w_out,
        d_b_out,
        d_gain_two,
        d_bias_two,
        d_w_up,
        d_b_up,
        d_w_down,
        d_b_down,
    )
    return (result, d_block, grads)


def swap(x, axis, bit):
    count = lax.axis_size(axis)
    route = [(i, i ^ (1 << bit)) for i in range(count)]
    return lax.ppermute(x, axis, route)


def add_low(one, two):
    f32 = jnp.float32
    return (one.astype(f32) + two.astype(f32)).astype(jnp.bfloat16)


def over_cores(part):
    half = part.shape[1] // 2
    core = lax.axis_index("dp")
    left, right = part[:, :half], part[:, half:]
    theirs = jnp.where(core == 0, right, left)
    own = jnp.where(core == 0, left, right)
    return add_low(own, swap(theirs, "dp", 0))


def halving(part, order):
    wide = lax.axis_size("wide")
    place = lax.axis_index("wide")
    bits = wide.bit_length() - 1
    rows, cols = part.shape
    part = part.reshape([2] * bits + [rows // wide, cols])
    for bit in order:
        axis = bits - 1 - bit
        mine = (place >> bit) & 1
        keep = lax.dynamic_index_in_dim(part, mine, axis, keepdims=True)
        send = lax.dynamic_index_in_dim(part, 1 - mine, axis, keepdims=True)
        part = add_low(keep, swap(send, "wide", bit))
    return part.reshape(rows // wide, cols)


def both_halves(share):
    core = lax.axis_index("dp")
    other = swap(share, "dp", 0)
    first = jnp.where(core == 0, share, other)
    second = jnp.where(core == 0, other, share)
    return jnp.concatenate([first, second], axis=1).astype(jnp.float32)


def on_device(
    tower_states,
    caption_lengths,
    assignment,
    cls_token,
    w_img,
    b_img,
    w_txt,
    b_txt,
    gain_one,
    bias_one,
    w_qkv,
    b_query,
    b_value,
    w_out,
    b_out,
    gain_two,
    bias_two,
    w_up,
    b_up,
    w_down,
    b_down,
    cotangent,
):
    bf16 = jnp.bfloat16
    f32 = jnp.float32
    wide = lax.axis_size("wide")
    place = lax.axis_index("wide")
    upper = place >= wide // 2
    pair = place % (wide // 2)
    lens = lax.dynamic_index_in_dim(caption_lengths[0], pair, 0, keepdims=False)
    order = lax.dynamic_index_in_dim(assignment[0], pair, 0, keepdims=False)
    rows = tower_states[0]
    patches = PATCHES
    span = 2 * patches
    width = rows.shape[1]
    block_len = BLOCK
    longest = block_len - 1 - patches
    bits = wide.bit_length() - 1
    mine = jnp.where(upper, order[1], order[0])
    other = jnp.where(upper, order[0], order[1])
    low_window, high_window = rows[:longest], rows[span - longest :]
    incoming = swap(jnp.where(other == 0, low_window, high_window), "wide", bits - 1)
    shift_back = span - longest
    start = jnp.where(mine == 0, 0, lens[0])
    count_text = jnp.where(mine == 0, lens[0], lens[1])
    place_row = jnp.arange(block_len)
    image_row = place_row - 1
    text_row = place_row - 1 - patches
    image_from = jnp.where(
        upper,
        span + image_row + jnp.where(mine == 0, 0, patches - shift_back),
        image_row + mine * patches,
    )
    text_from = jnp.where(
        upper, text_row + start, span + text_row + jnp.where(mine == 0, 0, start - shift_back)
    )
    is_image = (place_row >= 1) & (place_row <= patches)
    is_text = (place_row > patches) & (text_row < count_text)
    source = jnp.where(is_image, image_from, jnp.where(is_text, text_from, 0))
    every = jnp.concatenate([rows, incoming], axis=0)
    raw = jnp.where((is_image | is_text)[:, None], every[source], 0)
    cut = 1 + patches
    proj_image = jnp.dot(raw[1:cut], w_img, preferred_element_type=f32) + b_img.astype(f32)
    proj_text = jnp.dot(raw[cut:], w_txt, preferred_element_type=f32) + b_txt.astype(f32)
    proj_text = jnp.where(is_text[cut:, None], proj_text, 0.0)
    block = jnp.concatenate(
        [cls_token[None, :], proj_image.astype(bf16), proj_text.astype(bf16)], axis=0
    ).astype(f32)
    weights = (
        gain_one.astype(f32),
        bias_one.astype(f32),
        w_qkv,
        b_query.astype(f32),
        b_value.astype(f32),
        w_out,
        b_out.astype(f32),
        gain_two.astype(f32),
        bias_two.astype(f32),
        w_up,
        b_up.astype(f32),
        w_down,
        b_down.astype(f32),
    )
    live = place_row < cut + count_text
    upstream = cotangent[0].astype(f32)
    result, d_block, grads = block_pass(block, live, upstream, weights)
    (
        d_gain_one,
        d_bias_one,
        d_w_qkv,
        d_b_query,
        d_b_value,
        d_w_out,
        d_b_out,
        d_gain_two,
        d_bias_two,
        d_w_up,
        d_b_up,
        d_w_down,
        d_b_down,
    ) = grads
    d_cls = d_block[0]
    d_image = d_block[1:cut].astype(bf16)
    d_text = jnp.where(is_text[cut:, None], d_block[cut:], 0.0).astype(bf16)
    d_w_img = inner_rows(raw[1:cut], d_image)
    d_w_txt = inner_rows(raw[cut:], d_text)
    d_b_img = jnp.sum(d_image.astype(f32), axis=0)
    d_b_txt = jnp.sum(d_text.astype(f32), axis=0)
    t_image = by_rows(d_image, w_img).astype(bf16)
    t_text = by_rows(d_text, w_txt).astype(bf16)
    zeros = jnp.zeros((longest - patches, width), bf16)
    image_window = jnp.where(
        mine == 0,
        jnp.concatenate([t_image, zeros], axis=0),
        jnp.concatenate([zeros, t_image], axis=0),
    )
    text_padded = jnp.concatenate([t_text, t_text], axis=0)
    text_window = lax.dynamic_slice_in_dim(
        text_padded, jnp.where(mine == 0, 0, longest - (start - shift_back)), longest, 0
    )
    returned = swap(jnp.where(upper, image_window, text_window), "wide", bits - 1)
    gap = jnp.zeros((shift_back, width), bf16)
    returned = jnp.where(
        other == 0,
        jnp.concatenate([returned, gap], axis=0),
        jnp.concatenate([gap, returned], axis=0),
    )
    at = jnp.arange(span)
    inside = (at >= start) & (at < start + count_text)
    text_full = jnp.concatenate([t_text, jnp.zeros((span, width), bf16)], axis=0)
    own_text = lax.dynamic_slice_in_dim(
        jnp.concatenate([jnp.zeros((span, width), bf16), text_full], axis=0), span - start, span, 0
    )
    own_image = jnp.concatenate([t_image, t_image], axis=0)
    inside_image = (at >= mine * patches) & (at < (mine + 1) * patches)
    own = jnp.where(upper, own_text, own_image)
    d_rows = jnp.where(jnp.where(upper, inside, inside_image)[:, None], own, returned)

    vectors = [
        d_cls,
        d_b_img,
        d_b_txt,
        d_gain_one,
        d_bias_one,
        d_b_query,
        d_b_value,
        d_b_out,
        d_gain_two,
        d_bias_two,
        d_b_down,
    ]
    tall = d_b_up.reshape(wide, 4, width // wide).swapaxes(1, 2).reshape(width, 4)
    small = jnp.concatenate([jnp.stack(vectors, axis=1), tall], axis=1)
    small = jnp.pad(small, ((0, 0), (0, 256 - small.shape[1])))
    small = small.astype(bf16)
    rest = jnp.concatenate([t.astype(bf16) for t in (d_w_out, d_w_img, d_w_txt)] + [small], axis=1)
    straight = list(range(bits))
    crossed = [1, 0] + straight[2:]
    down = halving(over_cores(d_w_down.astype(bf16)), straight)
    up = halving(over_cores(d_w_up.astype(bf16)), crossed)
    qkv = halving(over_cores(d_w_qkv.astype(bf16)), straight)
    rest = halving(over_cores(rest), crossed)
    down, up, qkv, rest = [both_halves(t) for t in (down, up, qkv, rest)]
    out, img, txt = [rest[:, i * width : (i + 1) * width] for i in range(3)]
    small = rest[:, 3 * width :]
    vectors = [small[:, i] for i in range(11)]
    d_b_up = small[:, 11:15].T.reshape(-1)
    (
        d_cls,
        d_b_img,
        d_b_txt,
        d_gain_one,
        d_bias_one,
        d_b_query,
        d_b_value,
        d_b_out,
        d_gain_two,
        d_bias_two,
        d_b_down,
    ) = vectors
    return (
        result.astype(bf16)[None],
        d_rows[None],
        d_cls,
        img,
        d_b_img,
        txt,
        d_b_txt,
        d_gain_one,
        d_bias_one,
        qkv,
        d_b_query,
        d_b_value,
        out,
        d_b_out,
        d_gain_two,
        d_bias_two,
        up,
        d_b_up,
        down,
        d_b_down,
    )


def solution(mesh):
    placed = (
        P("dp", "wide", None),
        P("dp", None, None),
        P("dp", None, None),
        P(),
        P(),
        P(),
        P(),
        P(),
        P(),
        P(),
        P(),
        P(),
        P(),
        P(),
        P(),
        P(),
        P(),
        P(),
        P(),
        P(),
        P(),
        P("dp", "wide", None),
    )
    return jax.shard_map(
        on_device,
        mesh=mesh,
        in_specs=placed,
        out_specs=(
            P("dp", "wide", None),
            P("dp", "wide", None),
            P("wide"),
            P("wide", None),
            P("wide"),
            P("wide", None),
            P("wide"),
            P("wide"),
            P("wide"),
            P("wide", None),
            P("wide"),
            P("wide"),
            P("wide", None),
            P("wide"),
            P("wide"),
            P("wide"),
            P("wide", None),
            P("wide"),
            P("wide", None),
            P("wide"),
        ),
        check_vma=False,
    )
```

```python
import math
import jax
import jax.numpy as jnp
from jax import lax
from jax.experimental import pallas as pl
from jax.experimental.pallas import tpu as pltpu
from jax.sharding import PartitionSpec as P

HEAD = 64
PATCHES = 197
BLOCK = 512
WINDOW = 320
bf16 = jnp.bfloat16
f32 = jnp.float32
VMEM = pl.BlockSpec(memory_space=pltpu.VMEM)
SMEM = pl.BlockSpec(memory_space=pltpu.SMEM)
NN = (((1,), (0,)), ((), ()))
NT = (((1,), (1,)), ((), ()))
TN = (((0,), (0,)), ((), ()))


def dot(left, right, dims=NN):
    return lax.dot_general(left, right, dims, preferred_element_type=f32)


def params(mib, **more):
    return pltpu.CompilerParams(vmem_limit_bytes=mib << 20, **more)


def cost(flops, size):
    return pl.CostEstimate(flops=int(flops), bytes_accessed=int(size), transcendentals=0)


def struct(shape, dtype):
    return jax.ShapeDtypeStruct(shape, dtype)


def row_ids(shape):
    return lax.broadcasted_iota(jnp.int32, shape, 0)


def norm_stats(rows):
    mean = jnp.mean(rows, axis=-1, keepdims=True)
    centred = rows - mean
    factor = lax.rsqrt(jnp.mean(centred * centred, axis=-1, keepdims=True) + 1e-05)
    return centred * factor, factor


def norm_back(scaled, normed, factor):
    return factor * (
        scaled
        - jnp.mean(scaled, axis=-1, keepdims=True)
        - normed * jnp.mean(scaled * normed, axis=-1, keepdims=True)
    )


def hidden_grad_kernel(spots, cot, w_down, grad, d_bias):
    live = row_ids((BLOCK, 1)) < spots[6]
    dy = jnp.where(live, cot[...], jnp.zeros_like(cot))
    grad[...] = dot(dy, w_down[...], NT).astype(bf16)

    @pl.when(pl.program_id(0) == 0)
    def _():
        d_bias[...] = jnp.sum(dy.astype(f32), axis=0, keepdims=True)


def hidden_grad(spots, cot, w_down):
    hidden, width = w_down.shape
    tile = 512
    return pl.pallas_call(
        hidden_grad_kernel,
        grid=(hidden // tile,),
        in_specs=[
            SMEM,
            pl.BlockSpec((BLOCK, width), lambda i: (0, 0)),
            pl.BlockSpec((tile, width), lambda i: (i, 0)),
        ],
        out_specs=[
            pl.BlockSpec((BLOCK, tile), lambda i: (0, i)),
            pl.BlockSpec((1, width), lambda i: (0, 0)),
        ],
        out_shape=[struct((BLOCK, hidden), bf16), struct((1, width), f32)],
        compiler_params=params(16),
        cost_estimate=cost(2 * BLOCK * width * hidden, 2 * hidden * width + 2 * BLOCK * hidden),
        name="hidden_grad",
    )(spots, cot, w_down)


def build_kernel(
    spots, tower, incoming, cls, w_img, b_img, w_txt, b_txt, gain, bias, w_qkv, b_q, b_v,
    raw, x, qkv,
):
    def picker(cols, low, high, shift):
        at = row_ids((BLOCK, cols))
        col = lax.broadcasted_iota(jnp.int32, (BLOCK, cols), 1)
        hit = (col == at + shift) & (at >= low) & (at < high)
        return jnp.where(hit, 1.0, 0.0).astype(bf16)

    picked = dot(picker(tower.shape[0], spots[0], spots[1], spots[2]), tower[...])
    picked += dot(picker(incoming.shape[0], spots[3], spots[4], spots[5]), incoming[...])
    raw[...] = picked.astype(bf16)
    count = spots[6]
    edge, over = 192, 208
    image = dot(raw[:over], w_img[...]) + b_img[...].astype(f32)
    text = dot(raw[edge:], w_txt[...]) + b_txt[...].astype(f32)
    at = row_ids((edge, 1))
    top = jnp.where(at == 0, cls[...].astype(f32), image[:edge])
    at = row_ids((over - edge, 1)) + edge
    mid = jnp.where(at < 1 + PATCHES, image[edge:], text[: over - edge])
    mid = jnp.where(at < count, mid, 0.0)
    at = row_ids((BLOCK - over, 1)) + over
    low = jnp.where(at < count, text[over - edge :], 0.0)
    x[:edge] = top.astype(bf16)
    x[edge:over] = mid.astype(bf16)
    x[over:] = low.astype(bf16)
    normed, _ = norm_stats(x[...].astype(f32))
    a = (normed * gain[...].astype(f32) + bias[...].astype(f32)).astype(bf16)
    width = x.shape[1]
    q = dot(a, w_qkv[:, :width]) + b_q[...].astype(f32)
    qkv[:, :width] = q.astype(bf16) * jnp.asarray(0.125, bf16)
    qkv[:, width : 2 * width] = dot(a, w_qkv[:, width : 2 * width]).astype(bf16)
    v = dot(a, w_qkv[:, 2 * width :]) + b_v[...].astype(f32)
    qkv[:, 2 * width :] = v.astype(bf16)


def build(spots, tower, incoming, cls, w_img, b_img, w_txt, b_txt, gain, bias, w_qkv, b_q, b_v):
    width = tower.shape[1]
    args = (spots, tower, incoming, cls, w_img, b_img, w_txt, b_txt, gain, bias, w_qkv, b_q, b_v)
    return pl.pallas_call(
        build_kernel,
        in_specs=[SMEM] + [VMEM] * (len(args) - 1),
        out_specs=[VMEM] * 3,
        out_shape=[
            struct((BLOCK, width), bf16),
            struct((BLOCK, width), bf16),
            struct((BLOCK, 3 * width), bf16),
        ],
        compiler_params=params(40),
        cost_estimate=cost(2 * BLOCK * width * width * 6, 2 * width * width * 5 + 6 * BLOCK * width),
        name="build",
    )(*args)


def attend_kernel(spots, qkv, x, w_out, b_out, gain, bias, o_t, lse, h, m, m_t, probs):
    width = x.shape[1]
    count = spots[6]
    lane = lax.broadcasted_iota(jnp.int32, (BLOCK, 128), 1)
    dead = row_ids((BLOCK, 1)) >= count

    def pair(p, carry):
        def cols(k):
            return pl.ds(pl.multiple_of(k * width + p * 128, 128), 128)

        q, keys, values = qkv[:, cols(0)], qkv[:, cols(1)], qkv[:, cols(2)]
        v_t = values.T
        for head in range(2):
            own = (lane < HEAD) if head == 0 else (lane >= HEAD)
            s_t = dot(jnp.where(own, keys, jnp.zeros_like(keys)), q, NT)
            s_t = jnp.where(dead, -1000000000.0, s_t)
            top = jnp.max(s_t, axis=0, keepdims=True)
            e = jnp.exp(s_t - top)
            total = jnp.sum(e, axis=0, keepdims=True)
            probs[...] = e.astype(bf16)
            part = dot(v_t[head * HEAD : (head + 1) * HEAD], probs[...]) * (1.0 / total)
            at = pl.multiple_of(p * 128 + head * HEAD, HEAD)
            o_t[pl.ds(at, HEAD), :] = part.astype(bf16)
            lse[pl.ds(p * 2 + head, 1), :] = top + jnp.log(total)
        return carry

    lax.fori_loop(0, width // 128, pair, 0)
    h[...] = (
        x[...].astype(f32) + dot(o_t[...].T, w_out[...]) + b_out[...].astype(f32)
    )
    normed, _ = norm_stats(h[...])
    low = (normed * gain[...].astype(f32) + bias[...].astype(f32)).astype(bf16)
    m[...] = low
    m_t[...] = low.T


def attend(spots, qkv, x, w_out, b_out, gain, bias):
    width = x.shape[1]
    args = (spots, qkv, x, w_out, b_out, gain, bias)
    return pl.pallas_call(
        attend_kernel,
        in_specs=[SMEM] + [VMEM] * (len(args) - 1),
        out_specs=[VMEM] * 5,
        out_shape=[
            struct((width, BLOCK), bf16),
            struct((width // HEAD, BLOCK), f32),
            struct((BLOCK, width), f32),
            struct((BLOCK, width), bf16),
            struct((width, BLOCK), bf16),
        ],
        scratch_shapes=[pltpu.VMEM((BLOCK, BLOCK), bf16)],
        compiler_params=params(40),
        cost_estimate=cost(2 * BLOCK * width * (width + 8 * BLOCK), 12 * BLOCK * width),
        name="attend",
    )(*args)


def feed_kernel(
    spots, m, m_t, grad, w_up, b_up, w_down, h, cot, b_down,
    out, d_m, up_theirs, up_own, down_theirs, down_own, d_b_up,
    dy, total,
):
    step = pl.program_id(0)
    last = pl.num_programs(0) - 1
    core = spots[7]
    half = down_own.shape[1]
    live = row_ids((BLOCK, 1)) < spots[6]

    @pl.when(step == 0)
    def _():
        kept = jnp.where(live, cot[...], jnp.zeros_like(cot))
        first, second = kept[:, :half], kept[:, half:]
        dy[0] = jnp.where(core == 0, second, first)
        dy[1] = jnp.where(core == 0, first, second)

    inner = dot(m[...], w_up[...]) + b_up[...].astype(f32)
    below = 0.5 + 0.5 * lax.erf(inner * math.sqrt(0.5))
    active = (inner * below).astype(bf16)
    slope = below + inner * jnp.exp(-0.5 * inner * inner) * (1.0 / math.sqrt(2.0 * math.pi))
    d_low = (grad[...].astype(f32) * slope).astype(bf16)
    d_b_up[...] = jnp.sum(d_low.astype(f32), axis=0, keepdims=True)
    more = dot(active, w_down[...])
    back = dot(d_low, w_up[...], NT)

    @pl.when(step == 0)
    def _():
        d_m[...] = back
        total[...] = h[...] + b_down[...].astype(f32) + more

    @pl.when(step > 0)
    def _():
        d_m[...] += back
        total[...] += more

    active_t = active.T
    down_theirs[...] = dot(active_t, dy[0]).astype(bf16)
    down_own[...] = dot(active_t, dy[1]).astype(bf16)
    d_up = dot(m_t[...], d_low).astype(bf16)

    @pl.when(step <= last // 2)
    def _():
        up_theirs[...] = d_up

    @pl.when(step > last // 2)
    def _():
        up_own[...] = d_up

    @pl.when(step == last)
    def _():
        out[...] = jnp.where(live, total[...], 0.0).astype(bf16)


def feed(spots, m, m_t, grad, w_up, b_up, w_down, h, cot, b_down, tile=512):
    width, hidden = w_up.shape
    steps = hidden // tile
    half = steps // 2

    def at(i, spots):
        return lax.rem(i + half * (1 - spots[7]), steps)

    def whole(*shape):
        return pl.BlockSpec(shape, lambda i, spots: (0, 0))

    by_column = pl.BlockSpec((width, tile), lambda i, spots: (0, at(i, spots)))
    return pl.pallas_call(
        feed_kernel,
        grid_spec=pltpu.PrefetchScalarGridSpec(
            num_scalar_prefetch=1,
            grid=(steps,),
            in_specs=[
                whole(BLOCK, width),
                whole(width, BLOCK),
                pl.BlockSpec((BLOCK, tile), lambda i, spots: (0, at(i, spots))),
                by_column,
                pl.BlockSpec((1, tile), lambda i, spots: (0, at(i, spots))),
                pl.BlockSpec((tile, width), lambda i, spots: (at(i, spots), 0)),
                whole(BLOCK, width),
                whole(BLOCK, width),
                whole(1, width),
            ],
            out_specs=[
                whole(BLOCK, width),
                whole(BLOCK, width),
                pl.BlockSpec((width, tile), lambda i, spots: (0, jnp.minimum(i, half - 1))),
                pl.BlockSpec((width, tile), lambda i, spots: (0, jnp.maximum(i - half, 0))),
                pl.BlockSpec((tile, width // 2), lambda i, spots: (at(i, spots), 0)),
                pl.BlockSpec((tile, width // 2), lambda i, spots: (at(i, spots), 0)),
                pl.BlockSpec((1, tile), lambda i, spots: (0, at(i, spots))),
            ],
            scratch_shapes=[pltpu.VMEM((2, BLOCK, width // 2), bf16), pltpu.VMEM((BLOCK, width), f32)],
        ),
        out_shape=[
            struct((BLOCK, width), bf16),
            struct((BLOCK, width), f32),
            struct((width, hidden // 2), bf16),
            struct((width, hidden // 2), bf16),
            struct((hidden, width // 2), bf16),
            struct((hidden, width // 2), bf16),
            struct((1, hidden), f32),
        ],
        compiler_params=params(48),
        cost_estimate=cost(10 * BLOCK * width * hidden, 8 * hidden * width),
        name="feed",
    )(spots, m, m_t, grad, w_up, b_up, w_down, h, cot, b_down)


def unattend_kernel(
    spots, h, d_m, cot, gain, w_out, qkv, lse,
    d_h, d_low, d_qkv, sums,
    d_o, ds_t, probs,
):
    width = h.shape[1]
    count = spots[6]
    live = row_ids((BLOCK, 1)) < count
    normed, factor = norm_stats(h[...])
    up = d_m[...]
    sums[0:1] = jnp.sum(up * normed, axis=0, keepdims=True)
    sums[1:2] = jnp.sum(up, axis=0, keepdims=True)
    kept = jnp.where(live, cot[...].astype(f32), 0.0)
    grad = kept + norm_back(up * gain[...].astype(f32), normed, factor)
    d_h[...] = grad
    low = grad.astype(bf16)
    d_low[...] = low
    sums[2:3] = jnp.sum(low.astype(f32), axis=0, keepdims=True)
    d_o[...] = dot(low, w_out[...], NT).astype(bf16)
    lane = lax.broadcasted_iota(jnp.int32, (BLOCK, 128), 1)
    dead = row_ids((BLOCK, 1)) >= count

    def pair(p, carry):
        def cols(k):
            return pl.ds(pl.multiple_of(k * width + p * 128, 128), 128)

        q, keys, values = qkv[:, cols(0)], qkv[:, cols(1)], qkv[:, cols(2)]
        up = d_o[:, cols(0)]
        k_t = keys.T
        d_q, d_k, d_v = [], [], []
        for head in range(2):
            own = (lane < HEAD) if head == 0 else (lane >= HEAD)
            s_t = dot(jnp.where(own, keys, jnp.zeros_like(keys)), q, NT)
            p_t = jnp.exp(s_t - lse[pl.ds(p * 2 + head, 1), :])
            p_t = jnp.where(dead, 0.0, p_t)
            probs[...] = p_t.astype(bf16)
            g_t = dot(jnp.where(own, values, jnp.zeros_like(values)), up, NT)
            inner = p_t * g_t
            total = jnp.sum(inner, axis=0, keepdims=True)
            ds_t[...] = (inner - p_t * total).astype(bf16)
            d_v.append(dot(probs[...], up))
            d_k.append(dot(ds_t[...], q))
            d_q.append(dot(k_t[head * HEAD : (head + 1) * HEAD], ds_t[...]))
        first = lane < HEAD
        dq = (jnp.concatenate(d_q, axis=0) * 0.125).T
        d_qkv[:, cols(0)] = dq.astype(bf16)
        d_qkv[:, cols(1)] = jnp.where(first, d_k[0], d_k[1]).astype(bf16)
        d_qkv[:, cols(2)] = jnp.where(first, d_v[0], d_v[1]).astype(bf16)
        return carry

    lax.fori_loop(0, width // 128, pair, 0)
    sums[3:4] = jnp.sum(d_qkv[:, :width].astype(f32), axis=0, keepdims=True)
    sums[4:5] = jnp.sum(d_qkv[:, 2 * width :].astype(f32), axis=0, keepdims=True)


def unattend(spots, h, d_m, cot, gain, w_out, qkv, lse):
    width = h.shape[1]
    args = (spots, h, d_m, cot, gain, w_out, qkv, lse)
    return pl.pallas_call(
        unattend_kernel,
        in_specs=[SMEM] + [VMEM] * (len(args) - 1),
        out_specs=[VMEM] * 4,
        out_shape=[
            struct((BLOCK, width), f32),
            struct((BLOCK, width), bf16),
            struct((BLOCK, 3 * width), bf16),
            struct((8, width), f32),
        ],
        scratch_shapes=[
            pltpu.VMEM((BLOCK, width), bf16),
            pltpu.VMEM((BLOCK, BLOCK), bf16),
            pltpu.VMEM((BLOCK, BLOCK), bf16),
        ],
        compiler_params=params(40),
        cost_estimate=cost(2 * BLOCK * width * (width + 10 * BLOCK), 16 * BLOCK * width),
        name="unattend",
    )(*args)


def qkv_grad_kernel(spots, x, gain, bias, d_qkv, theirs, own):
    core = spots[7]
    normed, _ = norm_stats(x[...].astype(f32))
    a_t = (normed * gain[...].astype(f32) + bias[...].astype(f32)).astype(bf16).T
    half = own.shape[1]
    own[...] = dot(a_t, d_qkv[:, pl.ds(pl.multiple_of(core * half, 128), half)]).astype(bf16)
    theirs[...] = dot(
        a_t, d_qkv[:, pl.ds(pl.multiple_of((1 - core) * half, 128), half)]
    ).astype(bf16)


def qkv_grad(spots, x, gain, bias, d_qkv):
    width = x.shape[1]
    return pl.pallas_call(
        qkv_grad_kernel,
        in_specs=[SMEM] + [VMEM] * 4,
        out_specs=[VMEM] * 2,
        out_shape=[struct((width, 3 * width // 2), bf16)] * 2,
        compiler_params=params(40),
        cost_estimate=cost(6 * BLOCK * width * width, 6 * width * width),
        name="qkv_grad",
    )(spots, x, gain, bias, d_qkv)


def finish_kernel(
    spots, x, d_qkv, w_qkv, gain, d_h, raw, w_img, w_txt, o_t, d_low, sums, d_b_down, tall,
    theirs, own, own_rows, window,
    vectors,
):
    core = spots[7]
    width = x.shape[1]
    half = width // 2
    normed, factor = norm_stats(x[...].astype(f32))
    d_a = dot(d_qkv[...], w_qkv[...], NT)
    d_x = d_h[...] + norm_back(d_a * gain[...].astype(f32), normed, factor)
    at = row_ids((BLOCK, 1))
    is_image = (at >= 1) & (at < 1 + PATCHES)
    is_text = (at >= 1 + PATCHES) & (at < spots[6])
    image = jnp.where(is_image, d_x, 0.0).astype(bf16)
    text = jnp.where(is_text, d_x, 0.0).astype(bf16)

    vectors[...] = jnp.zeros_like(vectors)
    vectors[0:1] = d_x[0:1]
    vectors[1:2] = jnp.sum(image.astype(f32), axis=0, keepdims=True)
    vectors[2:3] = jnp.sum(text.astype(f32), axis=0, keepdims=True)
    vectors[3:4] = jnp.sum(d_a * normed, axis=0, keepdims=True)
    vectors[4:5] = jnp.sum(d_a, axis=0, keepdims=True)
    vectors[5:6] = sums[3:4]
    vectors[6:7] = sums[4:5]
    vectors[7:8] = sums[2:3]
    vectors[8:9] = sums[0:1]
    vectors[9:10] = sums[1:2]
    vectors[10:11] = d_b_down[...]
    vectors[11:15] = tall[...]

    raw_t = raw[...].T
    for target, side in ((theirs, 1 - core), (own, core)):
        columns = pl.ds(pl.multiple_of(side * half, 128), half)
        target[:, :half] = dot(o_t[...], d_low[:, columns]).astype(bf16)
        first = jnp.where(side == 0, image[:, :half], image[:, half:])
        target[:, half : 2 * half] = dot(raw_t[:, :256], first[:256]).astype(bf16)
        second = jnp.where(side == 0, text[:, :half], text[:, half:])
        target[:, 2 * half : 3 * half] = dot(raw_t, second).astype(bf16)
        picked = vectors[pl.ds(pl.multiple_of(side * 8, 8), 8)]
        tall_form = jnp.concatenate([picked, jnp.zeros((120, width), f32)], axis=0).T
        target[:, 3 * half :] = tall_form.astype(bf16)

    rows = dot(image, w_img[...], NT) + dot(text, w_txt[...], NT)
    rows = rows.astype(bf16)

    def placer(count, low, high, shift):
        at = lax.broadcasted_iota(jnp.int32, (count, BLOCK), 1)
        row = row_ids((count, BLOCK))
        hit = (row == at + shift) & (at >= low) & (at < high)
        return jnp.where(hit, 1.0, 0.0).astype(bf16)

    own_rows[...] = dot(placer(own_rows.shape[0], spots[0], spots[1], spots[2]), rows).astype(bf16)
    window[...] = dot(placer(window.shape[0], spots[3], spots[4], spots[5]), rows).astype(bf16)


def finish(
    spots, x, d_qkv, w_qkv, gain, d_h, raw, w_img, w_txt, o_t, d_low, sums, d_b_down, tall, span
):
    width = x.shape[1]
    args = (
        spots, x, d_qkv, w_qkv, gain, d_h, raw, w_img, w_txt, o_t, d_low, sums, d_b_down, tall
    )
    return pl.pallas_call(
        finish_kernel,
        in_specs=[SMEM] + [VMEM] * (len(args) - 1),
        out_specs=[VMEM] * 4,
        out_shape=[
            struct((width, 3 * width // 2 + 128), bf16),
            struct((width, 3 * width // 2 + 128), bf16),
            struct((span, width), bf16),
            struct((WINDOW, width), bf16),
        ],
        scratch_shapes=[pltpu.VMEM((16, width), f32)],
        compiler_params=params(48),
        cost_estimate=cost(2 * BLOCK * width * width * 10, 14 * width * width),
        name="finish",
    )(*args)


def swap(x, axis, bit):
    count = lax.axis_size(axis)
    route = [(i, i ^ (1 << bit)) for i in range(count)]
    return lax.ppermute(x, axis, route)


def add_low(one, two):
    f32 = jnp.float32
    return (one.astype(f32) + two.astype(f32)).astype(jnp.bfloat16)


def over_cores(theirs, own):
    return add_low(own, swap(theirs, "dp", 0))


def halving(part, order):
    wide = lax.axis_size("wide")
    place = lax.axis_index("wide")
    bits = wide.bit_length() - 1
    rows, cols = part.shape
    part = part.reshape([2] * bits + [rows // wide, cols])
    for bit in order:
        axis = bits - 1 - bit
        mine = (place >> bit) & 1
        keep = lax.dynamic_index_in_dim(part, mine, axis, keepdims=True)
        send = lax.dynamic_index_in_dim(part, 1 - mine, axis, keepdims=True)
        part = add_low(keep, swap(send, "wide", bit))
    return part.reshape(rows // wide, cols)


def both(share):
    core = lax.axis_index("dp")
    other = swap(share, "dp", 0)
    first = jnp.where(core == 0, share, other)
    second = jnp.where(core == 0, other, share)
    return first.astype(f32), second.astype(f32)


def on_device(
    tower_states,
    caption_lengths,
    assignment,
    cls_token,
    w_img,
    b_img,
    w_txt,
    b_txt,
    gain_one,
    bias_one,
    w_qkv,
    b_query,
    b_value,
    w_out,
    b_out,
    gain_two,
    bias_two,
    w_up,
    b_up,
    w_down,
    b_down,
    cotangent,
):
    wide = lax.axis_size("wide")
    place = lax.axis_index("wide")
    core = lax.axis_index("dp")
    upper = place >= wide // 2
    pair = place % (wide // 2)
    lens = lax.dynamic_index_in_dim(caption_lengths[0], pair, 0, keepdims=False)
    order = lax.dynamic_index_in_dim(assignment[0], pair, 0, keepdims=False)
    rows = tower_states[0]
    span, width = rows.shape
    bits = wide.bit_length() - 1
    mine = jnp.where(upper, order[1], order[0])
    other = jnp.where(upper, order[0], order[1])
    gap = span - WINDOW
    incoming = swap(jnp.where(other == 0, rows[:WINDOW], rows[gap:]), "wide", bits - 1)
    start = jnp.where(mine == 0, 0, lens[0])
    cut = 1 + PATCHES
    count = cut + jnp.where(mine == 0, lens[0], lens[1])
    image_shift, text_shift = mine * PATCHES - 1, start - cut
    back = jnp.where(mine == 0, 0, gap)
    image_spot = [1, cut, image_shift]
    text_spot = [cut, count, text_shift]
    spots = [jnp.where(upper, t, i) for t, i in zip(text_spot, image_spot)]
    spots += [jnp.where(upper, i, t) for t, i in zip(text_spot, image_spot)]
    spots[5] -= back
    spots = jnp.stack(spots + [count, core]).astype(jnp.int32)

    def flat(vector):
        return vector.reshape(1, -1)

    cot = cotangent[0]
    grad, d_b_down = hidden_grad(spots, cot, w_down)
    tower = jnp.pad(rows, ((0, -span % 16), (0, 0)))
    raw, x, qkv = build(
        spots, tower, incoming, flat(cls_token), w_img, flat(b_img), w_txt, flat(b_txt),
        flat(gain_one), flat(bias_one), w_qkv, flat(b_query), flat(b_value),
    )
    o_t, lse, h, m, m_t = attend(
        spots, qkv, x, w_out, flat(b_out), flat(gain_two), flat(bias_two)
    )
    out, d_m, up_theirs, up_own, down_theirs, down_own, d_b_up = feed(
        spots, m, m_t, grad, w_up, flat(b_up), w_down, h, cot, flat(b_down)
    )
    d_h, d_low, d_qkv, sums = unattend(spots, h, d_m, cot, flat(gain_two), w_out, qkv, lse)
    qkv_theirs, qkv_own = qkv_grad(spots, x, flat(gain_one), flat(bias_one), d_qkv)
    tall = d_b_up.reshape(wide, 4, width // wide).swapaxes(0, 1).reshape(4, width)
    rest_theirs, rest_own, own_rows, window = finish(
        spots, x, d_qkv, w_qkv, flat(gain_one), d_h, raw, w_img, w_txt, o_t, d_low, sums,
        d_b_down, tall, span,
    )
    returned = swap(window, "wide", bits - 1)
    returned = jnp.where(
        other == 0,
        jnp.pad(returned, ((0, gap), (0, 0))),
        jnp.pad(returned, ((gap, 0), (0, 0))),
    )
    d_rows = own_rows + returned

    straight = list(range(bits))
    crossed = [1, 0] + straight[2:]
    down = halving(over_cores(down_theirs, down_own), straight)
    up = halving(over_cores(up_theirs, up_own), crossed)
    d_w_qkv = halving(over_cores(qkv_theirs, qkv_own), straight)
    rest = halving(over_cores(rest_theirs, rest_own), crossed)
    down, up, d_w_qkv = [jnp.concatenate(both(t), axis=1) for t in (down, up, d_w_qkv)]
    first, second = both(rest)
    half = width // 2
    out_grad, img, txt = [
        jnp.concatenate([first[:, i : i + half], second[:, i : i + half]], axis=1)
        for i in (0, half, width)
    ]
    first, second = first[:, 3 * half :], second[:, 3 * half :]
    vectors = [first[:, i] for i in range(8)] + [second[:, i] for i in range(3)]
    d_b_up = second[:, 3:7].T.reshape(-1)
    (
        d_cls,
        d_b_img,
        d_b_txt,
        d_gain_one,
        d_bias_one,
        d_b_query,
        d_b_value,
        d_b_out,
        d_gain_two,
        d_bias_two,
        d_b_down,
    ) = vectors
    return (
        out[None],
        d_rows[None],
        d_cls,
        img,
        d_b_img,
        txt,
        d_b_txt,
        d_gain_one,
        d_bias_one,
        d_w_qkv,
        d_b_query,
        d_b_value,
        out_grad,
        d_b_out,
        d_gain_two,
        d_bias_two,
        up,
        d_b_up,
        down,
        d_b_down,
    )


def solution(mesh):
    placed = (
        P("dp", "wide", None),
        P("dp", None, None),
        P("dp", None, None),
        P(),
        P(),
        P(),
        P(),
        P(),
        P(),
        P(),
        P(),
        P(),
        P(),
        P(),
        P(),
        P(),
        P(),
        P(),
        P(),
        P(),
        P(),
        P("dp", "wide", None),
    )
    return jax.shard_map(
        on_device,
        mesh=mesh,
        in_specs=placed,
        out_specs=(
            P("dp", "wide", None),
            P("dp", "wide", None),
            P("wide"),
            P("wide", None),
            P("wide"),
            P("wide", None),
            P("wide"),
            P("wide"),
            P("wide"),
            P("wide", None),
            P("wide"),
            P("wide"),
            P("wide", None),
            P("wide"),
            P("wide"),
            P("wide"),
            P("wide", None),
            P("wide"),
            P("wide", None),
            P("wide"),
        ),
        check_vma=False,
    )
```

```python
from functools import partial
import math
import jax
import jax.numpy as jnp
from jax import lax
from jax.experimental import pallas as pl
from jax.experimental.pallas import tpu as pltpu
from jax.sharding import PartitionSpec as P

HEAD = 64
PATCHES = 197
BLOCK = 512
WINDOW = 320
TILE = 768
TOGETHER = 2
PARTS = 3
bf16 = jnp.bfloat16
f32 = jnp.float32
VMEM = pl.BlockSpec(memory_space=pltpu.VMEM)
SMEM = pl.BlockSpec(memory_space=pltpu.SMEM)
ANY = pl.BlockSpec(memory_space=pl.ANY)
HBM = pl.BlockSpec(memory_space=pltpu.HBM)
NN = (((1,), (0,)), ((), ()))
NT = (((1,), (1,)), ((), ()))
TN = (((0,), (0,)), ((), ()))


def dot(left, right, dims=NN):
    return lax.dot_general(left, right, dims, preferred_element_type=f32)


def params(mib, **more):
    return pltpu.CompilerParams(vmem_limit_bytes=mib << 20, **more)


def start_copy(group, source, target, sem):
    copy = pltpu.make_async_copy(source, target, sem)
    copy.start()
    group.append(copy)


def wait_all(group):
    for copy in group:
        copy.wait()


def columns(side, size):
    return pl.ds(pl.multiple_of(side * size, 128), size)


def cost(microseconds):
    flops = int(microseconds * 1153000000)
    return pl.CostEstimate(flops=flops, bytes_accessed=1024, transcendentals=0)


def struct(shape, dtype):
    return jax.ShapeDtypeStruct(shape, dtype)


def row(vector):
    return vector[...].astype(f32).reshape(1, -1)


def pick(vectors, k):
    return vectors[k : k + 1].astype(f32)


def row_ids(shape):
    return lax.broadcasted_iota(jnp.int32, shape, 0)


def norm_stats(rows):
    mean = jnp.mean(rows, axis=-1, keepdims=True)
    centred = rows - mean
    factor = lax.rsqrt(jnp.mean(centred * centred, axis=-1, keepdims=True) + 1e-05)
    return centred * factor, factor


def norm_back(scaled, normed, factor):
    return factor * (
        scaled
        - jnp.mean(scaled, axis=-1, keepdims=True)
        - normed * jnp.mean(scaled * normed, axis=-1, keepdims=True)
    )


def open_kernel(tables, rows, payload, spots):
    place, core = lax.axis_index("wide"), lax.axis_index("dp")
    half = lax.axis_size("wide") // 2
    upper = place >= half
    pair = lax.rem(place, half)

    def entry(table, column):
        value = tables[table]
        hit = (row_ids(value.shape) == pair) & (
            lax.broadcasted_iota(jnp.int32, value.shape, 1) == column
        )
        return jnp.sum(jnp.where(hit, value, 0))

    span = rows.shape[1]
    gap = span - WINDOW
    mine = entry(1, jnp.where(upper, 1, 0))
    other = 1 - mine
    first = entry(0, 0)
    begin = jnp.where(mine == 0, 0, first)
    cut = 1 + PATCHES
    count = cut + entry(0, mine)
    back = jnp.where(mine == 0, 0, gap)
    image, text = mine * PATCHES - 1, begin - cut
    spots[0] = jnp.where(upper, cut, 1)
    spots[1] = jnp.where(upper, count, cut)
    spots[2] = jnp.where(upper, text, image)
    spots[3] = jnp.where(upper, 1, cut)
    spots[4] = jnp.where(upper, cut, count)
    spots[5] = jnp.where(upper, image, text) - back
    spots[6] = count
    spots[7] = core
    spots[8] = other
    spots[9] = place
    value = rows[0]
    payload[...] = jnp.where(other == 0, value[:WINDOW], value[gap:])


def opening(lens, order, rows):
    width = rows.shape[2]
    return pl.pallas_call(
        open_kernel,
        in_specs=[VMEM, VMEM],
        out_specs=[VMEM, SMEM],
        out_shape=[struct((WINDOW, width), bf16), struct((10,), jnp.int32)],
        compiler_params=params(8),
        cost_estimate=cost(2),
        name="opening",
    )(jnp.concatenate([lens, order], axis=0), rows)


def hidden_grad_kernel(spots, cot, w_down, grad, d_bias, dy_other):
    live = row_ids((BLOCK, 1)) < spots[6]
    dy = jnp.where(live, cot[...], jnp.zeros_like(cot))
    grad[...] = dot(dy, w_down[...], NT).astype(bf16)

    @pl.when(pl.program_id(0) == 0)
    def _():
        d_bias[...] = jnp.sum(dy.astype(f32), axis=0, keepdims=True)
        half = dy_other.shape[1]
        dy_other[...] = jnp.where(spots[7] == 0, dy[:, half:], dy[:, :half])


def hidden_grad(spots, cot, w_down):
    hidden, width = w_down.shape
    return pl.pallas_call(
        hidden_grad_kernel,
        grid=(hidden // TILE,),
        in_specs=[
            SMEM,
            pl.BlockSpec((BLOCK, width), lambda i: (0, 0)),
            pl.BlockSpec((TILE, width), lambda i: (i, 0)),
        ],
        out_specs=[
            pl.BlockSpec((BLOCK, TILE), lambda i: (0, i)),
            pl.BlockSpec((1, width), lambda i: (0, 0)),
            pl.BlockSpec((BLOCK, width // 2), lambda i: (0, 0)),
        ],
        out_shape=[
            struct((BLOCK, hidden), bf16),
            struct((1, width), f32),
            struct((BLOCK, width // 2), bf16),
        ],
        compiler_params=params(16),
        cost_estimate=cost(4.4),
        name="hidden_grad",
    )(spots, cot, w_down)


def bias_tile(b_up, side, start):
    half = b_up.shape[0] // 2
    one, two = b_up[pl.ds(start, TILE)], b_up[pl.ds(half + start, TILE)]
    return jnp.where(side == 0, one.astype(f32), two.astype(f32)).reshape(1, -1)


def hidden_tile(m, w, b, grad, g, du):
    inner = dot(m, w) + b
    below = 0.5 + 0.5 * lax.erf(inner * math.sqrt(0.5))
    g[...] = (inner * below).astype(bf16)
    slope = below + inner * jnp.exp(-0.5 * inner * inner) * (1.0 / math.sqrt(2.0 * math.pi))
    low = (grad.astype(f32) * slope).astype(bf16)
    du[...] = low
    return jnp.sum(low.astype(f32), axis=0, keepdims=True)


def assemble(spots, rows, tower, incoming, vectors, w_img, w_txt, raw, x, waits):
    def picker(cols, low, high, shift):
        at = row_ids((BLOCK, cols))
        col = lax.broadcasted_iota(jnp.int32, (BLOCK, cols), 1)
        hit = (col == at + shift) & (at >= low) & (at < high)
        return jnp.where(hit, 1.0, 0.0).astype(bf16)

    span = rows.shape[1]
    tower[:span] = rows[0]
    tower[span:] = jnp.zeros((tower.shape[0] - span, rows.shape[2]), bf16)
    picked = dot(picker(tower.shape[0], spots[0], spots[1], spots[2]), tower[...])
    picked += dot(picker(incoming.shape[0], spots[3], spots[4], spots[5]), incoming[...])
    raw[...] = picked.astype(bf16)
    count = spots[6]
    edge, over = 192, 208
    waits[0].wait()
    image = dot(raw[:over], w_img[...]) + pick(vectors, 1)
    waits[1].wait()
    text = dot(raw[edge:], w_txt[...]) + pick(vectors, 2)
    at = row_ids((edge, 1))
    top = jnp.where(at == 0, pick(vectors, 0), image[:edge])
    at = row_ids((over - edge, 1)) + edge
    mid = jnp.where(at < 1 + PATCHES, image[edge:], text[: over - edge])
    mid = jnp.where(at < count, mid, 0.0)
    at = row_ids((BLOCK - over, 1)) + over
    low = jnp.where(at < count, text[over - edge :], 0.0)
    x[:edge] = top.astype(bf16)
    x[edge:over] = mid.astype(bf16)
    x[over:] = low.astype(bf16)


def attend(count, qkv, o_t, inverse, weights, kept, stores, sem):
    width = o_t.shape[0]
    lane = lax.broadcasted_iota(jnp.int32, (BLOCK, 128), 1)
    dead = row_ids((BLOCK, 1)) >= count
    group = 2 * TOGETHER
    for first in range(0, width // HEAD, group):
        scores = []
        for head in range(first, first + group):
            at = head // 2 * 128
            q, keys = qkv[:, at : at + 128], qkv[:, width + at : width + at + 128]
            own = (lane < HEAD) if head % 2 == 0 else (lane >= HEAD)
            scores.append(dot(jnp.where(own, keys, jnp.zeros_like(keys)), q, NT))
        for head, s_t in zip(range(first, first + group), scores):
            s_t = jnp.where(dead, -1000000000.0, s_t)
            top = jnp.max(s_t, axis=0, keepdims=True)
            e = jnp.exp(s_t - top)
            one_over = 1.0 / jnp.sum(e, axis=0, keepdims=True)
            weights[head] = e.astype(bf16)
            values = qkv[:, 2 * width + head // 2 * 128 : 2 * width + head // 2 * 128 + 128]
            v_t = values.T[head % 2 * HEAD : (head % 2 + 1) * HEAD]
            part = dot(v_t, weights[head]) * one_over
            o_t[head * HEAD : (head + 1) * HEAD] = part.astype(bf16)
            inverse[head : head + 1] = one_over
        heads = pl.ds(first, group)
        start_copy(stores, weights.at[heads], kept.at[heads], sem.at[first // group])


def forward_kernel(
    spots, rows, incoming, vectors, b_up, w_img_in, w_txt_in, w_qkv_in, w_out_in, w_up_in, grad_in,
    after,
    x_out, qkv_out, kept, du_out, h_out, early, late, g_low, g_high, inverse, d_b,
    w_img, w_txt, w_qkv, w_out, w_up, grad, tower, x, qkv, o_t, weights, du_own, h, g,
    in_sem, out_sem, kept_sem, hidden_sem,
):
    width, hidden = w_up_in.shape
    part = hidden // 2
    tiles = part // TILE
    core = spots[7]
    waits, stores = [], []
    for k, (source, target) in enumerate(
        ((w_img_in, w_img), (w_txt_in, w_txt), (w_qkv_in, w_qkv), (w_out_in, w_out))
    ):
        start_copy(waits, source, target, in_sem.at[k])
    for k, side in enumerate((1 - core, core)):
        start_copy(waits, w_up_in.at[:, columns(side, part)], w_up.at[k], in_sem.at[4 + 2 * k])
        start_copy(waits, grad_in.at[:, columns(side, part)], grad.at[k], in_sem.at[5 + 2 * k])
    raw, a = early.at[0], early.at[1]
    assemble(spots, rows, tower, incoming, vectors, w_img, w_txt, raw, x, waits)
    start_copy(stores, x, x_out, out_sem.at[0])
    normed, _ = norm_stats(x[...].astype(f32))
    a[...] = (normed * pick(vectors, 3) + pick(vectors, 4)).astype(bf16)
    waits[2].wait()
    q = dot(a[...], w_qkv[:, :width]) + pick(vectors, 5)
    qkv[:, :width] = q.astype(bf16) * jnp.asarray(0.125, bf16)
    qkv[:, width : 2 * width] = dot(a[...], w_qkv[:, width : 2 * width]).astype(bf16)
    qkv[:, 2 * width :] = (dot(a[...], w_qkv[:, 2 * width :]) + pick(vectors, 6)).astype(bf16)
    start_copy(stores, qkv, qkv_out, out_sem.at[1])
    inverse[...] = jnp.zeros_like(inverse)
    attend(spots[6], qkv, o_t, inverse, weights, kept, stores, kept_sem)
    o = o_t[...].T
    early[2] = o
    waits[3].wait()
    h[...] = x[...].astype(f32) + dot(o, w_out[...]) + pick(vectors, 7)
    start_copy(stores, h, h_out, out_sem.at[2])
    normed, _ = norm_stats(h[...])
    m = late.at[0]
    m[...] = (normed * pick(vectors, 8) + pick(vectors, 9)).astype(bf16)
    for k in range(4, 8):
        waits[k].wait()
    for k, side in enumerate((1 - core, core)):
        for j in range(tiles):
            at = pl.ds(j * TILE, TILE)
            b = bias_tile(b_up, side, j * TILE)
            target = late.at[1 + j] if k == 0 else du_own.at[j]
            sums = hidden_tile(m[...], w_up[k, :, at], b, grad[k, :, at], g.at[k, j], target)
            d_b[pl.ds(side, 1), at] = sums
            if k == 1:
                start_copy(stores, target, du_out.at[j], hidden_sem.at[j])
    core_first = core == 0
    g_low[...] = jnp.where(core_first, g[1], g[0])
    g_high[...] = jnp.where(core_first, g[0], g[1])
    wait_all(stores)


def forward(spots, rows, incoming, vectors, b_up, weights, *after):
    width, hidden = weights[4].shape
    part = hidden // 2
    tiles = part // TILE
    tile = (BLOCK, TILE)
    heads = width // HEAD
    return pl.pallas_call(
        forward_kernel,
        in_specs=[SMEM] + [VMEM] * 4 + [HBM] * 6 + [ANY] * len(after),
        out_specs=[HBM] * 5 + [VMEM] * 6,
        out_shape=[
            struct((BLOCK, width), bf16),
            struct((BLOCK, 3 * width), bf16),
            struct((heads, BLOCK, BLOCK), bf16),
            struct((tiles, *tile), bf16),
            struct((BLOCK, width), f32),
            struct((3, BLOCK, width), bf16),
            struct((1 + tiles, *tile), bf16),
            struct((tiles, *tile), bf16),
            struct((tiles, *tile), bf16),
            struct((heads + -heads % 8, BLOCK), f32),
            struct((2, part), f32),
        ],
        scratch_shapes=[
            pltpu.VMEM((width, width), bf16),
            pltpu.VMEM((width, width), bf16),
            pltpu.VMEM((width, 3 * width), bf16),
            pltpu.VMEM((width, width), bf16),
            pltpu.VMEM((2, width, part), bf16),
            pltpu.VMEM((2, BLOCK, part), bf16),
            pltpu.VMEM((rows.shape[1] + -rows.shape[1] % 16, width), bf16),
            pltpu.VMEM((BLOCK, width), bf16),
            pltpu.VMEM((BLOCK, 3 * width), bf16),
            pltpu.VMEM((width, BLOCK), bf16),
            pltpu.VMEM((heads, BLOCK, BLOCK), bf16),
            pltpu.VMEM((tiles, *tile), bf16),
            pltpu.VMEM((BLOCK, width), f32),
            pltpu.VMEM((2, tiles, *tile), bf16),
            pltpu.SemaphoreType.DMA((8,)),
            pltpu.SemaphoreType.DMA((3,)),
            pltpu.SemaphoreType.DMA((heads // 2 // TOGETHER,)),
            pltpu.SemaphoreType.DMA((tiles,)),
        ],
        compiler_params=params(50),
        cost_estimate=cost(23),
        name="forward",
    )(spots, rows, incoming, vectors, b_up, *weights, *after)


class Split:
    def __init__(self, blocks, rows, cols, wide, bit):
        low, high = (rows // wide) << bit, wide >> (bit + 1)
        self.bit, self.whole = bit, low % 16 != 0
        self.full = (blocks, rows, cols)
        self.scratch = self.full if self.whole else (blocks, high, 2, low, cols)
        self.half = (blocks, high, low, cols)
        shapes = [self.full] if self.whole else [self.half, self.half]
        self.outs = [struct(shape, bf16) for shape in shapes]

    def buffer(self):
        return pltpu.VMEM(self.scratch, bf16)

    def store(self, buffer, block, value):
        buffer[block] = value.astype(bf16).reshape(self.scratch[1:])

    def flush(self, group, place, buffer, outs, sems, blocks=slice(None)):
        if self.whole:
            start_copy(group, buffer, outs[0], sems.at[0])
            return
        mine = lax.rem(lax.div(place, 1 << self.bit), 2)
        start_copy(group, buffer.at[:, :, 1 - mine], outs[0], sems.at[0])
        start_copy(group, buffer.at[:, :, mine], outs[1], sems.at[1])

    def halves(self, outs):
        if not self.whole:
            return outs
        blocks, rows, cols = self.full
        part = outs[0].reshape(blocks, self.half[1], 2, self.half[2], cols)
        mine = (lax.axis_index("wide") >> self.bit) & 1
        return [lax.dynamic_index_in_dim(part, t, 2, keepdims=False) for t in (1 - mine, mine)]


def up_grad_kernel(split, spots, late, late_got, du_own, *rest):
    lhs, rhs, buffer, in_sem, out_sem = rest[-5:]
    outs = rest[-5 - len(split.outs) : -5]
    tiles = du_own.shape[0]
    per = TILE // 128
    waits, stores = [], []
    first, second = pl.ds(0, BLOCK), pl.ds(BLOCK, BLOCK)
    start_copy(waits, late.at[0], lhs.at[first], in_sem.at[0])
    start_copy(waits, late_got.at[0], lhs.at[second], in_sem.at[1])
    for j in range(tiles):
        start_copy(waits, du_own.at[j], rhs.at[j, first], in_sem.at[2 + 2 * j])
        start_copy(waits, late_got.at[1 + j], rhs.at[j, second], in_sem.at[3 + 2 * j])
    waits[0].wait()
    waits[1].wait()
    for j in range(tiles):
        waits[2 + 2 * j].wait()
        waits[3 + 2 * j].wait()
        value = dot(lhs[...], rhs[j], TN)
        for block in range(per):
            split.store(buffer, j * per + block, value[:, block * 128 : (block + 1) * 128])
        blocks = pl.ds(j * per, per)
        here = [out.at[blocks] for out in outs]
        split.flush(stores, spots[9], buffer.at[blocks], here, out_sem.at[j])
    wait_all(stores)


def up_grad(spots, late, late_got, du_own, wide, bit, *after):
    tiles, width = du_own.shape[0], late.shape[2]
    split = Split(tiles * TILE // 128, width, 128, wide, bit)
    outs = pl.pallas_call(
        partial(up_grad_kernel, split),
        in_specs=[SMEM] + [ANY] * 3 + [ANY] * len(after),
        out_specs=[HBM] * len(split.outs),
        out_shape=split.outs,
        scratch_shapes=[
            pltpu.VMEM((2 * BLOCK, width), bf16),
            pltpu.VMEM((tiles, 2 * BLOCK, TILE), bf16),
            split.buffer(),
            pltpu.SemaphoreType.DMA((2 + 2 * tiles,)),
            pltpu.SemaphoreType.DMA((tiles, 2)),
        ],
        compiler_params=params(20),
        cost_estimate=cost(5.7),
        name="up_grad",
    )(spots, late, late_got, du_own, *after)
    return split.halves(outs)


def down_grad_kernel(split, spots, cot_in, dy_got, g_low, g_high, got_low, got_high, *rest):
    lhs, rhs, cot, buffer, in_sem, out_sem = rest[-6:]
    outs = rest[-6 - len(split.outs) : -6]
    per, half = g_low.shape[0], dy_got.shape[1]
    tiles = 2 * per
    waits, stores = [], []
    first, second = pl.ds(0, BLOCK), pl.ds(BLOCK, BLOCK)
    for j in range(tiles):
        g, got = (g_low, got_low) if j < per else (g_high, got_high)
        start_copy(waits, g.at[j % per], lhs.at[j, first], in_sem.at[2 * j])
        start_copy(waits, got.at[j % per], lhs.at[j, second], in_sem.at[2 * j + 1])
        if j == 0:
            start_copy(waits, cot_in.at[0, :, columns(spots[7], half)], cot, in_sem.at[2 * tiles])
            start_copy(waits, dy_got, rhs.at[second], in_sem.at[2 * tiles + 1])
    live = row_ids((BLOCK, 1)) < spots[6]
    head, waits = waits[:4], waits[:2] + waits[4:]
    head[2].wait()
    head[3].wait()
    rhs[first] = jnp.where(live, cot[...], jnp.zeros_like(cot))
    mine = lax.rem(lax.div(spots[9], 1 << split.bit), 2)
    count = split.scratch[1] // tiles
    at_rows = [pl.ds(j * count, count) for j in range(tiles)]
    for j in range(tiles):
        waits[2 * j].wait()
        waits[2 * j + 1].wait()
        value = dot(lhs[j], rhs[...], TN).astype(bf16)
        for block in range(half // 128):
            piece = value[:, block * 128 : (block + 1) * 128]
            if split.whole:
                buffer[block, j * TILE : (j + 1) * TILE] = piece
            else:
                buffer[block, at_rows[j]] = piece.reshape(count, *split.scratch[2:])
        if not split.whole:
            at = at_rows[j]
            start_copy(stores, buffer.at[:, at, 1 - mine], outs[0].at[:, at], out_sem.at[0, j])
            start_copy(stores, buffer.at[:, at, mine], outs[1].at[:, at], out_sem.at[1, j])
    if split.whole:
        start_copy(stores, buffer, outs[0], out_sem.at[0, 0])
    wait_all(stores)


def down_grad(spots, cot, dy_got, g, g_got, wide, bit, *after):
    tiles, half = 2 * g[0].shape[0], dy_got.shape[1]
    split = Split(half // 128, tiles * TILE, 128, wide, bit)
    outs = pl.pallas_call(
        partial(down_grad_kernel, split),
        in_specs=[SMEM] + [ANY] * 6 + [ANY] * len(after),
        out_specs=[HBM] * len(split.outs),
        out_shape=split.outs,
        scratch_shapes=[
            pltpu.VMEM((tiles, 2 * BLOCK, TILE), bf16),
            pltpu.VMEM((2 * BLOCK, half), bf16),
            pltpu.VMEM((BLOCK, half), bf16),
            split.buffer(),
            pltpu.SemaphoreType.DMA((2 * tiles + 2,)),
            pltpu.SemaphoreType.DMA((2, tiles)),
        ],
        compiler_params=params(20),
        cost_estimate=cost(6.3),
        name="down_grad",
    )(spots, cot, dy_got, *g, *g_got, *after)
    return split.halves(outs)


def unfeed_kernel(spots, inverse, scales, d_b_down, d_b_up, cot, h, late_in, du_in, w_up_in, w_out, *rest):
    d_h, d_low, d_o, vectors, du, w_up, in_sem, du_sem = rest[-8:]
    width, hidden = w_up_in.shape
    part = hidden // 2
    tiles = part // TILE
    core = spots[7]
    waits, du_waits = [], []
    for s, side in enumerate((1 - core, core)):
        source = late_in.at[pl.ds(1, tiles)] if s == 0 else du_in
        start_copy(du_waits, source, du.at[s], du_sem.at[s])
        for j in range(tiles):
            place = pl.ds(pl.multiple_of(side * part + j * TILE, 128), TILE)
            start_copy(waits, w_up_in.at[:, place], w_up.at[s, j], in_sem.at[s * tiles + j])
    d_m = None
    for s in range(2):
        du_waits[s].wait()
        for j in range(tiles):
            waits[s * tiles + j].wait()
            term = dot(du[s, j], w_up[s, j], NT)
            d_m = term if d_m is None else d_m + term
    normed, factor = norm_stats(h[...])
    vectors[...] = jnp.zeros_like(vectors)
    vectors[8:9] = jnp.sum(d_m * normed, axis=0, keepdims=True)
    vectors[9:10] = jnp.sum(d_m, axis=0, keepdims=True)
    vectors[10:11] = d_b_down[...]
    for j in range(4):
        vectors[11 + j : 12 + j] = d_b_up[j // 2 : j // 2 + 1, j % 2 * width : (j % 2 + 1) * width]
    live = row_ids((BLOCK, 1)) < spots[6]
    kept_cot = jnp.where(live, cot[0].astype(f32), 0.0)
    d_h[...] = kept_cot + norm_back(d_m * pick(scales, 8), normed, factor)
    low = d_h[...].astype(bf16)
    d_low[...] = low
    vectors[7:8] = jnp.sum(low.astype(f32), axis=0, keepdims=True)
    heads = inverse.shape[0]
    lane = lax.broadcasted_iota(jnp.int32, (heads, width), 1)
    spread = jnp.where(lax.div(lane, HEAD) == row_ids((heads, width)), 1.0, 0.0)
    scale = lax.dot_general(
        inverse[...], spread, TN, precision=lax.Precision.HIGHEST, preferred_element_type=f32
    )
    d_o[...] = (dot(low, w_out[...], NT) * scale).astype(bf16)


def unfeed(spots, inverse, scales, d_b_down, d_b_up, cot, h, late, du_own, w_up, w_out, *after):
    width, hidden = w_up.shape
    tiles = hidden // 2 // TILE
    return pl.pallas_call(
        unfeed_kernel,
        in_specs=[SMEM] + [VMEM] * 6 + [ANY] * 3 + [VMEM] + [ANY] * len(after),
        out_specs=[VMEM] * 4,
        out_shape=[
            struct((BLOCK, width), f32),
            struct((BLOCK, width), bf16),
            struct((BLOCK, width), bf16),
            struct((16, width), f32),
        ],
        scratch_shapes=[
            pltpu.VMEM((2, tiles, BLOCK, TILE), bf16),
            pltpu.VMEM((2, tiles, width, TILE), bf16),
            pltpu.SemaphoreType.DMA((2 * tiles,)),
            pltpu.SemaphoreType.DMA((2,)),
        ],
        compiler_params=params(28),
        cost_estimate=cost(6.4),
        name="unfeed",
    )(spots, inverse, scales, d_b_down, d_b_up, cot, h, late, du_own, w_up, w_out, *after)


def attend_back(qkv, d_o, inverse, weights, ds_t, d_qkv, sums, waits):
    width = d_o.shape[1]
    group = 2 * TOGETHER
    lane = lax.broadcasted_iota(jnp.int32, (BLOCK, 128), 1)
    for first in range(0, width // HEAD, group):
        waits[first // group].wait()
        work = []
        for head in range(first, first + group):
            at = head // 2 * 128
            values, up = qkv[:, 2 * width + at : 2 * width + at + 128], d_o[:, at : at + 128]
            own = (lane < HEAD) if head % 2 == 0 else (lane >= HEAD)
            work.append(dot(jnp.where(own, values, jnp.zeros_like(values)), up, NT))
        grads = []
        for head, g_t in zip(range(first, first + group), work):
            at = head // 2 * 128
            q, keys = qkv[:, at : at + 128], qkv[:, width + at : width + at + 128]
            e = weights[head].astype(f32)
            inner = e * g_t
            total = jnp.sum(inner, axis=0, keepdims=True) * inverse[head : head + 1]
            ds_t[head - first] = (inner - e * total).astype(bf16)
            k_t = keys.T[head % 2 * HEAD : (head % 2 + 1) * HEAD]
            grads.append(
                (
                    dot(k_t, ds_t[head - first]),
                    dot(ds_t[head - first], q),
                    dot(weights[head], d_o[:, at : at + 128]),
                )
            )
        for k in range(TOGETHER):
            one, two = grads[2 * k], grads[2 * k + 1]
            at = (first // 2 + k) * 128
            dq = (jnp.concatenate([one[0], two[0]], axis=0) * 0.125).T.astype(bf16)
            dk = jnp.where(lane < HEAD, one[1], two[1]).astype(bf16)
            dv = jnp.where(lane < HEAD, one[2], two[2]).astype(bf16)
            d_qkv[:, at : at + 128] = dq
            d_qkv[:, width + at : width + at + 128] = dk
            d_qkv[:, 2 * width + at : 2 * width + at + 128] = dv
            sums[5:6, at : at + 128] = jnp.sum(dq.astype(f32), axis=0, keepdims=True)
            sums[6:7, at : at + 128] = jnp.sum(dv.astype(f32), axis=0, keepdims=True)


def back_kernel(
    spots, inverse, scales, before, d_h, d_low, d_o, w_qkv_in, w_img_in, w_txt_in, qkv_in, kept, x_in,
    *rest
):
    (
        sent_a, sent_b, sent_c, mine, own_rows, window, vectors,
        w_qkv, w_img, w_txt, qkv, weights, x, d_qkv, ds_t, d_proj, in_sem, kept_sem, out_sem,
    ) = rest[-19:]
    width = w_img_in.shape[0]
    half, wide = width // 2, 3 * width // 2
    core = spots[7]
    other = 1 - core
    group = 2 * TOGETHER
    waits, kept_waits, stores = [], [], []
    start_copy(waits, qkv_in, qkv, in_sem.at[0])
    for first in range(0, width // HEAD, group):
        heads = pl.ds(first, group)
        start_copy(kept_waits, kept.at[heads], weights.at[heads], kept_sem.at[first // group])
    for k, (source, target) in enumerate(
        ((x_in, x), (w_qkv_in, w_qkv), (w_img_in, w_img), (w_txt_in, w_txt))
    ):
        start_copy(waits, source, target, in_sem.at[1 + k])
    vectors[...] = before[...]
    third = sent_a.shape[1]
    rest_q = wide - third
    low = d_low[...]
    low_sides = low[:, :half], low[:, half:]

    def sides(pair):
        return jnp.where(core == 0, pair[0], pair[1]), jnp.where(core == 0, pair[1], pair[0])

    own, theirs = sides(low_sides)
    sent_b[:, rest_q:] = theirs[:, :128]
    sent_c[:, : half - 128] = theirs[:, 128:]
    mine[:, wide : wide + half] = own
    waits[0].wait()
    attend_back(qkv, d_o, inverse, weights, ds_t, d_qkv, vectors, kept_waits)
    own, theirs = sides((d_qkv[:, :wide], d_qkv[:, wide:]))
    sent_a[...] = theirs[:, :third]
    sent_b[:, :rest_q] = theirs[:, third:]
    mine[:, :wide] = own

    waits[1].wait()
    waits[2].wait()
    normed, factor = norm_stats(x[...].astype(f32))
    d_a = dot(d_qkv[...], w_qkv[...], NT)
    d_x = d_h[...] + norm_back(d_a * pick(scales, 3), normed, factor)
    at = row_ids((BLOCK, 1))
    is_image = (at >= 1) & (at < 1 + PATCHES)
    is_text = (at >= 1 + PATCHES) & (at < spots[6])
    image = jnp.where(is_image, d_x, 0.0).astype(bf16)
    text = jnp.where(is_text, d_x, 0.0).astype(bf16)
    both = jnp.where(is_image, image, text)
    own, theirs = sides((both[:, :half], both[:, half:]))
    sent_c[:, half - 128 :] = theirs
    mine[:, wide + half :] = own
    vectors[0:1] = d_x[0:1]
    vectors[1:2] = jnp.sum(image.astype(f32), axis=0, keepdims=True)
    vectors[2:3] = jnp.sum(text.astype(f32), axis=0, keepdims=True)
    vectors[3:4] = jnp.sum(d_a * normed, axis=0, keepdims=True)
    vectors[4:5] = jnp.sum(d_a, axis=0, keepdims=True)

    waits[3].wait()
    waits[4].wait()
    rows = dot(image[:256], w_img[...], NT)
    low = dot(text, w_txt[...], NT)
    rows = jnp.concatenate([rows + low[:256], low[256:]], axis=0).astype(bf16)

    def placer(count, low, high, shift):
        at = lax.broadcasted_iota(jnp.int32, (count, BLOCK), 1)
        spot = row_ids((count, BLOCK))
        hit = (spot == at + shift) & (at >= low) & (at < high)
        return jnp.where(hit, 1.0, 0.0).astype(bf16)

    window[...] = dot(placer(window.shape[0], spots[3], spots[4], spots[5]), rows).astype(bf16)
    own_rows[...] = dot(placer(own_rows.shape[0], spots[0], spots[1], spots[2]), rows).astype(bf16)


def back(spots, inverse, scales, before, d_h, d_low, d_o, w_qkv, w_img, w_txt, qkv, kept, x, span, *after):
    width = w_img.shape[0]
    heads = width // HEAD
    packed = 5 * width // 2
    return pl.pallas_call(
        back_kernel,
        in_specs=[SMEM] + [VMEM] * 6 + [ANY] * (6 + len(after)),
        out_specs=[VMEM] * 7,
        out_shape=[
            struct((BLOCK, packed // 3), bf16),
            struct((BLOCK, packed // 3), bf16),
            struct((BLOCK, packed // 3), bf16),
            struct((BLOCK, packed), bf16),
            struct((span, width), bf16),
            struct((WINDOW, width), bf16),
            struct((16, width), f32),
        ],
        scratch_shapes=[
            pltpu.VMEM((width, 3 * width), bf16),
            pltpu.VMEM((width, width), bf16),
            pltpu.VMEM((width, width), bf16),
            pltpu.VMEM((BLOCK, 3 * width), bf16),
            pltpu.VMEM((heads, BLOCK, BLOCK), bf16),
            pltpu.VMEM((BLOCK, width), bf16),
            pltpu.VMEM((BLOCK, 3 * width), bf16),
            pltpu.VMEM((2 * TOGETHER, BLOCK, BLOCK), bf16),
            pltpu.VMEM((BLOCK, width), bf16),
            pltpu.SemaphoreType.DMA((5,)),
            pltpu.SemaphoreType.DMA((heads // 2 // TOGETHER,)),
            pltpu.SemaphoreType.DMA((9,)),
        ],
        compiler_params=params(44),
        cost_estimate=cost(18),
        name="back",
    )(spots, inverse, scales, before, d_h, d_low, d_o, w_qkv, w_img, w_txt, qkv, kept, x, *after)


def late_grads_kernel(splits, spots, vectors, early_in, early_got, mine, got_a, got_b, got_c, *rest):
    count = sum(len(split.outs) for split in splits)
    outs = rest[-(count + len(splits) + 4) : -(len(splits) + 4)]
    buffers = rest[-(len(splits) + 4) : -4]
    early, rhs, in_sem, out_sem = rest[-4:]
    width = early_in.shape[2]
    half, wide = width // 2, 3 * width // 2
    first, second = pl.ds(0, BLOCK), pl.ds(BLOCK, BLOCK)
    waits, stores = [], []
    start_copy(waits, early_in.at[1], early.at[1, first], in_sem.at[2])
    start_copy(waits, early_got.at[1], early.at[1, second], in_sem.at[3])
    start_copy(waits, mine, rhs.at[first], in_sem.at[0])
    third = got_a.shape[1]
    start_copy(waits, got_a, rhs.at[second, pl.ds(0, third)], in_sem.at[1])
    start_copy(waits, got_b, rhs.at[second, pl.ds(third, third)], in_sem.at[9])
    start_copy(waits, got_c, rhs.at[second, pl.ds(2 * third, third)], in_sem.at[10])
    for k in (2, 0):
        start_copy(waits, early_in.at[k], early.at[k, first], in_sem.at[4 + k])
        start_copy(waits, early_got.at[k], early.at[k, second], in_sem.at[5 + k])

    filled = [0, 0]
    place = [0]

    def put(value):
        for j in range(value.shape[1] // 128):
            split, buffer = splits[filled[0]], buffers[filled[0]]
            split.store(buffer, filled[1], value[:, j * 128 : (j + 1) * 128])
            filled[1] += 1
            if filled[1] == split.full[0]:
                n = len(split.outs)
                sems = out_sem.at[filled[0]]
                split.flush(stores, spots[9], buffer, outs[place[0] : place[0] + n], sems)
                filled[0], filled[1], place[0] = filled[0] + 1, 0, place[0] + n

    for k in range(6):
        waits[k].wait()
    for j in range(3):
        put(dot(early[1], rhs[:, j * half : (j + 1) * half], TN))
    waits[6].wait()
    waits[7].wait()
    put(dot(early[2], rhs[:, wide : 2 * width], TN))
    waits[8].wait()
    waits[9].wait()
    at = row_ids((2 * BLOCK, 1))
    is_image = lax.rem(at, BLOCK) < 1 + PATCHES
    d_both = rhs[:, 2 * width :]
    zeros = jnp.zeros_like(d_both)
    image = jnp.where(is_image, d_both, zeros)
    raw = early[0]
    short = [jnp.concatenate([t[:256], t[BLOCK : BLOCK + 256]], axis=0) for t in (raw, image)]
    put(dot(short[0], short[1], TN))
    put(dot(raw, jnp.where(is_image, zeros, d_both), TN))
    side = pl.ds(pl.multiple_of(spots[7] * 8, 8), 8)
    put(jnp.concatenate([vectors[side], jnp.zeros((120, width), f32)], axis=0).T)
    wait_all(stores)


def late_grads(spots, vectors, early, early_got, mine, got, wide, parts, *after):
    width = early.shape[2]
    splits = [Split(blocks, width, 128, wide, bit) for blocks, bit in parts]
    shapes = [out for split in splits for out in split.outs]
    outs = pl.pallas_call(
        partial(late_grads_kernel, splits),
        in_specs=[SMEM, VMEM] + [ANY] * 6 + [ANY] * len(after),
        out_specs=[HBM] * len(shapes),
        out_shape=shapes,
        scratch_shapes=[split.buffer() for split in splits]
        + [
            pltpu.VMEM((3, 2 * BLOCK, width), bf16),
            pltpu.VMEM((2 * BLOCK, 5 * width // 2), bf16),
            pltpu.SemaphoreType.DMA((11,)),
            pltpu.SemaphoreType.DMA((len(splits), 2)),
        ],
        compiler_params=params(32),
        cost_estimate=cost(8),
        name="late_grads",
    )(spots, vectors, early, early_got, mine, *got, *after)
    pairs, low = [], 0
    for split in splits:
        pairs.append(split.halves(outs[low : low + len(split.outs)]))
        low += len(split.outs)
    return pairs


def result_kernel(spots, b_down, g_low, g_high, w_down_in, h_in, *rest):
    out, g, w_down, h, sem = rest[-5:]
    tiles = g.shape[0]
    waits = []
    for j in range(tiles):
        part = g_low if j < tiles // 2 else g_high
        start_copy(waits, part.at[j % (tiles // 2)], g.at[j], sem.at[2 * j])
        start_copy(waits, w_down_in.at[pl.ds(j * TILE, TILE)], w_down.at[j], sem.at[2 * j + 1])
    start_copy(waits, h_in, h, sem.at[2 * tiles])
    live = row_ids((BLOCK, 1)) < spots[6]
    value = None
    for j in range(tiles):
        waits[2 * j].wait()
        waits[2 * j + 1].wait()
        term = dot(g[j], w_down[j])
        value = term if value is None else value + term
    waits[2 * tiles].wait()
    out[...] = jnp.where(live, value + h[...] + row(b_down), 0.0).astype(bf16)


def result(spots, g, w_down, h, b_down, *after):
    tiles, width = 2 * g[0].shape[0], h.shape[1]
    return pl.pallas_call(
        result_kernel,
        in_specs=[SMEM, VMEM] + [ANY] * 4 + [ANY] * len(after),
        out_specs=VMEM,
        out_shape=struct(h.shape, bf16),
        scratch_shapes=[
            pltpu.VMEM((tiles, *g[0].shape[1:]), bf16),
            pltpu.VMEM((tiles, TILE, width), bf16),
            pltpu.VMEM(h.shape, f32),
            pltpu.SemaphoreType.DMA((2 * tiles + 1,)),
        ],
        compiler_params=params(20),
        cost_estimate=cost(6),
        name="result",
    )(spots, b_down, *g, w_down, h, *after)


def round_kernel(steps, spots, *refs):
    count = len(steps)
    keeps, gots, outs = refs[:count], refs[count : 2 * count], refs[len(refs) - 2 * count :]
    for k, bit in enumerate(steps):
        mine = lax.rem(lax.div(spots[9], 1 << bit), 2)
        for side, target in ((1 - mine, outs[2 * k]), (mine, outs[2 * k + 1])):
            at = (slice(None), pl.ds(side, 1))
            value = keeps[k][at].astype(f32) + gots[k][at].astype(f32)
            target[...] = value.reshape(target.shape).astype(bf16)


class Chain:
    def __init__(self, halves, order, share, wide):
        self.bits, self.order, self.share = wide.bit_length() - 1, order, share
        send, keep = halves
        self.blocks = keep.shape[0]
        self.wide = wide
        self.left = set(range(self.bits)) - {order[0]}
        self.keep, self.got = keep, swap(send, "wide", order[0])
        self.order = order[1:]

    def view(self, value):
        bit = self.order[0]
        below = sum(other < bit for other in self.left)
        above = len(self.left) - 1 - below
        return value.reshape(self.blocks << above, 2, self.share << below, 128)


def advance(spots, chains, *after):
    keeps = [chain.view(chain.keep) for chain in chains]
    gots = [chain.view(chain.got) for chain in chains]
    steps = [chain.order[0] for chain in chains]
    shapes = [(keep.shape[0], keep.shape[2], 128) for keep in keeps]
    if any(chain.share % 16 for chain in chains):
        outs = []
        for keep, got, bit in zip(keeps, gots, steps):
            part = add_low(keep, got)
            mine = (lax.axis_index("wide") >> bit) & 1
            outs += [lax.dynamic_index_in_dim(part, t, 1, keepdims=False) for t in (1 - mine, mine)]
    else:
        outs = pl.pallas_call(
            partial(round_kernel, steps),
            in_specs=[SMEM] + [VMEM] * (2 * len(chains)) + [ANY] * len(after),
            out_specs=[VMEM] * (2 * len(chains)),
            out_shape=[struct(shape, bf16) for shape in shapes for _ in range(2)],
            compiler_params=params(16),
            cost_estimate=cost(60),
            name="round",
        )(spots, *keeps, *gots, *after)
    for k, chain in enumerate(chains):
        bit = chain.order[0]
        chain.left = chain.left - {bit}
        chain.order = chain.order[1:]
        chain.keep, chain.got = outs[2 * k + 1], swap(outs[2 * k], "wide", bit)
    return chains[-1].keep


def total(chain):
    return add_low(chain.keep, chain.got).reshape(chain.blocks, chain.share, 128)


def unpack_kernel(spots, *refs):
    count = 2 + PARTS
    own, other, outs = refs[:count], refs[count : 2 * count], refs[2 * count :]
    first_core = spots[7] == 0

    def both(k):
        one, two = own[k][...], other[k][...]
        return jnp.where(first_core, one, two).astype(f32), jnp.where(first_core, two, one).astype(f32)

    down, up, qkv, out, img, txt = outs[:6]

    def pieces(*parts):
        blocks = []
        for k in parts:
            left, right = both(k)
            blocks += [(left[j], right[j]) for j in range(left.shape[0])]
        return blocks

    def spread(target, blocks):
        count = len(blocks)
        for j, (left, right) in enumerate(blocks):
            target[:, j * 128 : (j + 1) * 128] = left
            target[:, (count + j) * 128 : (count + j + 1) * 128] = right

    spread(down, pieces(0))
    spread(up, pieces(1))
    blocks = pieces(*range(2, count))
    per = out.shape[1] // 256
    spread(qkv, blocks[: 3 * per])
    spread(out, blocks[3 * per : 4 * per])
    spread(img, blocks[4 * per : 5 * per])
    spread(txt, blocks[5 * per : 6 * per])

    left, right = blocks[6 * per]
    rows = jnp.concatenate([left.T[:8], right.T[:8]], axis=0)
    for k in range(11):
        outs[6 + k][...] = rows[k]
    outs[17][...] = rows[11:15]


def unpack(spots, own, other):
    share, width = own[0].shape[1] // 4, own[0].shape[0] * 256
    shapes = [(4 * share, width), (share, 4 * width), (share, 3 * width)] + [(share, width)] * 3
    shapes += [(share,)] * 11 + [(4, share)]
    return pl.pallas_call(
        unpack_kernel,
        in_specs=[SMEM] + [VMEM] * (2 * len(own)),
        out_specs=[VMEM] * len(shapes),
        out_shape=[struct(shape, f32) for shape in shapes],
        compiler_params=params(32),
        cost_estimate=cost(2),
        name="unpack",
    )(spots, *own, *other)


def swap(x, axis, bit):
    count = lax.axis_size(axis)
    route = [(i, i ^ (1 << bit)) for i in range(count)]
    return lax.ppermute(x, axis, route)


def add_low(one, two):
    f32 = jnp.float32
    return (one.astype(f32) + two.astype(f32)).astype(jnp.bfloat16)


def behind(value, *after):
    return lax.optimization_barrier((value, *after))[0] if after else value


def on_device(
    tower_states,
    caption_lengths,
    assignment,
    cls_token,
    w_img,
    b_img,
    w_txt,
    b_txt,
    gain_one,
    bias_one,
    w_qkv,
    b_query,
    b_value,
    w_out,
    b_out,
    gain_two,
    bias_two,
    w_up,
    b_up,
    w_down,
    b_down,
    cotangent,
):
    wide = lax.axis_size("wide")
    rows = tower_states[0]
    span, width = rows.shape
    bits = wide.bit_length() - 1
    payload, spots = opening(caption_lengths, assignment, tower_states)
    incoming = swap(payload, "wide", bits - 1)
    cot = cotangent[0]
    grad, d_b_down, dy_other = hidden_grad(spots, cot, w_down)
    dy_got = swap(dy_other, "dp", 0)
    vectors = jnp.stack(
        [cls_token, b_img, b_txt, gain_one, bias_one, b_query, b_value, b_out, gain_two, bias_two]
    )
    share, tail = width // wide, list(range(3, bits))

    def order(*first):
        return list(first) + tail

    x, qkv, kept, du_own, h, early, late, *g, inverse, d_b_up = forward(
        spots, tower_states, incoming, vectors, b_up, (w_img, w_txt, w_qkv, w_out, w_up, grad), dy_got
    )
    late_got = swap(late, "dp", 0)
    g_got = [swap(t, "dp", 0) for t in g]
    early_got = swap(early, "dp", 0)
    d_h, d_low, d_o, before = unfeed(
        spots, inverse, vectors, d_b_down, d_b_up, cotangent, h, late, du_own, w_up, w_out
    )
    up = up_grad(spots, late, late_got, du_own, wide, 1, d_o)
    down = down_grad(spots, cotangent, dy_got, g, g_got, wide, 0, up[1])
    down = Chain(down, order(0, 1, 2), 4 * share, wide)
    up = Chain(up, order(1, 0, 2), share, wide)
    *sent, mine, own_rows, window, own_vectors = back(
        spots, inverse, vectors, before, d_h, d_low, d_o, w_qkv, w_img, w_txt, qkv, kept, x, span,
        down.keep, early_got,
    )
    got = [swap(t, "dp", 0) for t in sent]
    step = advance(spots, [down, up], mine)
    returned = swap(window, "wide", bits - 1)
    every = own_vectors + swap(own_vectors, "dp", 0)
    tall = every[11:15].reshape(wide, 4, share).swapaxes(0, 1).reshape(4, width)
    every = jnp.concatenate([every[:11], tall, every[15:]], axis=0)
    parts = [(6, order(0, 1, 2)), (6, order(1, 0, 2)), (7, order(2, 1, 0))]
    lasts = late_grads(
        spots, every, early, early_got, mine, got, wide,
        [(blocks, t[0]) for blocks, t in parts], step,
    )
    lasts = [Chain(halves, t, share, wide) for halves, (_, t) in zip(lasts, parts)]
    out = result(spots, g, w_down, h, b_down, lasts[0].keep)
    chains = [down, up] + lasts
    step = advance(spots, chains[:2], out, returned)
    step = advance(spots, lasts, step)
    while any(t.order for t in chains):
        step = advance(spots, [t for t in chains if t.order], step)
    own = [total(t) for t in chains]
    joined = jnp.concatenate([t.reshape(-1, 128) for t in own], axis=0)
    other = swap(joined, "dp", 0)
    pieces, low = [], 0
    for t in own:
        high = low + t.size // 128
        pieces.append(other[low:high].reshape(t.shape))
        low = high
    results = unpack(spots, own, pieces)
    down, up, d_w_qkv, d_w_out, d_w_img, d_w_txt = results[:6]
    vectors, d_b_up = results[6:17], results[17].reshape(-1)
    (
        d_cls,
        d_b_img,
        d_b_txt,
        d_gain_one,
        d_bias_one,
        d_b_query,
        d_b_value,
        d_b_out,
        d_gain_two,
        d_bias_two,
        d_b_down,
    ) = vectors
    gap = span - WINDOW
    gap_low = jnp.pad(returned, ((0, gap), (0, 0)))
    gap_high = jnp.pad(returned, ((gap, 0), (0, 0)))
    d_rows = own_rows + jnp.where(spots[8] == 0, gap_low, gap_high)
    return (
        out[None],
        d_rows[None],
        d_cls,
        d_w_img,
        d_b_img,
        d_w_txt,
        d_b_txt,
        d_gain_one,
        d_bias_one,
        d_w_qkv,
        d_b_query,
        d_b_value,
        d_w_out,
        d_b_out,
        d_gain_two,
        d_bias_two,
        up,
        d_b_up,
        down,
        d_b_down,
    )


def solution(mesh):
    placed = (
        P("dp", "wide", None),
        P("dp", None, None),
        P("dp", None, None),
        P(),
        P(),
        P(),
        P(),
        P(),
        P(),
        P(),
        P(),
        P(),
        P(),
        P(),
        P(),
        P(),
        P(),
        P(),
        P(),
        P(),
        P(),
        P("dp", "wide", None),
    )
    return jax.shard_map(
        on_device,
        mesh=mesh,
        in_specs=placed,
        out_specs=(
            P("dp", "wide", None),
            P("dp", "wide", None),
            P("wide"),
            P("wide", None),
            P("wide"),
            P("wide", None),
            P("wide"),
            P("wide"),
            P("wide"),
            P("wide", None),
            P("wide"),
            P("wide"),
            P("wide", None),
            P("wide"),
            P("wide"),
            P("wide"),
            P("wide", None),
            P("wide"),
            P("wide", None),
            P("wide"),
        ),
        check_vma=False,
    )
```

```python
from functools import partial
import math
import jax
import jax.numpy as jnp
from jax import lax
from jax.experimental import pallas as pl
from jax.experimental.pallas import tpu as pltpu
from jax.sharding import PartitionSpec as P

HEAD = 64
PATCHES = 197
BLOCK = 512
WINDOW = 320
TILE = 768
TOGETHER = 2
bf16 = jnp.bfloat16
f32 = jnp.float32
VMEM = pl.BlockSpec(memory_space=pltpu.VMEM)
SMEM = pl.BlockSpec(memory_space=pltpu.SMEM)
ANY = pl.BlockSpec(memory_space=pl.ANY)
HBM = pl.BlockSpec(memory_space=pltpu.HBM)
NN = (((1,), (0,)), ((), ()))
NT = (((1,), (1,)), ((), ()))
TN = (((0,), (0,)), ((), ()))


def dot(left, right, dims=NN):
    return lax.dot_general(left, right, dims, preferred_element_type=f32)


def params(mib, **more):
    return pltpu.CompilerParams(vmem_limit_bytes=mib << 20, **more)


def start_copy(group, source, target, sem):
    copy = pltpu.make_async_copy(source, target, sem)
    copy.start()
    group.append(copy)


def wait_all(group):
    for copy in group:
        copy.wait()


def columns(side, size):
    return pl.ds(pl.multiple_of(side * size, 128), size)


def cost(microseconds):
    flops = int(microseconds * 1153000000)
    return pl.CostEstimate(flops=flops, bytes_accessed=1024, transcendentals=0)


def struct(shape, dtype):
    return jax.ShapeDtypeStruct(shape, dtype)


def row(vector):
    return vector[...].astype(f32).reshape(1, -1)


def pick(vectors, k):
    return vectors[k : k + 1].astype(f32)


def row_ids(shape):
    return lax.broadcasted_iota(jnp.int32, shape, 0)


def norm_stats(rows):
    mean = jnp.mean(rows, axis=-1, keepdims=True)
    centred = rows - mean
    factor = lax.rsqrt(jnp.mean(centred * centred, axis=-1, keepdims=True) + 1e-05)
    return centred * factor, factor


def norm_back(scaled, normed, factor):
    return factor * (
        scaled
        - jnp.mean(scaled, axis=-1, keepdims=True)
        - normed * jnp.mean(scaled * normed, axis=-1, keepdims=True)
    )


def open_kernel(tables, rows, payload, spots):
    place, core = lax.axis_index("wide"), lax.axis_index("dp")
    half = lax.axis_size("wide") // 2
    upper = place >= half
    pair = lax.rem(place, half)

    def entry(table, column):
        value = tables[table]
        hit = (row_ids(value.shape) == pair) & (
            lax.broadcasted_iota(jnp.int32, value.shape, 1) == column
        )
        return jnp.sum(jnp.where(hit, value, 0))

    span = rows.shape[1]
    gap = span - WINDOW
    mine = entry(1, jnp.where(upper, 1, 0))
    other = 1 - mine
    first = entry(0, 0)
    begin = jnp.where(mine == 0, 0, first)
    cut = 1 + PATCHES
    count = cut + entry(0, mine)
    back = jnp.where(mine == 0, 0, gap)
    image, text = mine * PATCHES - 1, begin - cut
    spots[0] = jnp.where(upper, cut, 1)
    spots[1] = jnp.where(upper, count, cut)
    spots[2] = jnp.where(upper, text, image)
    spots[3] = jnp.where(upper, 1, cut)
    spots[4] = jnp.where(upper, cut, count)
    spots[5] = jnp.where(upper, image, text) - back
    spots[6] = count
    spots[7] = core
    spots[8] = other
    spots[9] = place
    value = rows[0]
    payload[...] = jnp.where(other == 0, value[:WINDOW], value[gap:])


def opening(lens, order, rows):
    width = rows.shape[2]
    return pl.pallas_call(
        open_kernel,
        in_specs=[VMEM, VMEM],
        out_specs=[VMEM, SMEM],
        out_shape=[struct((WINDOW, width), bf16), struct((10,), jnp.int32)],
        compiler_params=params(8),
        cost_estimate=cost(0.1),
        name="opening",
    )(jnp.concatenate([lens, order], axis=0), rows)


def hidden_grad_kernel(spots, cot, w_down, grad, d_bias, dy_other):
    live = row_ids((BLOCK, 1)) < spots[6]
    dy = jnp.where(live, cot[...], jnp.zeros_like(cot))
    grad[...] = dot(dy, w_down[...], NT).astype(bf16)

    @pl.when(pl.program_id(0) == 0)
    def _():
        d_bias[...] = jnp.sum(dy.astype(f32), axis=0, keepdims=True)
        half = dy_other.shape[1]
        dy_other[...] = jnp.where(spots[7] == 0, dy[:, half:], dy[:, :half])


def hidden_grad(spots, cot, w_down):
    hidden, width = w_down.shape
    return pl.pallas_call(
        hidden_grad_kernel,
        grid=(hidden // TILE,),
        in_specs=[
            SMEM,
            pl.BlockSpec((BLOCK, width), lambda i: (0, 0)),
            pl.BlockSpec((TILE, width), lambda i: (i, 0)),
        ],
        out_specs=[
            pl.BlockSpec((BLOCK, TILE), lambda i: (0, i)),
            pl.BlockSpec((1, width), lambda i: (0, 0)),
            pl.BlockSpec((BLOCK, width // 2), lambda i: (0, 0)),
        ],
        out_shape=[
            struct((BLOCK, hidden), bf16),
            struct((1, width), f32),
            struct((BLOCK, width // 2), bf16),
        ],
        compiler_params=params(16),
        cost_estimate=cost(0.1),
        name="hidden_grad",
    )(spots, cot, w_down)


def bias_tile(b_up, side, start):
    half = b_up.shape[0] // 2
    one, two = b_up[pl.ds(start, TILE)], b_up[pl.ds(half + start, TILE)]
    return jnp.where(side == 0, one.astype(f32), two.astype(f32)).reshape(1, -1)


def hidden_tile(m, w, b, grad, g, du):
    inner = dot(m, w) + b
    below = 0.5 + 0.5 * lax.erf(inner * math.sqrt(0.5))
    g[...] = (inner * below).astype(bf16)
    slope = below + inner * jnp.exp(-0.5 * inner * inner) * (1.0 / math.sqrt(2.0 * math.pi))
    low = (grad.astype(f32) * slope).astype(bf16)
    du[...] = low
    return jnp.sum(low.astype(f32), axis=0, keepdims=True)


def assemble(spots, rows, tower, incoming, vectors, w_img, w_txt, raw, x, waits):
    def picker(cols, low, high, shift):
        at = row_ids((BLOCK, cols))
        col = lax.broadcasted_iota(jnp.int32, (BLOCK, cols), 1)
        hit = (col == at + shift) & (at >= low) & (at < high)
        return jnp.where(hit, 1.0, 0.0).astype(bf16)

    span = rows.shape[1]
    tower[:span] = rows[0]
    tower[span:] = jnp.zeros((tower.shape[0] - span, rows.shape[2]), bf16)
    picked = dot(picker(tower.shape[0], spots[0], spots[1], spots[2]), tower[...])
    picked += dot(picker(incoming.shape[0], spots[3], spots[4], spots[5]), incoming[...])
    raw[...] = picked.astype(bf16)
    count = spots[6]
    edge, over = 192, 208
    waits[0].wait()
    image = dot(raw[:over], w_img[...]) + pick(vectors, 1)
    waits[1].wait()
    text = dot(raw[edge:], w_txt[...]) + pick(vectors, 2)
    at = row_ids((edge, 1))
    top = jnp.where(at == 0, pick(vectors, 0), image[:edge])
    at = row_ids((over - edge, 1)) + edge
    mid = jnp.where(at < 1 + PATCHES, image[edge:], text[: over - edge])
    mid = jnp.where(at < count, mid, 0.0)
    at = row_ids((BLOCK - over, 1)) + over
    low = jnp.where(at < count, text[over - edge :], 0.0)
    x[:edge] = top.astype(bf16)
    x[edge:over] = mid.astype(bf16)
    x[over:] = low.astype(bf16)


def attend(count, qkv, o_t, inverse, weights, kept, stores, sem):
    width = o_t.shape[0]
    lane = lax.broadcasted_iota(jnp.int32, (BLOCK, 128), 1)
    dead = row_ids((BLOCK, 1)) >= count
    group = 2 * TOGETHER
    for first in range(0, width // HEAD, group):
        scores = []
        for head in range(first, first + group):
            at = head // 2 * 128
            q, keys = qkv[:, at : at + 128], qkv[:, width + at : width + at + 128]
            own = (lane < HEAD) if head % 2 == 0 else (lane >= HEAD)
            scores.append(dot(jnp.where(own, keys, jnp.zeros_like(keys)), q, NT))
        for head, s_t in zip(range(first, first + group), scores):
            s_t = jnp.where(dead, -1000000000.0, s_t)
            top = jnp.max(s_t, axis=0, keepdims=True)
            e = jnp.exp(s_t - top)
            one_over = 1.0 / jnp.sum(e, axis=0, keepdims=True)
            weights[head] = e.astype(bf16)
            values = qkv[:, 2 * width + head // 2 * 128 : 2 * width + head // 2 * 128 + 128]
            v_t = values.T[head % 2 * HEAD : (head % 2 + 1) * HEAD]
            part = dot(v_t, weights[head]) * one_over
            o_t[head * HEAD : (head + 1) * HEAD] = part.astype(bf16)
            inverse[head : head + 1] = one_over
        heads = pl.ds(first, group)
        start_copy(stores, weights.at[heads], kept.at[heads], sem.at[first // group])


def forward_kernel(
    spots, rows, incoming, vectors, b_up, w_img_in, w_txt_in, w_qkv_in, w_out_in, w_up_in, grad_in,
    after,
    x_out, qkv_out, kept, du_out, h_out, early, late, g_low, g_high, inverse, d_b,
    w_img, w_txt, w_qkv, w_out, w_up, grad, tower, x, qkv, o_t, weights, du_own, h, g,
    in_sem, out_sem, kept_sem, hidden_sem,
):
    width, hidden = w_up_in.shape
    part = hidden // 2
    tiles = part // TILE
    core = spots[7]
    waits, stores = [], []
    for k, (source, target) in enumerate(
        ((w_img_in, w_img), (w_txt_in, w_txt), (w_qkv_in, w_qkv), (w_out_in, w_out))
    ):
        start_copy(waits, source, target, in_sem.at[k])
    for k, side in enumerate((1 - core, core)):
        start_copy(waits, w_up_in.at[:, columns(side, part)], w_up.at[k], in_sem.at[4 + 2 * k])
        start_copy(waits, grad_in.at[:, columns(side, part)], grad.at[k], in_sem.at[5 + 2 * k])
    raw, a = early.at[0], early.at[1]
    assemble(spots, rows, tower, incoming, vectors, w_img, w_txt, raw, x, waits)
    start_copy(stores, x, x_out, out_sem.at[0])
    normed, _ = norm_stats(x[...].astype(f32))
    a[...] = (normed * pick(vectors, 3) + pick(vectors, 4)).astype(bf16)
    waits[2].wait()
    q = dot(a[...], w_qkv[:, :width]) + pick(vectors, 5)
    qkv[:, :width] = q.astype(bf16) * jnp.asarray(0.125, bf16)
    qkv[:, width : 2 * width] = dot(a[...], w_qkv[:, width : 2 * width]).astype(bf16)
    qkv[:, 2 * width :] = (dot(a[...], w_qkv[:, 2 * width :]) + pick(vectors, 6)).astype(bf16)
    start_copy(stores, qkv, qkv_out, out_sem.at[1])
    inverse[...] = jnp.zeros_like(inverse)
    attend(spots[6], qkv, o_t, inverse, weights, kept, stores, kept_sem)
    o = o_t[...].T
    early[2] = o
    waits[3].wait()
    h[...] = x[...].astype(f32) + dot(o, w_out[...]) + pick(vectors, 7)
    start_copy(stores, h, h_out, out_sem.at[2])
    normed, _ = norm_stats(h[...])
    m = late.at[0]
    m[...] = (normed * pick(vectors, 8) + pick(vectors, 9)).astype(bf16)
    for k in range(4, 8):
        waits[k].wait()
    for k, side in enumerate((1 - core, core)):
        for j in range(tiles):
            at = pl.ds(j * TILE, TILE)
            b = bias_tile(b_up, side, j * TILE)
            target = late.at[1 + j] if k == 0 else du_own.at[j]
            sums = hidden_tile(m[...], w_up[k, :, at], b, grad[k, :, at], g.at[k, j], target)
            d_b[pl.ds(side, 1), at] = sums
            if k == 1:
                start_copy(stores, target, du_out.at[j], hidden_sem.at[j])
    core_first = core == 0
    g_low[...] = jnp.where(core_first, g[1], g[0])
    g_high[...] = jnp.where(core_first, g[0], g[1])
    wait_all(stores)


def forward(spots, rows, incoming, vectors, b_up, weights, *after):
    width, hidden = weights[4].shape
    part = hidden // 2
    tiles = part // TILE
    tile = (BLOCK, TILE)
    heads = width // HEAD
    return pl.pallas_call(
        forward_kernel,
        in_specs=[SMEM] + [VMEM] * 4 + [HBM] * 6 + [ANY] * len(after),
        out_specs=[HBM] * 5 + [VMEM] * 6,
        out_shape=[
            struct((BLOCK, width), bf16),
            struct((BLOCK, 3 * width), bf16),
            struct((heads, BLOCK, BLOCK), bf16),
            struct((tiles, *tile), bf16),
            struct((BLOCK, width), f32),
            struct((3, BLOCK, width), bf16),
            struct((1 + tiles, *tile), bf16),
            struct((tiles, *tile), bf16),
            struct((tiles, *tile), bf16),
            struct((heads + -heads % 8, BLOCK), f32),
            struct((2, part), f32),
        ],
        scratch_shapes=[
            pltpu.VMEM((width, width), bf16),
            pltpu.VMEM((width, width), bf16),
            pltpu.VMEM((width, 3 * width), bf16),
            pltpu.VMEM((width, width), bf16),
            pltpu.VMEM((2, width, part), bf16),
            pltpu.VMEM((2, BLOCK, part), bf16),
            pltpu.VMEM((rows.shape[1] + -rows.shape[1] % 16, width), bf16),
            pltpu.VMEM((BLOCK, width), bf16),
            pltpu.VMEM((BLOCK, 3 * width), bf16),
            pltpu.VMEM((width, BLOCK), bf16),
            pltpu.VMEM((heads, BLOCK, BLOCK), bf16),
            pltpu.VMEM((tiles, *tile), bf16),
            pltpu.VMEM((BLOCK, width), f32),
            pltpu.VMEM((2, tiles, *tile), bf16),
            pltpu.SemaphoreType.DMA((8,)),
            pltpu.SemaphoreType.DMA((3,)),
            pltpu.SemaphoreType.DMA((heads // 2 // TOGETHER,)),
            pltpu.SemaphoreType.DMA((tiles,)),
        ],
        compiler_params=params(50),
        cost_estimate=cost(0.1),
        name="forward",
    )(spots, rows, incoming, vectors, b_up, *weights, *after)


class Split:
    def __init__(self, blocks, rows, cols, wide, bit):
        low, high = (rows // wide) << bit, wide >> (bit + 1)
        self.bit, self.whole = bit, low % 16 != 0
        self.full = (blocks, rows, cols)
        self.scratch = self.full if self.whole else (blocks, high, 2, low, cols)
        self.half = (blocks, high, low, cols)
        shapes = [self.full] if self.whole else [self.half, self.half]
        self.outs = [struct(shape, bf16) for shape in shapes]

    def buffer(self):
        return pltpu.VMEM(self.scratch, bf16)

    def store(self, buffer, block, value):
        buffer[block] = value.astype(bf16).reshape(self.scratch[1:])

    def flush(self, group, place, buffer, outs, sems, blocks=slice(None)):
        if self.whole:
            start_copy(group, buffer, outs[0], sems.at[0])
            return
        mine = lax.rem(lax.div(place, 1 << self.bit), 2)
        start_copy(group, buffer.at[:, :, 1 - mine], outs[0], sems.at[0])
        start_copy(group, buffer.at[:, :, mine], outs[1], sems.at[1])

    def halves(self, outs):
        if not self.whole:
            return outs
        blocks, rows, cols = self.full
        part = outs[0].reshape(blocks, self.half[1], 2, self.half[2], cols)
        mine = (lax.axis_index("wide") >> self.bit) & 1
        return [lax.dynamic_index_in_dim(part, t, 2, keepdims=False) for t in (1 - mine, mine)]


def up_grad_kernel(split, spots, late, late_got, du_own, *rest):
    lhs, rhs, buffer, in_sem, out_sem = rest[-5:]
    outs = rest[-5 - len(split.outs) : -5]
    tiles = du_own.shape[0]
    per = TILE // 128
    waits, stores = [], []
    first, second = pl.ds(0, BLOCK), pl.ds(BLOCK, BLOCK)
    start_copy(waits, late.at[0], lhs.at[first], in_sem.at[0])
    start_copy(waits, late_got.at[0], lhs.at[second], in_sem.at[1])
    for j in range(tiles):
        start_copy(waits, du_own.at[j], rhs.at[j, first], in_sem.at[2 + 2 * j])
        start_copy(waits, late_got.at[1 + j], rhs.at[j, second], in_sem.at[3 + 2 * j])
    waits[0].wait()
    waits[1].wait()
    for j in range(tiles):
        waits[2 + 2 * j].wait()
        waits[3 + 2 * j].wait()
        value = dot(lhs[...], rhs[j], TN)
        for block in range(per):
            split.store(buffer, j * per + block, value[:, block * 128 : (block + 1) * 128])
        blocks = pl.ds(j * per, per)
        here = [out.at[blocks] for out in outs]
        split.flush(stores, spots[9], buffer.at[blocks], here, out_sem.at[j])
    wait_all(stores)


def up_grad(spots, late, late_got, du_own, wide, bit, *after):
    tiles, width = du_own.shape[0], late.shape[2]
    split = Split(tiles * TILE // 128, width, 128, wide, bit)
    outs = pl.pallas_call(
        partial(up_grad_kernel, split),
        in_specs=[SMEM] + [ANY] * 3 + [ANY] * len(after),
        out_specs=[HBM] * len(split.outs),
        out_shape=split.outs,
        scratch_shapes=[
            pltpu.VMEM((2 * BLOCK, width), bf16),
            pltpu.VMEM((tiles, 2 * BLOCK, TILE), bf16),
            split.buffer(),
            pltpu.SemaphoreType.DMA((2 + 2 * tiles,)),
            pltpu.SemaphoreType.DMA((tiles, 2)),
        ],
        compiler_params=params(20),
        cost_estimate=cost(0.1),
        name="up_grad",
    )(spots, late, late_got, du_own, *after)
    return split.halves(outs)


def down_grad_kernel(split, spots, cot_in, dy_got, g_low, g_high, got_low, got_high, *rest):
    lhs, rhs, cot, buffer, in_sem, out_sem = rest[-6:]
    outs = rest[-6 - len(split.outs) : -6]
    per, half = g_low.shape[0], dy_got.shape[1]
    tiles = 2 * per
    waits, stores = [], []
    first, second = pl.ds(0, BLOCK), pl.ds(BLOCK, BLOCK)
    for j in range(tiles):
        g, got = (g_low, got_low) if j < per else (g_high, got_high)
        start_copy(waits, g.at[j % per], lhs.at[j, first], in_sem.at[2 * j])
        start_copy(waits, got.at[j % per], lhs.at[j, second], in_sem.at[2 * j + 1])
        if j == 0:
            start_copy(waits, cot_in.at[0, :, columns(spots[7], half)], cot, in_sem.at[2 * tiles])
            start_copy(waits, dy_got, rhs.at[second], in_sem.at[2 * tiles + 1])
    live = row_ids((BLOCK, 1)) < spots[6]
    head, waits = waits[:4], waits[:2] + waits[4:]
    head[2].wait()
    head[3].wait()
    rhs[first] = jnp.where(live, cot[...], jnp.zeros_like(cot))
    mine = lax.rem(lax.div(spots[9], 1 << split.bit), 2)
    count = split.scratch[1] // tiles
    at_rows = [pl.ds(j * count, count) for j in range(tiles)]
    for j in range(tiles):
        waits[2 * j].wait()
        waits[2 * j + 1].wait()
        value = dot(lhs[j], rhs[...], TN).astype(bf16)
        for block in range(half // 128):
            piece = value[:, block * 128 : (block + 1) * 128]
            if split.whole:
                buffer[block, j * TILE : (j + 1) * TILE] = piece
            else:
                buffer[block, at_rows[j]] = piece.reshape(count, *split.scratch[2:])
        if not split.whole:
            at = at_rows[j]
            start_copy(stores, buffer.at[:, at, 1 - mine], outs[0].at[:, at], out_sem.at[0, j])
            start_copy(stores, buffer.at[:, at, mine], outs[1].at[:, at], out_sem.at[1, j])
    if split.whole:
        start_copy(stores, buffer, outs[0], out_sem.at[0, 0])
    wait_all(stores)


def down_grad(spots, cot, dy_got, g, g_got, wide, bit, *after):
    tiles, half = 2 * g[0].shape[0], dy_got.shape[1]
    split = Split(half // 128, tiles * TILE, 128, wide, bit)
    outs = pl.pallas_call(
        partial(down_grad_kernel, split),
        in_specs=[SMEM] + [ANY] * 6 + [ANY] * len(after),
        out_specs=[HBM] * len(split.outs),
        out_shape=split.outs,
        scratch_shapes=[
            pltpu.VMEM((tiles, 2 * BLOCK, TILE), bf16),
            pltpu.VMEM((2 * BLOCK, half), bf16),
            pltpu.VMEM((BLOCK, half), bf16),
            split.buffer(),
            pltpu.SemaphoreType.DMA((2 * tiles + 2,)),
            pltpu.SemaphoreType.DMA((2, tiles)),
        ],
        compiler_params=params(20),
        cost_estimate=cost(0.1),
        name="down_grad",
    )(spots, cot, dy_got, *g, *g_got, *after)
    return split.halves(outs)


def unfeed_kernel(spots, inverse, scales, d_b_down, d_b_up, cot, h, late_in, du_in, w_up_in, w_out, *rest):
    d_h, d_low, d_o, vectors, du, w_up, in_sem, du_sem = rest[-8:]
    width, hidden = w_up_in.shape
    part = hidden // 2
    tiles = part // TILE
    core = spots[7]
    waits, du_waits = [], []
    for s, side in enumerate((1 - core, core)):
        source = late_in.at[pl.ds(1, tiles)] if s == 0 else du_in
        start_copy(du_waits, source, du.at[s], du_sem.at[s])
        for j in range(tiles):
            place = pl.ds(pl.multiple_of(side * part + j * TILE, 128), TILE)
            start_copy(waits, w_up_in.at[:, place], w_up.at[s, j], in_sem.at[s * tiles + j])
    d_m = None
    for s in range(2):
        du_waits[s].wait()
        for j in range(tiles):
            waits[s * tiles + j].wait()
            term = dot(du[s, j], w_up[s, j], NT)
            d_m = term if d_m is None else d_m + term
    normed, factor = norm_stats(h[...])
    vectors[...] = jnp.zeros_like(vectors)
    vectors[8:9] = jnp.sum(d_m * normed, axis=0, keepdims=True)
    vectors[9:10] = jnp.sum(d_m, axis=0, keepdims=True)
    vectors[10:11] = d_b_down[...]
    for j in range(4):
        vectors[11 + j : 12 + j] = d_b_up[j // 2 : j // 2 + 1, j % 2 * width : (j % 2 + 1) * width]
    live = row_ids((BLOCK, 1)) < spots[6]
    kept_cot = jnp.where(live, cot[0].astype(f32), 0.0)
    d_h[...] = kept_cot + norm_back(d_m * pick(scales, 8), normed, factor)
    low = d_h[...].astype(bf16)
    d_low[...] = low
    vectors[7:8] = jnp.sum(low.astype(f32), axis=0, keepdims=True)
    heads = inverse.shape[0]
    lane = lax.broadcasted_iota(jnp.int32, (heads, width), 1)
    spread = jnp.where(lax.div(lane, HEAD) == row_ids((heads, width)), 1.0, 0.0)
    scale = lax.dot_general(
        inverse[...], spread, TN, precision=lax.Precision.HIGHEST, preferred_element_type=f32
    )
    d_o[...] = (dot(low, w_out[...], NT) * scale).astype(bf16)


def unfeed(spots, inverse, scales, d_b_down, d_b_up, cot, h, late, du_own, w_up, w_out, *after):
    width, hidden = w_up.shape
    tiles = hidden // 2 // TILE
    return pl.pallas_call(
        unfeed_kernel,
        in_specs=[SMEM] + [VMEM] * 6 + [ANY] * 3 + [VMEM] + [ANY] * len(after),
        out_specs=[VMEM] * 4,
        out_shape=[
            struct((BLOCK, width), f32),
            struct((BLOCK, width), bf16),
            struct((BLOCK, width), bf16),
            struct((16, width), f32),
        ],
        scratch_shapes=[
            pltpu.VMEM((2, tiles, BLOCK, TILE), bf16),
            pltpu.VMEM((2, tiles, width, TILE), bf16),
            pltpu.SemaphoreType.DMA((2 * tiles,)),
            pltpu.SemaphoreType.DMA((2,)),
        ],
        compiler_params=params(28),
        cost_estimate=cost(0.1),
        name="unfeed",
    )(spots, inverse, scales, d_b_down, d_b_up, cot, h, late, du_own, w_up, w_out, *after)


def attend_back(qkv, d_o, inverse, weights, ds_t, d_qkv, sums, waits):
    width = d_o.shape[1]
    group = 2 * TOGETHER
    lane = lax.broadcasted_iota(jnp.int32, (BLOCK, 128), 1)
    for first in range(0, width // HEAD, group):
        waits[first // group].wait()
        work = []
        for head in range(first, first + group):
            at = head // 2 * 128
            values, up = qkv[:, 2 * width + at : 2 * width + at + 128], d_o[:, at : at + 128]
            own = (lane < HEAD) if head % 2 == 0 else (lane >= HEAD)
            work.append(dot(jnp.where(own, values, jnp.zeros_like(values)), up, NT))
        grads = []
        for head, g_t in zip(range(first, first + group), work):
            at = head // 2 * 128
            q, keys = qkv[:, at : at + 128], qkv[:, width + at : width + at + 128]
            e = weights[head].astype(f32)
            inner = e * g_t
            total = jnp.sum(inner, axis=0, keepdims=True) * inverse[head : head + 1]
            ds_t[head - first] = (inner - e * total).astype(bf16)
            k_t = keys.T[head % 2 * HEAD : (head % 2 + 1) * HEAD]
            grads.append(
                (
                    dot(k_t, ds_t[head - first]),
                    dot(ds_t[head - first], q),
                    dot(weights[head], d_o[:, at : at + 128]),
                )
            )
        for k in range(TOGETHER):
            one, two = grads[2 * k], grads[2 * k + 1]
            at = (first // 2 + k) * 128
            dq = (jnp.concatenate([one[0], two[0]], axis=0) * 0.125).T.astype(bf16)
            dk = jnp.where(lane < HEAD, one[1], two[1]).astype(bf16)
            dv = jnp.where(lane < HEAD, one[2], two[2]).astype(bf16)
            d_qkv[:, at : at + 128] = dq
            d_qkv[:, width + at : width + at + 128] = dk
            d_qkv[:, 2 * width + at : 2 * width + at + 128] = dv
            sums[5:6, at : at + 128] = jnp.sum(dq.astype(f32), axis=0, keepdims=True)
            sums[6:7, at : at + 128] = jnp.sum(dv.astype(f32), axis=0, keepdims=True)


def sides(core, one, two):
    return jnp.where(core == 0, one, two), jnp.where(core == 0, two, one)


def heads_back_kernel(spots, inverse, before, d_o, d_low, qkv_in, kept, *rest):
    d_qkv, sent_a, sent_b, sent_c, mine, vectors, qkv, weights, ds_t, in_sem, kept_sem = rest[-11:]
    width = d_o.shape[1]
    half, wide = width // 2, 3 * width // 2
    group = 2 * TOGETHER
    waits, kept_waits = [], []
    start_copy(waits, qkv_in, qkv, in_sem.at[0])
    for first in range(0, width // HEAD, group):
        heads = pl.ds(first, group)
        start_copy(kept_waits, kept.at[heads], weights.at[heads], kept_sem.at[first // group])
    vectors[...] = before[...]
    own, theirs = sides(spots[7], d_low[:, :half], d_low[:, half:])
    mine[:, wide:] = own
    sent_c[:, half:] = theirs
    waits[0].wait()
    attend_back(qkv, d_o, inverse, weights, ds_t, d_qkv, vectors, kept_waits)
    own, theirs = sides(spots[7], d_qkv[:, :wide], d_qkv[:, wide:])
    mine[:, :wide] = own
    sent_a[...] = theirs[:, :half]
    sent_b[...] = theirs[:, half : 2 * half]
    sent_c[:, :half] = theirs[:, 2 * half :]


def heads_back(spots, inverse, before, d_o, d_low, qkv, kept, *after):
    width = d_o.shape[1]
    heads = width // HEAD
    packed = 2 * width
    return pl.pallas_call(
        heads_back_kernel,
        in_specs=[SMEM] + [VMEM] * 4 + [ANY] * (2 + len(after)),
        out_specs=[VMEM] * 6,
        out_shape=[
            struct((BLOCK, 3 * width), bf16),
            struct((BLOCK, width // 2), bf16),
            struct((BLOCK, width // 2), bf16),
            struct((BLOCK, width), bf16),
            struct((BLOCK, packed), bf16),
            struct((16, width), f32),
        ],
        scratch_shapes=[
            pltpu.VMEM((BLOCK, 3 * width), bf16),
            pltpu.VMEM((heads, BLOCK, BLOCK), bf16),
            pltpu.VMEM((2 * TOGETHER, BLOCK, BLOCK), bf16),
            pltpu.SemaphoreType.DMA((1,)),
            pltpu.SemaphoreType.DMA((heads // 2 // TOGETHER,)),
        ],
        compiler_params=params(40),
        cost_estimate=cost(0.1),
        name="heads_back",
    )(spots, inverse, before, d_o, d_low, qkv, kept, *after)


def rows_back_kernel(spots, scales, before, d_qkv, d_h, x, w_qkv, w_img, w_txt, *rest):
    sent, mine, own_rows, window, own_vectors, vectors = rest[-6:]
    core = spots[7]
    width = x.shape[1]
    half = width // 2
    vectors[...] = before[...]
    normed, factor = norm_stats(x[...].astype(f32))
    d_a = dot(d_qkv[...], w_qkv[...], NT)
    d_x = d_h[...] + norm_back(d_a * pick(scales, 3), normed, factor)
    at = row_ids((BLOCK, 1))
    is_image = (at >= 1) & (at < 1 + PATCHES)
    is_text = (at >= 1 + PATCHES) & (at < spots[6])
    image = jnp.where(is_image, d_x, 0.0).astype(bf16)
    text = jnp.where(is_text, d_x, 0.0).astype(bf16)
    both = jnp.where(is_image, image, text)
    own, theirs = sides(core, both[:, :half], both[:, half:])
    sent[:BLOCK] = theirs
    mine[...] = own
    vectors[0:1] = d_x[0:1]
    vectors[1:2] = jnp.sum(image.astype(f32), axis=0, keepdims=True)
    vectors[2:3] = jnp.sum(text.astype(f32), axis=0, keepdims=True)
    vectors[3:4] = jnp.sum(d_a * normed, axis=0, keepdims=True)
    vectors[4:5] = jnp.sum(d_a, axis=0, keepdims=True)
    share = width // lax.axis_size("wide")
    size = width // 4
    spot, place = row_ids((width, size)), lax.broadcasted_iota(jnp.int32, (width, size), 1)
    base = 4 * share * lax.div(place, share) + lax.rem(place, share)
    natural = vectors[8:16].astype(bf16)
    for j in range(4):
        lines = dot(natural, jnp.where(spot == base + share * j, 1.0, 0.0).astype(bf16))
        line = jnp.concatenate([lines[3 + k : 4 + k] for k in range(4)], axis=1)
        vectors[11 + j : 12 + j] = line
    own, theirs = sides(core, vectors[0:8], vectors[8:16])
    sent[BLOCK:] = jnp.concatenate([theirs[:, :half], theirs[:, half:]], axis=0).astype(bf16)
    own_vectors[...] = own

    rows = dot(image[:256], w_img[...], NT)
    low = dot(text, w_txt[...], NT)
    rows = jnp.concatenate([rows + low[:256], low[256:]], axis=0).astype(bf16)

    def placer(count, low, high, shift):
        at = lax.broadcasted_iota(jnp.int32, (count, BLOCK), 1)
        spot = row_ids((count, BLOCK))
        hit = (spot == at + shift) & (at >= low) & (at < high)
        return jnp.where(hit, 1.0, 0.0).astype(bf16)

    window[...] = dot(placer(window.shape[0], spots[3], spots[4], spots[5]), rows).astype(bf16)
    own_rows[...] = dot(placer(own_rows.shape[0], spots[0], spots[1], spots[2]), rows).astype(bf16)


def rows_back(spots, scales, before, d_qkv, d_h, x, w_qkv, w_img, w_txt, span, *after):
    width = w_img.shape[0]
    return pl.pallas_call(
        rows_back_kernel,
        in_specs=[SMEM] + [VMEM] * 8 + [ANY] * len(after),
        out_specs=[VMEM] * 5,
        out_shape=[
            struct((BLOCK + 16, width // 2), bf16),
            struct((BLOCK, width // 2), bf16),
            struct((span, width), bf16),
            struct((WINDOW, width), bf16),
            struct((8, width), f32),
        ],
        scratch_shapes=[pltpu.VMEM((16, width), f32)],
        compiler_params=params(32),
        cost_estimate=cost(0.1),
        name="rows_back",
    )(spots, scales, before, d_qkv, d_h, x, w_qkv, w_img, w_txt, *after)


class Filler:
    def __init__(self, splits, buffers, outs, place, sems, stores):
        self.splits, self.buffers, self.outs = splits, buffers, outs
        self.place, self.sems, self.stores = place, sems, stores
        self.chain, self.block = 0, 0

    def put(self, value):
        for j in range(value.shape[1] // 128):
            split, buffer = self.splits[self.chain], self.buffers[self.chain]
            split.store(buffer, self.block, value[:, j * 128 : (j + 1) * 128])
            self.block += 1
            if self.block == split.full[0]:
                n = len(split.outs)
                outs = self.outs[self.chain * n : (self.chain + 1) * n]
                split.flush(self.stores, self.place, buffer, outs, self.sems.at[self.chain])
                self.chain, self.block = self.chain + 1, 0


def heads_grads_kernel(splits, spots, mine, got_a, got_b, got_c, early, early_got, *rest):
    count, n = sum(len(split.outs) for split in splits), len(splits)
    outs, buffers, out_sem = rest[-count - n - 1 : -n - 1], rest[-n - 1 : -1], rest[-1]
    stores = []
    filler = Filler(splits, buffers, outs, spots[9], out_sem, stores)
    half = got_a.shape[1]
    for k, (got, low) in enumerate(((got_a, 0), (got_b, 0), (got_c, 0), (got_c, half))):
        left = 1 if k < 3 else 2
        filler.put(
            dot(early[left], mine[:, k * half : (k + 1) * half], TN)
            + dot(early_got[left], got[:, low : low + half], TN)
        )
    wait_all(stores)


def rows_grads_kernel(splits, spots, mine, got, vectors, early, early_got, *rest):
    count, n = sum(len(split.outs) for split in splits), len(splits)
    outs, buffers, out_sem = rest[-count - n - 1 : -n - 1], rest[-n - 1 : -1], rest[-1]
    stores = []
    filler = Filler(splits, buffers, outs, spots[9], out_sem, stores)
    at = row_ids((BLOCK, 1))
    is_image = at < 1 + PATCHES
    zeros = jnp.zeros_like(mine)
    image = dot(early[0, :256], jnp.where(is_image, mine[...], zeros)[:256], TN)
    image += dot(early_got[0, :256], jnp.where(is_image, got[:BLOCK], zeros)[:256], TN)
    filler.put(image)
    text = dot(early[0], jnp.where(is_image, zeros, mine[...]), TN)
    text += dot(early_got[0], jnp.where(is_image, zeros, got[:BLOCK]), TN)
    filler.put(text)
    more = got[BLOCK:].astype(f32)
    every = vectors[...] + jnp.concatenate([more[:8], more[8:]], axis=1)
    filler.put(jnp.concatenate([every, jnp.zeros((120, every.shape[1]), f32)], axis=0).T)
    wait_all(stores)


def late_grads(kernel, name, spots, args, wide, parts, *after):
    width = args[-1].shape[2]
    splits = [Split(blocks, width, 128, wide, bit) for blocks, bit in parts]
    shapes = [out for split in splits for out in split.outs]
    outs = pl.pallas_call(
        partial(kernel, splits),
        in_specs=[SMEM] + [VMEM] * len(args) + [ANY] * len(after),
        out_specs=[HBM] * len(shapes),
        out_shape=shapes,
        scratch_shapes=[split.buffer() for split in splits]
        + [pltpu.SemaphoreType.DMA((len(splits), 2))],
        compiler_params=params(32),
        cost_estimate=cost(0.1),
        name=name,
    )(spots, *args, *after)
    n = len(splits[0].outs)
    return [split.halves(outs[k * n : (k + 1) * n]) for k, split in enumerate(splits)]


def result_kernel(spots, b_down, g_low, g_high, w_down_in, h_in, *rest):
    out, g, w_down, h, sem = rest[-5:]
    tiles = g.shape[0]
    waits = []
    for j in range(tiles):
        part = g_low if j < tiles // 2 else g_high
        start_copy(waits, part.at[j % (tiles // 2)], g.at[j], sem.at[2 * j])
        start_copy(waits, w_down_in.at[pl.ds(j * TILE, TILE)], w_down.at[j], sem.at[2 * j + 1])
    start_copy(waits, h_in, h, sem.at[2 * tiles])
    live = row_ids((BLOCK, 1)) < spots[6]
    value = None
    for j in range(tiles):
        waits[2 * j].wait()
        waits[2 * j + 1].wait()
        term = dot(g[j], w_down[j])
        value = term if value is None else value + term
    waits[2 * tiles].wait()
    out[0] = jnp.where(live, value + h[...] + row(b_down), 0.0).astype(bf16)


def result(spots, g, w_down, h, b_down, *after):
    tiles, width = 2 * g[0].shape[0], h.shape[1]
    return pl.pallas_call(
        result_kernel,
        in_specs=[SMEM, VMEM] + [ANY] * 4 + [ANY] * len(after),
        out_specs=VMEM,
        out_shape=struct((1, *h.shape), bf16),
        scratch_shapes=[
            pltpu.VMEM((tiles, *g[0].shape[1:]), bf16),
            pltpu.VMEM((tiles, TILE, width), bf16),
            pltpu.VMEM(h.shape, f32),
            pltpu.SemaphoreType.DMA((2 * tiles + 1,)),
        ],
        compiler_params=params(20),
        cost_estimate=cost(1.5),
        name="result",
    )(spots, b_down, *g, w_down, h, *after)


def round_kernel(steps, lows, joined, spots, *refs):
    count = len(steps)
    keeps, gots = refs[:count], refs[count : 2 * count]
    outs = refs[len(refs) - count - (1 if joined else count) :]
    low = 0
    for k, bit in enumerate(steps):
        blocks, _, rows, _ = keeps[k].shape
        size = 2 * blocks * rows
        got = gots[k][lows[k] : lows[k] + size].reshape(keeps[k].shape)
        value = (keeps[k][...].astype(f32) + got.astype(f32)).astype(bf16)
        first = lax.rem(lax.div(spots[9], 1 << bit), 2) == 0
        outs[k][...] = jnp.where(first, value[:, 0], value[:, 1])
        send = jnp.where(first, value[:, 1], value[:, 0])
        if joined:
            outs[count][low : low + size // 2] = send.reshape(size // 2, 128)
            low += size // 2
        else:
            outs[count + k][...] = send.reshape(size // 2, 128)


class Chain:
    def __init__(self, halves, order, share, wide):
        self.bits, self.order, self.share = wide.bit_length() - 1, order[1:], share
        send, keep = halves
        self.blocks = keep.shape[0]
        self.left = set(range(self.bits)) - {order[0]}
        self.keep, self.got, self.low = keep, swap(send, "wide", order[0]).reshape(-1, 128), 0

    def view(self, value):
        bit = self.order[0]
        below = sum(other < bit for other in self.left)
        above = len(self.left) - 1 - below
        return value.reshape(self.blocks << above, 2, self.share << below, 128)


def advance(spots, chains, *after, joined=False):
    keeps = [chain.view(chain.keep) for chain in chains]
    gots = [chain.got for chain in chains]
    lows = [chain.low for chain in chains]
    steps = [chain.order[0] for chain in chains]
    sizes = [keep.size // 256 for keep in keeps]
    if any(chain.share % 16 for chain in chains):
        outs, sends = [], []
        for keep, got, low, bit in zip(keeps, gots, lows, steps):
            got = got[low : low + keep.size // 128].reshape(keep.shape)
            part = add_low(keep, got)
            mine = (lax.axis_index("wide") >> bit) & 1
            outs.append(lax.dynamic_index_in_dim(part, mine, 1, keepdims=False))
            sends.append(lax.dynamic_index_in_dim(part, 1 - mine, 1).reshape(-1, 128))
        if joined:
            sends = [jnp.concatenate(sends, axis=0)]
        outs += sends
    else:
        shapes = [(keep.shape[0], keep.shape[2], 128) for keep in keeps]
        shapes += [(sum(sizes), 128)] if joined else [(size, 128) for size in sizes]
        outs = pl.pallas_call(
            partial(round_kernel, steps, lows, joined),
            in_specs=[SMEM] + [VMEM] * (2 * len(chains)) + [ANY] * len(after),
            out_specs=[VMEM] * len(shapes),
            out_shape=[struct(shape, bf16) for shape in shapes],
            compiler_params=params(16),
            cost_estimate=cost(0.1),
            name="round",
        )(spots, *keeps, *gots, *after)
    count, low = len(chains), 0
    if joined:
        arrived = swap(outs[count], "wide", steps[0])
    for k, chain in enumerate(chains):
        chain.left = chain.left - {chain.order[0]}
        chain.order = chain.order[1:]
        chain.keep = outs[k]
        if joined:
            chain.got, chain.low = arrived, low
            low += sizes[k]
        else:
            chain.got, chain.low = swap(outs[count + k], "wide", steps[k]), 0
    return chains[-1].keep


def close_kernel(lows, *refs):
    count = len(lows)
    keeps, gots, out = refs[:count], refs[count : 2 * count], refs[-1]
    low = 0
    for keep, got, first in zip(keeps, gots, lows):
        size = keep.shape[0]
        arrived = got[first : first + size].astype(f32)
        out[low : low + size] = (keep[...].astype(f32) + arrived).astype(bf16)
        low += size


def close(chains):
    keeps = [chain.keep.reshape(-1, 128) for chain in chains]
    gots = [chain.got for chain in chains]
    lows = [chain.low for chain in chains]
    if any(chain.share % 16 for chain in chains):
        pairs = zip(keeps, gots, lows)
        return jnp.concatenate([add_low(k, g[a : a + k.shape[0]]) for k, g, a in pairs], axis=0)
    return pl.pallas_call(
        partial(close_kernel, lows),
        in_specs=[VMEM] * (2 * len(chains)),
        out_specs=VMEM,
        out_shape=struct((sum(keep.shape[0] for keep in keeps), 128), bf16),
        compiler_params=params(8),
        cost_estimate=cost(0.1),
        name="close",
    )(*keeps, *gots)


def unpack_kernel(forms, spots, own, other, own_rows, returned, *outs):
    first_core = spots[7] == 0
    pairs, low = [], 0
    for blocks, share in forms:
        pairs.append([])
        for _ in range(blocks):
            one, two = own[low : low + share].astype(f32), other[low : low + share].astype(f32)
            pairs[-1].append((jnp.where(first_core, one, two), jnp.where(first_core, two, one)))
            low += share
    down, up, qkv, out, img, txt = outs[:6]

    def spread(target, blocks):
        count = len(blocks)
        for j, (left, right) in enumerate(blocks):
            target[:, j * 128 : (j + 1) * 128] = left
            target[:, (count + j) * 128 : (count + j + 1) * 128] = right

    spread(down, pairs[0])
    spread(up, pairs[1])
    blocks = sum(pairs[2:], [])
    per = out.shape[1] // 256
    spread(qkv, blocks[: 3 * per])
    spread(out, blocks[3 * per : 4 * per])
    spread(img, blocks[4 * per : 5 * per])
    spread(txt, blocks[5 * per : 6 * per])
    left, right = blocks[6 * per]
    rows = jnp.concatenate([left.T[:8], right.T[:8]], axis=0)
    for k in range(11):
        outs[6 + k][...] = rows[k]
    share = out.shape[0]
    for j in range(4):
        outs[17][pl.ds(j * share, share)] = rows[11 + j]
    d_rows = outs[18]
    blank = jnp.zeros((d_rows.shape[1] - WINDOW, d_rows.shape[2]), bf16)
    low = jnp.concatenate([returned[...], blank], axis=0)
    high = jnp.concatenate([blank, returned[...]], axis=0)
    d_rows[0] = own_rows[...] + jnp.where(spots[8] == 0, low, high)


def unpack(spots, forms, own, other, own_rows, returned):
    share, width = forms[0][1] // 4, forms[0][0] * 256
    shapes = [(4 * share, width), (share, 4 * width), (share, 3 * width)] + [(share, width)] * 3
    shapes += [(share,)] * 11 + [(4 * share,)]
    return pl.pallas_call(
        partial(unpack_kernel, forms),
        in_specs=[SMEM] + [VMEM] * 4,
        out_specs=[VMEM] * (len(shapes) + 1),
        out_shape=[struct(shape, f32) for shape in shapes] + [struct((1, *own_rows.shape), bf16)],
        compiler_params=params(16),
        cost_estimate=cost(0.1),
        name="unpack",
    )(spots, own, other, own_rows, returned)


def swap(x, axis, bit):
    count = lax.axis_size(axis)
    route = [(i, i ^ (1 << bit)) for i in range(count)]
    return lax.ppermute(x, axis, route)


def add_low(one, two):
    f32 = jnp.float32
    return (one.astype(f32) + two.astype(f32)).astype(jnp.bfloat16)


def on_device(
    tower_states,
    caption_lengths,
    assignment,
    cls_token,
    w_img,
    b_img,
    w_txt,
    b_txt,
    gain_one,
    bias_one,
    w_qkv,
    b_query,
    b_value,
    w_out,
    b_out,
    gain_two,
    bias_two,
    w_up,
    b_up,
    w_down,
    b_down,
    cotangent,
):
    wide = lax.axis_size("wide")
    rows = tower_states[0]
    span, width = rows.shape
    bits = wide.bit_length() - 1
    payload, spots = opening(caption_lengths, assignment, tower_states)
    incoming = swap(payload, "wide", bits - 1)
    cot = cotangent[0]
    grad, d_b_down, dy_other = hidden_grad(spots, cot, w_down)
    dy_got = swap(dy_other, "dp", 0)
    vectors = jnp.stack(
        [cls_token, b_img, b_txt, gain_one, bias_one, b_query, b_value, b_out, gain_two, bias_two]
    )
    share, tail = width // wide, list(range(3, bits))

    def order(*first):
        return list(first) + tail

    x, qkv, kept, du_own, h, early, late, *g, inverse, d_b_up = forward(
        spots, tower_states, incoming, vectors, b_up, (w_img, w_txt, w_qkv, w_out, w_up, grad), dy_got
    )
    late_got = swap(late, "dp", 0)
    g_got = [swap(t, "dp", 0) for t in g]
    early_got = swap(early, "dp", 0)
    up = up_grad(spots, late, late_got, du_own, wide, 1)
    down = down_grad(spots, cotangent, dy_got, g, g_got, wide, 0, up[1])
    up = Chain(up, order(1, 0, 2), share, wide)
    down = Chain(down, order(0, 1, 2), 4 * share, wide)
    firsts = [down, up]
    d_h, d_low, d_o, before = unfeed(
        spots, inverse, vectors, d_b_down, d_b_up, cotangent, h, late, du_own, w_up, w_out, down.keep
    )
    d_qkv, *sent, mine, before = heads_back(
        spots, inverse, before, d_o, d_low, qkv, kept, down.keep, early_got
    )
    got = [swap(t, "dp", 0) for t in sent]
    step = advance(spots, firsts, mine)
    parts = [(6, order(0, 1, 2)), (6, order(1, 0, 2))]
    heads = late_grads(
        heads_grads_kernel, "heads_grads", spots, (mine, *got, early, early_got), wide,
        [(blocks, t[0]) for blocks, t in parts], step,
    )
    heads = [Chain(halves, t, share, wide) for halves, (_, t) in zip(heads, parts)]
    sent, mine, own_rows, window, own_vectors = rows_back(
        spots, vectors, before, d_qkv, d_h, x, w_qkv, w_img, w_txt, span, heads[0].keep
    )
    got = swap(sent, "dp", 0)
    step = advance(spots, firsts, mine, joined=True)
    parts = [(7, order(1, 0, 2))]
    lasts = late_grads(
        rows_grads_kernel, "rows_grads", spots, (mine, got, own_vectors, early, early_got), wide,
        [(blocks, t[0]) for blocks, t in parts], step,
    )
    lasts = [Chain(halves, t, share, wide) for halves, (_, t) in zip(lasts, parts)]
    returned = swap(window, "wide", bits - 1)
    step = advance(spots, heads, lasts[0].keep)
    out = result(spots, g, w_down, h, b_down, step)
    step = advance(spots, firsts, out, joined=True)
    step = advance(spots, lasts, step)
    step = advance(spots, heads, step, returned, joined=True)
    step = advance(spots, lasts, step)
    chains = heads + lasts
    while chains[0].order:
        step = advance(spots, chains, step, joined=True)
    while firsts[0].order:
        step = advance(spots, firsts, step, joined=True)
    chains = firsts + chains
    own = close(chains)
    forms = [(t.blocks, t.share) for t in chains]
    *results, d_rows = unpack(spots, forms, own, swap(own, "dp", 0), own_rows, returned)
    down, up, d_w_qkv, d_w_out, d_w_img, d_w_txt = results[:6]
    vectors, d_b_up = results[6:17], results[17]
    (
        d_cls,
        d_b_img,
        d_b_txt,
        d_gain_one,
        d_bias_one,
        d_b_query,
        d_b_value,
        d_b_out,
        d_gain_two,
        d_bias_two,
        d_b_down,
    ) = vectors
    return (
        out,
        d_rows,
        d_cls,
        d_w_img,
        d_b_img,
        d_w_txt,
        d_b_txt,
        d_gain_one,
        d_bias_one,
        d_w_qkv,
        d_b_query,
        d_b_value,
        d_w_out,
        d_b_out,
        d_gain_two,
        d_bias_two,
        up,
        d_b_up,
        down,
        d_b_down,
    )


def solution(mesh):
    placed = (
        P("dp", "wide", None),
        P("dp", None, None),
        P("dp", None, None),
        P(),
        P(),
        P(),
        P(),
        P(),
        P(),
        P(),
        P(),
        P(),
        P(),
        P(),
        P(),
        P(),
        P(),
        P(),
        P(),
        P(),
        P(),
        P("dp", "wide", None),
    )
    return jax.shard_map(
        on_device,
        mesh=mesh,
        in_specs=placed,
        out_specs=(
            P("dp", "wide", None),
            P("dp", "wide", None),
            P("wide"),
            P("wide", None),
            P("wide"),
            P("wide", None),
            P("wide"),
            P("wide"),
            P("wide"),
            P("wide", None),
            P("wide"),
            P("wide"),
            P("wide", None),
            P("wide"),
            P("wide"),
            P("wide"),
            P("wide", None),
            P("wide"),
            P("wide", None),
            P("wide"),
        ),
        check_vma=False,
    )
```

```python
from functools import partial
import math
import jax
import jax.numpy as jnp
from jax import lax
from jax.experimental import pallas as pl
from jax.experimental.pallas import tpu as pltpu
from jax.sharding import PartitionSpec as P

HEAD = 64
PATCHES = 197
BLOCK = 512
WINDOW = 320
TILE = 768
TOGETHER = 2
bf16 = jnp.bfloat16
f32 = jnp.float32
VMEM = pl.BlockSpec(memory_space=pltpu.VMEM)
SMEM = pl.BlockSpec(memory_space=pltpu.SMEM)
ANY = pl.BlockSpec(memory_space=pl.ANY)
HBM = pl.BlockSpec(memory_space=pltpu.HBM)
NN = (((1,), (0,)), ((), ()))
NT = (((1,), (1,)), ((), ()))
TN = (((0,), (0,)), ((), ()))


def dot(left, right, dims=NN):
    return lax.dot_general(left, right, dims, preferred_element_type=f32)


def params(mib, **more):
    return pltpu.CompilerParams(vmem_limit_bytes=mib << 20, **more)


def start_copy(group, source, target, sem):
    copy = pltpu.make_async_copy(source, target, sem)
    copy.start()
    group.append(copy)


def wait_all(group):
    for copy in group:
        copy.wait()


def columns(side, size):
    return pl.ds(pl.multiple_of(side * size, 128), size)


def cost(microseconds):
    flops = int(microseconds * 1153000000)
    return pl.CostEstimate(flops=flops, bytes_accessed=1024, transcendentals=0)


def struct(shape, dtype):
    return jax.ShapeDtypeStruct(shape, dtype)


def row(vector):
    return vector[...].astype(f32).reshape(1, -1)


def pick(vectors, k):
    return vectors[k : k + 1].astype(f32)


def row_ids(shape):
    return lax.broadcasted_iota(jnp.int32, shape, 0)


def norm_stats(rows):
    mean = jnp.mean(rows, axis=-1, keepdims=True)
    centred = rows - mean
    factor = lax.rsqrt(jnp.mean(centred * centred, axis=-1, keepdims=True) + 1e-05)
    return centred * factor, factor


def norm_back(scaled, normed, factor):
    return factor * (
        scaled
        - jnp.mean(scaled, axis=-1, keepdims=True)
        - normed * jnp.mean(scaled * normed, axis=-1, keepdims=True)
    )


def open_kernel(tables, rows, payload, spots):
    place, core = lax.axis_index("wide"), lax.axis_index("dp")
    half = lax.axis_size("wide") // 2
    upper = place >= half
    pair = lax.rem(place, half)

    def entry(table, column):
        value = tables[table]
        hit = (row_ids(value.shape) == pair) & (
            lax.broadcasted_iota(jnp.int32, value.shape, 1) == column
        )
        return jnp.sum(jnp.where(hit, value, 0))

    span = rows.shape[1]
    gap = span - WINDOW
    mine = entry(1, jnp.where(upper, 1, 0))
    other = 1 - mine
    first = entry(0, 0)
    begin = jnp.where(mine == 0, 0, first)
    cut = 1 + PATCHES
    count = cut + entry(0, mine)
    back = jnp.where(mine == 0, 0, gap)
    image, text = mine * PATCHES - 1, begin - cut
    spots[0] = jnp.where(upper, cut, 1)
    spots[1] = jnp.where(upper, count, cut)
    spots[2] = jnp.where(upper, text, image)
    spots[3] = jnp.where(upper, 1, cut)
    spots[4] = jnp.where(upper, cut, count)
    spots[5] = jnp.where(upper, image, text) - back
    spots[6] = count
    spots[7] = core
    spots[8] = other
    spots[9] = place
    value = rows[0]
    payload[...] = jnp.where(other == 0, value[:WINDOW], value[gap:])


def opening(lens, order, rows):
    width = rows.shape[2]
    return pl.pallas_call(
        open_kernel,
        in_specs=[VMEM, VMEM],
        out_specs=[VMEM, SMEM],
        out_shape=[struct((WINDOW, width), bf16), struct((10,), jnp.int32)],
        compiler_params=params(8),
        cost_estimate=cost(0.1),
        name="opening",
    )(jnp.concatenate([lens, order], axis=0), rows)


def hidden_grad_kernel(spots, cot, w_down, grad, d_bias, dy_other):
    live = row_ids((BLOCK, 1)) < spots[6]
    dy = jnp.where(live, cot[...], jnp.zeros_like(cot))
    grad[...] = dot(dy, w_down[...], NT).astype(bf16)

    @pl.when(pl.program_id(0) == 0)
    def _():
        d_bias[...] = jnp.sum(dy.astype(f32), axis=0, keepdims=True)
        half = dy_other.shape[1]
        dy_other[...] = jnp.where(spots[7] == 0, dy[:, half:], dy[:, :half])


def hidden_grad(spots, cot, w_down):
    hidden, width = w_down.shape
    return pl.pallas_call(
        hidden_grad_kernel,
        grid=(hidden // TILE,),
        in_specs=[
            SMEM,
            pl.BlockSpec((BLOCK, width), lambda i: (0, 0)),
            pl.BlockSpec((TILE, width), lambda i: (i, 0)),
        ],
        out_specs=[
            pl.BlockSpec((BLOCK, TILE), lambda i: (0, i)),
            pl.BlockSpec((1, width), lambda i: (0, 0)),
            pl.BlockSpec((BLOCK, width // 2), lambda i: (0, 0)),
        ],
        out_shape=[
            struct((BLOCK, hidden), bf16),
            struct((1, width), f32),
            struct((BLOCK, width // 2), bf16),
        ],
        compiler_params=params(16),
        cost_estimate=cost(0.1),
        name="hidden_grad",
    )(spots, cot, w_down)


def bias_tile(b_up, side, start):
    half = b_up.shape[0] // 2
    one, two = b_up[pl.ds(start, TILE)], b_up[pl.ds(half + start, TILE)]
    return jnp.where(side == 0, one.astype(f32), two.astype(f32)).reshape(1, -1)


def hidden_tile(m, w, b, grad, g, du):
    inner = dot(m, w) + b
    below = 0.5 + 0.5 * lax.erf(inner * math.sqrt(0.5))
    g[...] = (inner * below).astype(bf16)
    slope = below + inner * jnp.exp(-0.5 * inner * inner) * (1.0 / math.sqrt(2.0 * math.pi))
    low = (grad.astype(f32) * slope).astype(bf16)
    du[...] = low
    return jnp.sum(low.astype(f32), axis=0, keepdims=True)


def assemble(spots, rows, tower, incoming, vectors, w_img, w_txt, raw, x, waits):
    def picker(cols, low, high, shift):
        at = row_ids((BLOCK, cols))
        col = lax.broadcasted_iota(jnp.int32, (BLOCK, cols), 1)
        hit = (col == at + shift) & (at >= low) & (at < high)
        return jnp.where(hit, 1.0, 0.0).astype(bf16)

    span = rows.shape[1]
    tower[:span] = rows[0]
    tower[span:] = jnp.zeros((tower.shape[0] - span, rows.shape[2]), bf16)
    picked = dot(picker(tower.shape[0], spots[0], spots[1], spots[2]), tower[...])
    picked += dot(picker(incoming.shape[0], spots[3], spots[4], spots[5]), incoming[...])
    raw[...] = picked.astype(bf16)
    count = spots[6]
    edge, over = 192, 208
    waits[0].wait()
    image = dot(raw[:over], w_img[...]) + pick(vectors, 1)
    waits[1].wait()
    text = dot(raw[edge:], w_txt[...]) + pick(vectors, 2)
    at = row_ids((edge, 1))
    top = jnp.where(at == 0, pick(vectors, 0), image[:edge])
    at = row_ids((over - edge, 1)) + edge
    mid = jnp.where(at < 1 + PATCHES, image[edge:], text[: over - edge])
    mid = jnp.where(at < count, mid, 0.0)
    at = row_ids((BLOCK - over, 1)) + over
    low = jnp.where(at < count, text[over - edge :], 0.0)
    x[:edge] = top.astype(bf16)
    x[edge:over] = mid.astype(bf16)
    x[over:] = low.astype(bf16)


def attend(count, qkv, o_t, inverse, weights, kept, stores, sem):
    width = o_t.shape[0]
    lane = lax.broadcasted_iota(jnp.int32, (BLOCK, 128), 1)
    dead = row_ids((BLOCK, 1)) >= count
    group = 2 * TOGETHER
    for first in range(0, width // HEAD, group):
        scores = []
        for head in range(first, first + group):
            at = head // 2 * 128
            q, keys = qkv[:, at : at + 128], qkv[:, width + at : width + at + 128]
            own = (lane < HEAD) if head % 2 == 0 else (lane >= HEAD)
            scores.append(dot(jnp.where(own, keys, jnp.zeros_like(keys)), q, NT))
        for head, s_t in zip(range(first, first + group), scores):
            s_t = jnp.where(dead, -1000000000.0, s_t)
            top = jnp.max(s_t, axis=0, keepdims=True)
            e = jnp.exp(s_t - top)
            one_over = 1.0 / jnp.sum(e, axis=0, keepdims=True)
            weights[head] = e.astype(bf16)
            values = qkv[:, 2 * width + head // 2 * 128 : 2 * width + head // 2 * 128 + 128]
            v_t = values.T[head % 2 * HEAD : (head % 2 + 1) * HEAD]
            part = dot(v_t, weights[head]) * one_over
            o_t[head * HEAD : (head + 1) * HEAD] = part.astype(bf16)
            inverse[head : head + 1] = one_over
        heads = pl.ds(first, group)
        start_copy(stores, weights.at[heads], kept.at[heads], sem.at[first // group])


def forward_kernel(
    spots, rows, incoming, vectors, b_up, w_img_in, w_txt_in, w_qkv_in, w_out_in, w_up_in, grad_in,
    after,
    x_out, qkv_out, kept, du_out, h_out, early, late, g_low, g_high, inverse, d_b,
    w_img, w_txt, w_qkv, w_out, w_up, grad, tower, x, qkv, o_t, weights, du_own, h, g,
    in_sem, out_sem, kept_sem, hidden_sem,
):
    width, hidden = w_up_in.shape
    part = hidden // 2
    tiles = part // TILE
    core = spots[7]
    waits, stores = [], []
    for k, (source, target) in enumerate(
        ((w_img_in, w_img), (w_txt_in, w_txt), (w_qkv_in, w_qkv), (w_out_in, w_out))
    ):
        start_copy(waits, source, target, in_sem.at[k])
    for k, side in enumerate((1 - core, core)):
        start_copy(waits, w_up_in.at[:, columns(side, part)], w_up.at[k], in_sem.at[4 + 2 * k])
        start_copy(waits, grad_in.at[:, columns(side, part)], grad.at[k], in_sem.at[5 + 2 * k])
    raw, a = early.at[0], early.at[1]
    assemble(spots, rows, tower, incoming, vectors, w_img, w_txt, raw, x, waits)
    start_copy(stores, x, x_out, out_sem.at[0])
    normed, _ = norm_stats(x[...].astype(f32))
    a[...] = (normed * pick(vectors, 3) + pick(vectors, 4)).astype(bf16)
    waits[2].wait()
    q = dot(a[...], w_qkv[:, :width]) + pick(vectors, 5)
    qkv[:, :width] = q.astype(bf16) * jnp.asarray(0.125, bf16)
    qkv[:, width : 2 * width] = dot(a[...], w_qkv[:, width : 2 * width]).astype(bf16)
    qkv[:, 2 * width :] = (dot(a[...], w_qkv[:, 2 * width :]) + pick(vectors, 6)).astype(bf16)
    start_copy(stores, qkv, qkv_out, out_sem.at[1])
    inverse[...] = jnp.zeros_like(inverse)
    attend(spots[6], qkv, o_t, inverse, weights, kept, stores, kept_sem)
    o = o_t[...].T
    early[2] = o
    waits[3].wait()
    h[...] = x[...].astype(f32) + dot(o, w_out[...]) + pick(vectors, 7)
    start_copy(stores, h, h_out, out_sem.at[2])
    normed, _ = norm_stats(h[...])
    m = late.at[0]
    m[...] = (normed * pick(vectors, 8) + pick(vectors, 9)).astype(bf16)
    for k in range(4, 8):
        waits[k].wait()
    for k, side in enumerate((1 - core, core)):
        for j in range(tiles):
            at = pl.ds(j * TILE, TILE)
            b = bias_tile(b_up, side, j * TILE)
            target = late.at[1 + j] if k == 0 else du_own.at[j]
            sums = hidden_tile(m[...], w_up[k, :, at], b, grad[k, :, at], g.at[k, j], target)
            d_b[pl.ds(side, 1), at] = sums
            if k == 1:
                start_copy(stores, target, du_out.at[j], hidden_sem.at[j])
    core_first = core == 0
    g_low[...] = jnp.where(core_first, g[1], g[0])
    g_high[...] = jnp.where(core_first, g[0], g[1])
    wait_all(stores)


def forward(spots, rows, incoming, vectors, b_up, weights, *after):
    width, hidden = weights[4].shape
    part = hidden // 2
    tiles = part // TILE
    tile = (BLOCK, TILE)
    heads = width // HEAD
    return pl.pallas_call(
        forward_kernel,
        in_specs=[SMEM] + [VMEM] * 4 + [HBM] * 6 + [ANY] * len(after),
        out_specs=[HBM] * 5 + [VMEM] * 6,
        out_shape=[
            struct((BLOCK, width), bf16),
            struct((BLOCK, 3 * width), bf16),
            struct((heads, BLOCK, BLOCK), bf16),
            struct((tiles, *tile), bf16),
            struct((BLOCK, width), f32),
            struct((3, BLOCK, width), bf16),
            struct((1 + tiles, *tile), bf16),
            struct((tiles, *tile), bf16),
            struct((tiles, *tile), bf16),
            struct((heads + -heads % 8, BLOCK), f32),
            struct((2, part), f32),
        ],
        scratch_shapes=[
            pltpu.VMEM((width, width), bf16),
            pltpu.VMEM((width, width), bf16),
            pltpu.VMEM((width, 3 * width), bf16),
            pltpu.VMEM((width, width), bf16),
            pltpu.VMEM((2, width, part), bf16),
            pltpu.VMEM((2, BLOCK, part), bf16),
            pltpu.VMEM((rows.shape[1] + -rows.shape[1] % 16, width), bf16),
            pltpu.VMEM((BLOCK, width), bf16),
            pltpu.VMEM((BLOCK, 3 * width), bf16),
            pltpu.VMEM((width, BLOCK), bf16),
            pltpu.VMEM((heads, BLOCK, BLOCK), bf16),
            pltpu.VMEM((tiles, *tile), bf16),
            pltpu.VMEM((BLOCK, width), f32),
            pltpu.VMEM((2, tiles, *tile), bf16),
            pltpu.SemaphoreType.DMA((8,)),
            pltpu.SemaphoreType.DMA((3,)),
            pltpu.SemaphoreType.DMA((heads // 2 // TOGETHER,)),
            pltpu.SemaphoreType.DMA((tiles,)),
        ],
        compiler_params=params(50),
        cost_estimate=cost(0.1),
        name="forward",
    )(spots, rows, incoming, vectors, b_up, *weights, *after)


class Split:
    def __init__(self, blocks, rows, cols, wide, bit):
        low, high = (rows // wide) << bit, wide >> (bit + 1)
        self.bit, self.whole = bit, low % 16 != 0
        self.full = (blocks, rows, cols)
        self.scratch = self.full if self.whole else (blocks, high, 2, low, cols)
        self.half = (blocks, high, low, cols)
        shapes = [self.full] if self.whole else [self.half, self.half]
        self.outs = [struct(shape, bf16) for shape in shapes]

    def buffer(self):
        return pltpu.VMEM(self.scratch, bf16)

    def store(self, buffer, block, value):
        buffer[block] = value.astype(bf16).reshape(self.scratch[1:])

    def flush(self, group, place, buffer, outs, sems, blocks=slice(None)):
        if self.whole:
            start_copy(group, buffer, outs[0], sems.at[0])
            return
        mine = lax.rem(lax.div(place, 1 << self.bit), 2)
        start_copy(group, buffer.at[:, :, 1 - mine], outs[0], sems.at[0])
        start_copy(group, buffer.at[:, :, mine], outs[1], sems.at[1])

    def halves(self, outs):
        if not self.whole:
            return outs
        blocks, rows, cols = self.full
        part = outs[0].reshape(blocks, self.half[1], 2, self.half[2], cols)
        mine = (lax.axis_index("wide") >> self.bit) & 1
        return [lax.dynamic_index_in_dim(part, t, 2, keepdims=False) for t in (1 - mine, mine)]


def up_grad_kernel(split, spots, late, late_got, du_own, *rest):
    buffer, out_sem = rest[-2:]
    outs = rest[-2 - len(split.outs) : -2]
    tiles = du_own.shape[0]
    per = TILE // 128
    stores = []
    for j in range(tiles):
        value = dot(late[0], du_own[j], TN) + dot(late_got[0], late_got[1 + j], TN)
        for block in range(per):
            split.store(buffer, j * per + block, value[:, block * 128 : (block + 1) * 128])
        blocks = pl.ds(j * per, per)
        here = [out.at[blocks] for out in outs]
        split.flush(stores, spots[9], buffer.at[blocks], here, out_sem.at[j])
    wait_all(stores)


def up_grad(spots, late, late_got, du_own, wide, bit, *after):
    tiles, width = du_own.shape[0], late.shape[2]
    split = Split(tiles * TILE // 128, width, 128, wide, bit)
    outs = pl.pallas_call(
        partial(up_grad_kernel, split),
        in_specs=[SMEM] + [VMEM] * 3 + [ANY] * len(after),
        out_specs=[ANY] * len(split.outs),
        out_shape=split.outs,
        scratch_shapes=[split.buffer(), pltpu.SemaphoreType.DMA((tiles, 2))],
        compiler_params=params(20),
        cost_estimate=cost(0.1),
        name="up_grad",
    )(spots, late, late_got, du_own, *after)
    return split.halves(outs)


def down_grad_kernel(split, spots, cot, dy_got, g_low, g_high, got_low, got_high, *rest):
    buffer, out_sem = rest[-2:]
    outs = rest[-2 - len(split.outs) : -2]
    per, half = g_low.shape[0], dy_got.shape[1]
    tiles = 2 * per
    stores = []
    live = row_ids((BLOCK, 1)) < spots[6]
    kept = jnp.where(spots[7] == 0, cot[0, :, :half], cot[0, :, half:])
    dy = jnp.where(live, kept, jnp.zeros_like(kept))
    mine = lax.rem(lax.div(spots[9], 1 << split.bit), 2)
    count = split.scratch[1] // tiles
    for j in range(tiles):
        g, got = (g_low, got_low) if j < per else (g_high, got_high)
        value = dot(g[j % per], dy, TN) + dot(got[j % per], dy_got[...], TN)
        value = value.astype(bf16)
        for block in range(half // 128):
            piece = value[:, block * 128 : (block + 1) * 128]
            if split.whole:
                buffer[block, j * TILE : (j + 1) * TILE] = piece
            else:
                buffer[block, j * count : (j + 1) * count] = piece.reshape(count, *split.scratch[2:])
        if not split.whole:
            at = pl.ds(j * count, count)
            start_copy(stores, buffer.at[:, at, 1 - mine], outs[0].at[:, at], out_sem.at[0, j])
            start_copy(stores, buffer.at[:, at, mine], outs[1].at[:, at], out_sem.at[1, j])
    if split.whole:
        start_copy(stores, buffer, outs[0], out_sem.at[0, 0])
    wait_all(stores)


def down_grad(spots, cot, dy_got, g, g_got, wide, bit, *after):
    tiles, half = 2 * g[0].shape[0], dy_got.shape[1]
    split = Split(half // 128, tiles * TILE, 128, wide, bit)
    outs = pl.pallas_call(
        partial(down_grad_kernel, split),
        in_specs=[SMEM] + [VMEM] * 6 + [ANY] * len(after),
        out_specs=[ANY] * len(split.outs),
        out_shape=split.outs,
        scratch_shapes=[split.buffer(), pltpu.SemaphoreType.DMA((2, tiles))],
        compiler_params=params(20),
        cost_estimate=cost(0.1),
        name="down_grad",
    )(spots, cot, dy_got, *g, *g_got, *after)
    return split.halves(outs)


def unfeed_kernel(spots, inverse, scales, d_b_down, d_b_up, cot, h, late_in, du_in, w_up_in, w_out, *rest):
    d_h, d_low, d_o, vectors, du, w_up, in_sem, du_sem = rest[-8:]
    width, hidden = w_up_in.shape
    part = hidden // 2
    tiles = part // TILE
    core = spots[7]
    waits, du_waits = [], []
    for s, side in enumerate((1 - core, core)):
        source = late_in.at[pl.ds(1, tiles)] if s == 0 else du_in
        start_copy(du_waits, source, du.at[s], du_sem.at[s])
        for j in range(tiles):
            place = pl.ds(pl.multiple_of(side * part + j * TILE, 128), TILE)
            start_copy(waits, w_up_in.at[:, place], w_up.at[s, j], in_sem.at[s * tiles + j])
    d_m = None
    for s in range(2):
        du_waits[s].wait()
        for j in range(tiles):
            waits[s * tiles + j].wait()
            term = dot(du[s, j], w_up[s, j], NT)
            d_m = term if d_m is None else d_m + term
    normed, factor = norm_stats(h[...])
    vectors[...] = jnp.zeros_like(vectors)
    vectors[8:9] = jnp.sum(d_m * normed, axis=0, keepdims=True)
    vectors[9:10] = jnp.sum(d_m, axis=0, keepdims=True)
    vectors[10:11] = d_b_down[...]
    for j in range(4):
        vectors[11 + j : 12 + j] = d_b_up[j // 2 : j // 2 + 1, j % 2 * width : (j % 2 + 1) * width]
    live = row_ids((BLOCK, 1)) < spots[6]
    kept_cot = jnp.where(live, cot[0].astype(f32), 0.0)
    d_h[...] = kept_cot + norm_back(d_m * pick(scales, 8), normed, factor)
    low = d_h[...].astype(bf16)
    d_low[...] = low
    vectors[7:8] = jnp.sum(low.astype(f32), axis=0, keepdims=True)
    heads = inverse.shape[0]
    lane = lax.broadcasted_iota(jnp.int32, (heads, width), 1)
    spread = jnp.where(lax.div(lane, HEAD) == row_ids((heads, width)), 1.0, 0.0).astype(bf16)
    exact = inverse[...]
    coarse = exact.astype(bf16)
    fine = (exact - coarse.astype(f32)).astype(bf16)
    scale = dot(coarse, spread, TN) + dot(fine, spread, TN)
    d_o[...] = (dot(low, w_out[...], NT) * scale).astype(bf16)


def unfeed(spots, inverse, scales, d_b_down, d_b_up, cot, h, late, du_own, w_up, w_out, *after):
    width, hidden = w_up.shape
    tiles = hidden // 2 // TILE
    return pl.pallas_call(
        unfeed_kernel,
        in_specs=[SMEM] + [VMEM] * 6 + [ANY] * 3 + [VMEM] + [ANY] * len(after),
        out_specs=[VMEM] * 4,
        out_shape=[
            struct((BLOCK, width), f32),
            struct((BLOCK, width), bf16),
            struct((BLOCK, width), bf16),
            struct((16, width), f32),
        ],
        scratch_shapes=[
            pltpu.VMEM((2, tiles, BLOCK, TILE), bf16),
            pltpu.VMEM((2, tiles, width, TILE), bf16),
            pltpu.SemaphoreType.DMA((2 * tiles,)),
            pltpu.SemaphoreType.DMA((2,)),
        ],
        compiler_params=params(28),
        cost_estimate=cost(0.1),
        name="unfeed",
    )(spots, inverse, scales, d_b_down, d_b_up, cot, h, late, du_own, w_up, w_out, *after)


def attend_back(qkv, d_o, inverse, weights, ds_t, d_qkv, sums, waits):
    width = d_o.shape[1]
    group = 2 * TOGETHER
    lane = lax.broadcasted_iota(jnp.int32, (BLOCK, 128), 1)
    for first in range(0, width // HEAD, group):
        waits[first // group].wait()
        work = []
        for head in range(first, first + group):
            at = head // 2 * 128
            values, up = qkv[:, 2 * width + at : 2 * width + at + 128], d_o[:, at : at + 128]
            own = (lane < HEAD) if head % 2 == 0 else (lane >= HEAD)
            work.append(dot(jnp.where(own, values, jnp.zeros_like(values)), up, NT))
        grads = []
        for head, g_t in zip(range(first, first + group), work):
            at = head // 2 * 128
            q, keys = qkv[:, at : at + 128], qkv[:, width + at : width + at + 128]
            e = weights[head].astype(f32)
            inner = e * g_t
            total = jnp.sum(inner, axis=0, keepdims=True) * inverse[head : head + 1]
            ds_t[head - first] = (inner - e * total).astype(bf16)
            k_t = keys.T[head % 2 * HEAD : (head % 2 + 1) * HEAD]
            grads.append(
                (
                    dot(k_t, ds_t[head - first]),
                    dot(ds_t[head - first], q),
                    dot(weights[head], d_o[:, at : at + 128]),
                )
            )
        for k in range(TOGETHER):
            one, two = grads[2 * k], grads[2 * k + 1]
            at = (first // 2 + k) * 128
            dq = (jnp.concatenate([one[0], two[0]], axis=0) * 0.125).T.astype(bf16)
            dk = jnp.where(lane < HEAD, one[1], two[1]).astype(bf16)
            dv = jnp.where(lane < HEAD, one[2], two[2]).astype(bf16)
            d_qkv[:, at : at + 128] = dq
            d_qkv[:, width + at : width + at + 128] = dk
            d_qkv[:, 2 * width + at : 2 * width + at + 128] = dv
            sums[5:6, at : at + 128] = jnp.sum(dq.astype(f32), axis=0, keepdims=True)
            sums[6:7, at : at + 128] = jnp.sum(dv.astype(f32), axis=0, keepdims=True)


def sides(core, one, two):
    return jnp.where(core == 0, one, two), jnp.where(core == 0, two, one)


def heads_back_kernel(spots, inverse, before, d_o, d_low, qkv_in, kept, *rest):
    d_qkv, sent_a, sent_b, sent_c, mine, vectors, qkv, weights, ds_t, in_sem, kept_sem = rest[-11:]
    width = d_o.shape[1]
    half, wide = width // 2, 3 * width // 2
    group = 2 * TOGETHER
    waits, kept_waits = [], []
    start_copy(waits, qkv_in, qkv, in_sem.at[0])
    for first in range(0, width // HEAD, group):
        heads = pl.ds(first, group)
        start_copy(kept_waits, kept.at[heads], weights.at[heads], kept_sem.at[first // group])
    vectors[...] = before[...]
    own, theirs = sides(spots[7], d_low[:, :half], d_low[:, half:])
    mine[:, wide:] = own
    sent_c[:, half:] = theirs
    waits[0].wait()
    attend_back(qkv, d_o, inverse, weights, ds_t, d_qkv, vectors, kept_waits)
    own, theirs = sides(spots[7], d_qkv[:, :wide], d_qkv[:, wide:])
    mine[:, :wide] = own
    sent_a[...] = theirs[:, :half]
    sent_b[...] = theirs[:, half : 2 * half]
    sent_c[:, :half] = theirs[:, 2 * half :]


def heads_back(spots, inverse, before, d_o, d_low, qkv, kept, *after):
    width = d_o.shape[1]
    heads = width // HEAD
    packed = 2 * width
    return pl.pallas_call(
        heads_back_kernel,
        in_specs=[SMEM] + [VMEM] * 4 + [ANY] * (2 + len(after)),
        out_specs=[VMEM] * 6,
        out_shape=[
            struct((BLOCK, 3 * width), bf16),
            struct((BLOCK, width // 2), bf16),
            struct((BLOCK, width // 2), bf16),
            struct((BLOCK, width), bf16),
            struct((BLOCK, packed), bf16),
            struct((16, width), f32),
        ],
        scratch_shapes=[
            pltpu.VMEM((BLOCK, 3 * width), bf16),
            pltpu.VMEM((heads, BLOCK, BLOCK), bf16),
            pltpu.VMEM((2 * TOGETHER, BLOCK, BLOCK), bf16),
            pltpu.SemaphoreType.DMA((1,)),
            pltpu.SemaphoreType.DMA((heads // 2 // TOGETHER,)),
        ],
        compiler_params=params(40),
        cost_estimate=cost(0.1),
        name="heads_back",
    )(spots, inverse, before, d_o, d_low, qkv, kept, *after)


def rows_back_kernel(spots, scales, before, d_qkv, d_h, x, w_qkv, w_img, w_txt, *rest):
    sent, mine, own_rows, window, own_vectors, vectors = rest[-6:]
    core = spots[7]
    width = x.shape[1]
    half = width // 2
    vectors[...] = before[...]
    normed, factor = norm_stats(x[...].astype(f32))
    d_a = dot(d_qkv[...], w_qkv[...], NT)
    d_x = d_h[...] + norm_back(d_a * pick(scales, 3), normed, factor)
    at = row_ids((BLOCK, 1))
    is_image = (at >= 1) & (at < 1 + PATCHES)
    is_text = (at >= 1 + PATCHES) & (at < spots[6])
    image = jnp.where(is_image, d_x, 0.0).astype(bf16)
    text = jnp.where(is_text, d_x, 0.0).astype(bf16)
    both = jnp.where(is_image, image, text)
    own, theirs = sides(core, both[:, :half], both[:, half:])
    sent[:BLOCK] = theirs
    mine[...] = own
    vectors[0:1] = d_x[0:1]
    vectors[1:2] = jnp.sum(image.astype(f32), axis=0, keepdims=True)
    vectors[2:3] = jnp.sum(text.astype(f32), axis=0, keepdims=True)
    vectors[3:4] = jnp.sum(d_a * normed, axis=0, keepdims=True)
    vectors[4:5] = jnp.sum(d_a, axis=0, keepdims=True)
    share = width // lax.axis_size("wide")
    size = width // 4
    spot, place = row_ids((width, size)), lax.broadcasted_iota(jnp.int32, (width, size), 1)
    base = 4 * share * lax.div(place, share) + lax.rem(place, share)
    natural = vectors[8:16].astype(bf16)
    for j in range(4):
        lines = dot(natural, jnp.where(spot == base + share * j, 1.0, 0.0).astype(bf16))
        line = jnp.concatenate([lines[3 + k : 4 + k] for k in range(4)], axis=1)
        vectors[11 + j : 12 + j] = line
    own, theirs = sides(core, vectors[0:8], vectors[8:16])
    sent[BLOCK:] = jnp.concatenate([theirs[:, :half], theirs[:, half:]], axis=0).astype(bf16)
    own_vectors[...] = own

    rows = dot(image[:256], w_img[...], NT)
    low = dot(text, w_txt[...], NT)
    rows = jnp.concatenate([rows + low[:256], low[256:]], axis=0).astype(bf16)

    def placer(count, low, high, shift):
        at = lax.broadcasted_iota(jnp.int32, (count, BLOCK), 1)
        spot = row_ids((count, BLOCK))
        hit = (spot == at + shift) & (at >= low) & (at < high)
        return jnp.where(hit, 1.0, 0.0).astype(bf16)

    window[...] = dot(placer(window.shape[0], spots[3], spots[4], spots[5]), rows).astype(bf16)
    own_rows[...] = dot(placer(own_rows.shape[0], spots[0], spots[1], spots[2]), rows).astype(bf16)


def rows_back(spots, scales, before, d_qkv, d_h, x, w_qkv, w_img, w_txt, span, *after):
    width = w_img.shape[0]
    return pl.pallas_call(
        rows_back_kernel,
        in_specs=[SMEM] + [VMEM] * 8 + [ANY] * len(after),
        out_specs=[VMEM] * 5,
        out_shape=[
            struct((BLOCK + 16, width // 2), bf16),
            struct((BLOCK, width // 2), bf16),
            struct((span, width), bf16),
            struct((WINDOW, width), bf16),
            struct((8, width), f32),
        ],
        scratch_shapes=[pltpu.VMEM((16, width), f32)],
        compiler_params=params(32),
        cost_estimate=cost(0.1),
        name="rows_back",
    )(spots, scales, before, d_qkv, d_h, x, w_qkv, w_img, w_txt, *after)


class Filler:
    def __init__(self, splits, buffers, outs, place, sems, stores):
        self.splits, self.buffers, self.outs = splits, buffers, outs
        self.place, self.sems, self.stores = place, sems, stores
        self.chain, self.block = 0, 0

    def put(self, value):
        for j in range(value.shape[1] // 128):
            split, buffer = self.splits[self.chain], self.buffers[self.chain]
            split.store(buffer, self.block, value[:, j * 128 : (j + 1) * 128])
            self.block += 1
            if self.block == split.full[0]:
                n = len(split.outs)
                outs = self.outs[self.chain * n : (self.chain + 1) * n]
                split.flush(self.stores, self.place, buffer, outs, self.sems.at[self.chain])
                self.chain, self.block = self.chain + 1, 0


def heads_grads_kernel(splits, spots, mine, got_a, got_b, got_c, early, early_got, *rest):
    count, n = sum(len(split.outs) for split in splits), len(splits)
    outs, buffers, out_sem = rest[-count - n - 1 : -n - 1], rest[-n - 1 : -1], rest[-1]
    stores = []
    filler = Filler(splits, buffers, outs, spots[9], out_sem, stores)
    half = got_a.shape[1]
    for k, (got, low) in enumerate(((got_a, 0), (got_b, 0), (got_c, 0), (got_c, half))):
        left = 1 if k < 3 else 2
        filler.put(
            dot(early[left], mine[:, k * half : (k + 1) * half], TN)
            + dot(early_got[left], got[:, low : low + half], TN)
        )
    wait_all(stores)


def rows_grads_kernel(splits, spots, mine, got, vectors, early, early_got, *rest):
    count, n = sum(len(split.outs) for split in splits), len(splits)
    outs, buffers, out_sem = rest[-count - n - 1 : -n - 1], rest[-n - 1 : -1], rest[-1]
    stores = []
    filler = Filler(splits, buffers, outs, spots[9], out_sem, stores)
    at = row_ids((BLOCK, 1))
    is_image = at < 1 + PATCHES
    zeros = jnp.zeros_like(mine)
    image = dot(early[0, :256], jnp.where(is_image, mine[...], zeros)[:256], TN)
    image += dot(early_got[0, :256], jnp.where(is_image, got[:BLOCK], zeros)[:256], TN)
    filler.put(image)
    text = dot(early[0], jnp.where(is_image, zeros, mine[...]), TN)
    text += dot(early_got[0], jnp.where(is_image, zeros, got[:BLOCK]), TN)
    filler.put(text)
    more = got[BLOCK:].astype(f32)
    every = vectors[...] + jnp.concatenate([more[:8], more[8:]], axis=1)
    filler.put(jnp.concatenate([every, jnp.zeros((120, every.shape[1]), f32)], axis=0).T)
    wait_all(stores)


def late_grads(kernel, name, spots, args, wide, parts, *after):
    width = args[-1].shape[2]
    splits = [Split(blocks, width, 128, wide, bit) for blocks, bit in parts]
    shapes = [out for split in splits for out in split.outs]
    outs = pl.pallas_call(
        partial(kernel, splits),
        in_specs=[SMEM] + [VMEM] * len(args) + [ANY] * len(after),
        out_specs=[HBM] * len(shapes),
        out_shape=shapes,
        scratch_shapes=[split.buffer() for split in splits]
        + [pltpu.SemaphoreType.DMA((len(splits), 2))],
        compiler_params=params(32),
        cost_estimate=cost(0.1),
        name=name,
    )(spots, *args, *after)
    n = len(splits[0].outs)
    return [split.halves(outs[k * n : (k + 1) * n]) for k, split in enumerate(splits)]


def result_kernel(spots, b_down, g_low, g_high, w_down_in, h_in, *rest):
    out, g, w_down, h, sem = rest[-5:]
    tiles = g.shape[0]
    waits = []
    for j in range(tiles):
        part = g_low if j < tiles // 2 else g_high
        start_copy(waits, part.at[j % (tiles // 2)], g.at[j], sem.at[2 * j])
        start_copy(waits, w_down_in.at[pl.ds(j * TILE, TILE)], w_down.at[j], sem.at[2 * j + 1])
    start_copy(waits, h_in, h, sem.at[2 * tiles])
    live = row_ids((BLOCK, 1)) < spots[6]
    value = None
    for j in range(tiles):
        waits[2 * j].wait()
        waits[2 * j + 1].wait()
        term = dot(g[j], w_down[j])
        value = term if value is None else value + term
    waits[2 * tiles].wait()
    out[0] = jnp.where(live, value + h[...] + row(b_down), 0.0).astype(bf16)


def result(spots, g, w_down, h, b_down, *after):
    tiles, width = 2 * g[0].shape[0], h.shape[1]
    return pl.pallas_call(
        result_kernel,
        in_specs=[SMEM, VMEM] + [ANY] * 4 + [ANY] * len(after),
        out_specs=VMEM,
        out_shape=struct((1, *h.shape), bf16),
        scratch_shapes=[
            pltpu.VMEM((tiles, *g[0].shape[1:]), bf16),
            pltpu.VMEM((tiles, TILE, width), bf16),
            pltpu.VMEM(h.shape, f32),
            pltpu.SemaphoreType.DMA((2 * tiles + 1,)),
        ],
        compiler_params=params(20),
        cost_estimate=cost(1.5),
        name="result",
    )(spots, b_down, *g, w_down, h, *after)


def round_kernel(steps, lows, joined, spots, *refs):
    count = len(steps)
    keeps, gots = refs[:count], refs[count : 2 * count]
    outs = refs[len(refs) - count - (1 if joined else count) :]
    low = 0
    for k, bit in enumerate(steps):
        blocks, _, rows, _ = keeps[k].shape
        size = 2 * blocks * rows
        got = gots[k][lows[k] : lows[k] + size].reshape(keeps[k].shape)
        value = (keeps[k][...].astype(f32) + got.astype(f32)).astype(bf16)
        first = lax.rem(lax.div(spots[9], 1 << bit), 2) == 0
        outs[k][...] = jnp.where(first, value[:, 0], value[:, 1])
        send = jnp.where(first, value[:, 1], value[:, 0])
        if joined:
            outs[count][low : low + size // 2] = send.reshape(size // 2, 128)
            low += size // 2
        else:
            outs[count + k][...] = send.reshape(size // 2, 128)


class Chain:
    def __init__(self, halves, order, share, wide):
        self.bits, self.order, self.share = wide.bit_length() - 1, order[1:], share
        send, keep = halves
        self.blocks = keep.shape[0]
        self.left = set(range(self.bits)) - {order[0]}
        self.keep, self.got, self.low = keep, swap(send, "wide", order[0]).reshape(-1, 128), 0

    def view(self, value):
        bit = self.order[0]
        below = sum(other < bit for other in self.left)
        above = len(self.left) - 1 - below
        return value.reshape(self.blocks << above, 2, self.share << below, 128)


def advance(spots, chains, *after, joined=False):
    keeps = [chain.view(chain.keep) for chain in chains]
    gots = [chain.got for chain in chains]
    lows = [chain.low for chain in chains]
    steps = [chain.order[0] for chain in chains]
    sizes = [keep.size // 256 for keep in keeps]
    if any(chain.share % 16 for chain in chains):
        outs, sends = [], []
        for keep, got, low, bit in zip(keeps, gots, lows, steps):
            got = got[low : low + keep.size // 128].reshape(keep.shape)
            part = add_low(keep, got)
            mine = (lax.axis_index("wide") >> bit) & 1
            outs.append(lax.dynamic_index_in_dim(part, mine, 1, keepdims=False))
            sends.append(lax.dynamic_index_in_dim(part, 1 - mine, 1).reshape(-1, 128))
        if joined:
            sends = [jnp.concatenate(sends, axis=0)]
        outs += sends
    else:
        shapes = [(keep.shape[0], keep.shape[2], 128) for keep in keeps]
        shapes += [(sum(sizes), 128)] if joined else [(size, 128) for size in sizes]
        outs = pl.pallas_call(
            partial(round_kernel, steps, lows, joined),
            in_specs=[SMEM] + [VMEM] * (2 * len(chains)) + [ANY] * len(after),
            out_specs=[VMEM] * len(shapes),
            out_shape=[struct(shape, bf16) for shape in shapes],
            compiler_params=params(16),
            cost_estimate=cost(0.1),
            name="round",
        )(spots, *keeps, *gots, *after)
    count, low = len(chains), 0
    if joined:
        arrived = swap(outs[count], "wide", steps[0])
    for k, chain in enumerate(chains):
        chain.left = chain.left - {chain.order[0]}
        chain.order = chain.order[1:]
        chain.keep = outs[k]
        if joined:
            chain.got, chain.low = arrived, low
            low += sizes[k]
        else:
            chain.got, chain.low = swap(outs[count + k], "wide", steps[k]), 0
    return chains[-1].keep


def close_kernel(lows, *refs):
    count = len(lows)
    keeps, gots, out = refs[:count], refs[count : 2 * count], refs[-1]
    low = 0
    for keep, got, first in zip(keeps, gots, lows):
        size = keep.shape[0]
        arrived = got[first : first + size].astype(f32)
        out[low : low + size] = (keep[...].astype(f32) + arrived).astype(bf16)
        low += size


def close(chains):
    keeps = [chain.keep.reshape(-1, 128) for chain in chains]
    gots = [chain.got for chain in chains]
    lows = [chain.low for chain in chains]
    if any(chain.share % 16 for chain in chains):
        pairs = zip(keeps, gots, lows)
        return jnp.concatenate([add_low(k, g[a : a + k.shape[0]]) for k, g, a in pairs], axis=0)
    return pl.pallas_call(
        partial(close_kernel, lows),
        in_specs=[VMEM] * (2 * len(chains)),
        out_specs=VMEM,
        out_shape=struct((sum(keep.shape[0] for keep in keeps), 128), bf16),
        compiler_params=params(8),
        cost_estimate=cost(0.1),
        name="close",
    )(*keeps, *gots)


def unpack_kernel(forms, spots, own, other, own_rows, returned, *outs):
    first_core = spots[7] == 0
    pairs, low = [], 0
    for blocks, share in forms:
        pairs.append([])
        for _ in range(blocks):
            one, two = own[low : low + share].astype(f32), other[low : low + share].astype(f32)
            pairs[-1].append((jnp.where(first_core, one, two), jnp.where(first_core, two, one)))
            low += share
    down, up, qkv, out, img, txt = outs[:6]

    def spread(target, blocks):
        count = len(blocks)
        for j, (left, right) in enumerate(blocks):
            target[:, j * 128 : (j + 1) * 128] = left
            target[:, (count + j) * 128 : (count + j + 1) * 128] = right

    spread(down, pairs[0])
    spread(up, pairs[1])
    blocks = sum(pairs[2:], [])
    per = out.shape[1] // 256
    spread(qkv, blocks[: 3 * per])
    spread(out, blocks[3 * per : 4 * per])
    spread(img, blocks[4 * per : 5 * per])
    spread(txt, blocks[5 * per : 6 * per])
    left, right = blocks[6 * per]
    rows = jnp.concatenate([left.T[:8], right.T[:8]], axis=0)
    for k in range(11):
        outs[6 + k][...] = rows[k]
    share = out.shape[0]
    for j in range(4):
        outs[17][pl.ds(j * share, share)] = rows[11 + j]
    d_rows = outs[18]
    blank = jnp.zeros((d_rows.shape[1] - WINDOW, d_rows.shape[2]), bf16)
    low = jnp.concatenate([returned[...], blank], axis=0)
    high = jnp.concatenate([blank, returned[...]], axis=0)
    d_rows[0] = own_rows[...] + jnp.where(spots[8] == 0, low, high)


def unpack(spots, forms, own, other, own_rows, returned):
    share, width = forms[0][1] // 4, forms[0][0] * 256
    shapes = [(4 * share, width), (share, 4 * width), (share, 3 * width)] + [(share, width)] * 3
    shapes += [(share,)] * 11 + [(4 * share,)]
    return pl.pallas_call(
        partial(unpack_kernel, forms),
        in_specs=[SMEM] + [VMEM] * 4,
        out_specs=[VMEM] * (len(shapes) + 1),
        out_shape=[struct(shape, f32) for shape in shapes] + [struct((1, *own_rows.shape), bf16)],
        compiler_params=params(16),
        cost_estimate=cost(0.1),
        name="unpack",
    )(spots, own, other, own_rows, returned)


def swap(x, axis, bit):
    count = lax.axis_size(axis)
    route = [(i, i ^ (1 << bit)) for i in range(count)]
    return lax.ppermute(x, axis, route)


def add_low(one, two):
    f32 = jnp.float32
    return (one.astype(f32) + two.astype(f32)).astype(jnp.bfloat16)


def on_device(
    tower_states,
    caption_lengths,
    assignment,
    cls_token,
    w_img,
    b_img,
    w_txt,
    b_txt,
    gain_one,
    bias_one,
    w_qkv,
    b_query,
    b_value,
    w_out,
    b_out,
    gain_two,
    bias_two,
    w_up,
    b_up,
    w_down,
    b_down,
    cotangent,
):
    wide = lax.axis_size("wide")
    rows = tower_states[0]
    span, width = rows.shape
    bits = wide.bit_length() - 1
    payload, spots = opening(caption_lengths, assignment, tower_states)
    incoming = swap(payload, "wide", bits - 1)
    cot = cotangent[0]
    grad, d_b_down, dy_other = hidden_grad(spots, cot, w_down)
    dy_got = swap(dy_other, "dp", 0)
    vectors = jnp.stack(
        [cls_token, b_img, b_txt, gain_one, bias_one, b_query, b_value, b_out, gain_two, bias_two]
    )
    share, tail = width // wide, list(range(3, bits))

    def order(*first):
        return list(first) + tail

    x, qkv, kept, du_own, h, early, late, *g, inverse, d_b_up = forward(
        spots, tower_states, incoming, vectors, b_up, (w_img, w_txt, w_qkv, w_out, w_up, grad), dy_got
    )
    late_got = swap(late, "dp", 0)
    g_got = [swap(t, "dp", 0) for t in g]
    early_got = swap(early, "dp", 0)
    up = up_grad(spots, late, late_got, du_own, wide, 1)
    down = down_grad(spots, cotangent, dy_got, g, g_got, wide, 0, up[1])
    up = Chain(up, order(1, 0, 2), share, wide)
    down = Chain(down, order(0, 1, 2), 4 * share, wide)
    firsts = [down, up]
    d_h, d_low, d_o, before = unfeed(
        spots, inverse, vectors, d_b_down, d_b_up, cotangent, h, late, du_own, w_up, w_out, down.keep
    )
    d_qkv, *sent, mine, before = heads_back(
        spots, inverse, before, d_o, d_low, qkv, kept, down.keep, early_got
    )
    got = [swap(t, "dp", 0) for t in sent]
    step = advance(spots, firsts[::-1], mine)
    parts = [(6, order(0, 1, 2)), (6, order(1, 0, 2))]
    heads = late_grads(
        heads_grads_kernel, "heads_grads", spots, (mine, *got, early, early_got), wide,
        [(blocks, t[0]) for blocks, t in parts], step,
    )
    heads = [Chain(halves, t, share, wide) for halves, (_, t) in zip(heads, parts)]
    sent, mine, own_rows, window, own_vectors = rows_back(
        spots, vectors, before, d_qkv, d_h, x, w_qkv, w_img, w_txt, span, heads[0].keep
    )
    got = swap(sent, "dp", 0)
    step = advance(spots, firsts, mine, joined=True)
    parts = [(7, order(1, 0, 2))]
    lasts = late_grads(
        rows_grads_kernel, "rows_grads", spots, (mine, got, own_vectors, early, early_got), wide,
        [(blocks, t[0]) for blocks, t in parts], step,
    )
    lasts = [Chain(halves, t, share, wide) for halves, (_, t) in zip(lasts, parts)]
    returned = swap(window, "wide", bits - 1)
    step = advance(spots, heads, lasts[0].keep)
    out = result(spots, g, w_down, h, b_down, step)
    step = out
    step = advance(spots, lasts, step)
    step = advance(spots, firsts, step, joined=True)
    step = advance(spots, heads, step, returned, joined=True)
    step = advance(spots, lasts, step)
    step = advance(spots, heads + lasts, step, joined=True)
    while lasts[0].order:
        step = advance(spots, heads + lasts, step, joined=True)
    while firsts[0].order:
        step = advance(spots, firsts, step, joined=True)
    chains = firsts + heads + lasts
    own = close(chains)
    forms = [(t.blocks, t.share) for t in chains]
    *results, d_rows = unpack(spots, forms, own, swap(own, "dp", 0), own_rows, returned)
    down, up, d_w_qkv, d_w_out, d_w_img, d_w_txt = results[:6]
    vectors, d_b_up = results[6:17], results[17]
    (
        d_cls,
        d_b_img,
        d_b_txt,
        d_gain_one,
        d_bias_one,
        d_b_query,
        d_b_value,
        d_b_out,
        d_gain_two,
        d_bias_two,
        d_b_down,
    ) = vectors
    return (
        out,
        d_rows,
        d_cls,
        d_w_img,
        d_b_img,
        d_w_txt,
        d_b_txt,
        d_gain_one,
        d_bias_one,
        d_w_qkv,
        d_b_query,
        d_b_value,
        d_w_out,
        d_b_out,
        d_gain_two,
        d_bias_two,
        up,
        d_b_up,
        down,
        d_b_down,
    )


def solution(mesh):
    placed = (
        P("dp", "wide", None),
        P("dp", None, None),
        P("dp", None, None),
        P(),
        P(),
        P(),
        P(),
        P(),
        P(),
        P(),
        P(),
        P(),
        P(),
        P(),
        P(),
        P(),
        P(),
        P(),
        P(),
        P(),
        P(),
        P("dp", "wide", None),
    )
    return jax.shard_map(
        on_device,
        mesh=mesh,
        in_specs=placed,
        out_specs=(
            P("dp", "wide", None),
            P("dp", "wide", None),
            P("wide"),
            P("wide", None),
            P("wide"),
            P("wide", None),
            P("wide"),
            P("wide"),
            P("wide"),
            P("wide", None),
            P("wide"),
            P("wide"),
            P("wide", None),
            P("wide"),
            P("wide"),
            P("wide"),
            P("wide", None),
            P("wide"),
            P("wide", None),
            P("wide"),
        ),
        check_vma=False,
    )
```
